128 devices in a mesh: ctx: 32 (over z_hi, x, y), grp: 4 (over z_lo, core).
Axes of the slice: x: 4, y: 4, z: 4 (z_hi: 2, z_lo: 2; z = z_hi * 2 + z_lo), core: 2. Of those that a mesh axis runs over, the one named last changes fastest.
Arguments:
- prefill_queries: bfloat16 [4096, 40960], P('ctx', 'grp'), may hold values from -30 to 30
- latents: bfloat16 [4096, 1024], P('ctx', 'grp'), may hold values from -5 to 5
- rope_keys: bfloat16 [4096, 64], P('ctx'), may hold values from -5 to 5
- span_slots: int32 [64], replicated, may hold values from 0 to 63, each once
- decode_queries: bfloat16 [2, 256, 40960], P(None, 'ctx', 'grp'), may hold values from -30 to 30
- new_latents: bfloat16 [2, 256, 1024], P(None, 'ctx', 'grp'), may hold values from -5 to 5
- new_rope: bfloat16 [2, 256, 64], P(None, 'ctx'), may hold values from -5 to 5
- context_lengths: int32 [256], P('ctx'), may hold values from 1 to 1024, 131072 in all
- page_table: int32 [256, 16], P('ctx'), may hold values from 0 to 63
- value_up: bfloat16 [128, 256, 128], P('grp'), may hold values from -0.375 to 0.375
- out_proj: bfloat16 [16384, 7168], P('grp', 'ctx'), may hold values from -0.046875 to 0.046875
Outputs:
- prefill_values: bfloat16 [4096, 16384], P('ctx', 'grp')
- decoded: bfloat16 [2, 256, 7168], P(None, 'grp', 'ctx')
The draws below stay inside these ranges and needn't reach their ends.
Inputs may be any that keep to these rules, and one draw needn't show every extreme that they name: `span_slots`: each of 0 to 63 stands once.
All inputs are finite; a program needn't handle non-finite values. No bound on the sum of `context_lengths` on one device may be relied on, other than what follows from the above.
Results may differ from the reference program's by a relative error of at most 0.015.
Values may be sent and summed in bfloat16 or wider, within the bound.
No kernel may reach another device: no remote copies, remote signals or barrier semaphores. Data moves between devices by JAX's collectives and lax.ppermute only.
A program may use at most 128 MiB of HBM per device.

```python
import math
import jax
import jax.numpy as jnp
import numpy as np
from jax import lax

HEADS = 128
ROPE = 64
VDIM = 128
D = 7168
LATENT = 256
GROUPS = 4
TOK_DEV = 128
SPAN = 64
SLOTS = 64
SEQ = 4096
PAGE = 64
PAGES_ROW = 16
NPAGES = 64
MAXLEN = 1024
B = 256
STEPS = 2


def mixed_normal(key, array_shape):
    normal_key = jax.random.fold_in(key, 0)
    gaussian = jnp.clip(jax.random.normal(normal_key, array_shape, jnp.float32), -5.0, 5.0)
    return gaussian


def prefill_base(key, lift_flag):
    key = jax.random.fold_in(key, 11)
    keys_all = jax.random.split(key, 3)
    head_group = HEADS // GROUPS
    half_width = LATENT // 2
    latent_all = mixed_normal(keys_all[0], (SEQ, GROUPS, LATENT))
    rope_all = mixed_normal(keys_all[1], (SEQ, ROPE))
    query_all = 2.0 * mixed_normal(keys_all[2], (SEQ, HEADS, LATENT + ROPE))
    row_ids = jnp.arange(SEQ)
    chosen = (row_ids % SPAN == SPAN - 1) & (lift_flag > 0.5)
    partner = (row_ids % SPAN == SPAN - 2) & (lift_flag > 0.5)
    strength = 9.0 + 4.0 * (row_ids // SPAN % 3).astype(jnp.float32)
    next_latent = jnp.roll(latent_all, -1, axis=0)
    next_rope = jnp.roll(rope_all, -1, axis=0)
    next_strength = jnp.roll(strength, -1)
    copied = jnp.concatenate([next_latent[:, :, :half_width], latent_all[:, :, half_width:]], axis=2)
    latent_new = jnp.where(partner[:, None, None], copied, latent_all)
    rope_new = jnp.where(partner[:, None], (1.0 - 0.43 / next_strength)[:, None] * next_rope, rope_all)
    aligned_latent = jnp.concatenate([latent_all[:, :, :half_width], jnp.zeros_like(latent_all[:, :, half_width:])], axis=2)
    aligned_latent = jnp.repeat(aligned_latent, head_group, axis=1)
    aligned = jnp.concatenate([aligned_latent, jnp.broadcast_to(rope_all[:, None, :], (SEQ, HEADS, ROPE))], axis=2)
    query_new = jnp.where(chosen[:, None, None], strength[:, None, None] * aligned, query_all)
    return (query_new, latent_new, rope_new)


def decode_base(key, lift_flag):
    key = jax.random.fold_in(key, 23)
    keys_all = jax.random.split(key, 3)
    head_group = HEADS // GROUPS
    half_width = LATENT // 2
    latent_all = mixed_normal(keys_all[0], (STEPS, B, GROUPS, LATENT))
    rope_all = mixed_normal(keys_all[1], (STEPS, B, ROPE))
    query_all = 2.0 * mixed_normal(keys_all[2], (STEPS, B, HEADS, LATENT + ROPE))
    row_ids = jnp.arange(B)
    chosen = (row_ids % 4 == 0) & (lift_flag > 0.5)
    strength = 9.0 + 4.0 * (row_ids // 4 % 3).astype(jnp.float32)
    copied = jnp.concatenate([latent_all[0, :, :, :half_width], latent_all[1, :, :, half_width:]], axis=2)
    second_latent = jnp.where(chosen[:, None, None], copied, latent_all[1])
    latent_new = jnp.concatenate([latent_all[:1], second_latent[None], latent_all[2:]], axis=0)
    second_rope = jnp.where(chosen[:, None], (1.0 - 0.43 / strength)[:, None] * rope_all[0], rope_all[1])
    rope_new = jnp.concatenate([rope_all[:1], second_rope[None], rope_all[2:]], axis=0)
    aligned_latent = jnp.concatenate([latent_all[0, :, :, :half_width], jnp.zeros_like(latent_all[0, :, :, half_width:])], axis=2)
    aligned_latent = jnp.repeat(aligned_latent, head_group, axis=1)
    aligned = jnp.concatenate([aligned_latent, jnp.broadcast_to(rope_all[0][:, None, :], (B, HEADS, ROPE))], axis=2)
    query_new = jnp.where(chosen[None, :, None, None], strength[None, :, None, None] * aligned[None], query_all)
    return (query_new, latent_new, rope_new)


def draw_prefill_queries(key, part):
    query_new, latent_new, rope_new = prefill_base(key, 0.0)
    return query_new.reshape(SEQ, HEADS * (LATENT + ROPE)).astype(jnp.bfloat16)


def draw_latents(key, part):
    query_new, latent_new, rope_new = prefill_base(key, 0.0)
    return latent_new.reshape(SEQ, GROUPS * LATENT).astype(jnp.bfloat16)


def draw_rope_keys(key, part):
    query_new, latent_new, rope_new = prefill_base(key, 0.0)
    return rope_new.astype(jnp.bfloat16)


def draw_decode_queries(key, part):
    query_new, latent_new, rope_new = decode_base(key, 0.0)
    return query_new.reshape(STEPS, B, HEADS * (LATENT + ROPE)).astype(jnp.bfloat16)


def draw_new_latents(key, part):
    query_new, latent_new, rope_new = decode_base(key, 0.0)
    return latent_new.reshape(STEPS, B, GROUPS * LATENT).astype(jnp.bfloat16)


def draw_new_rope(key, part):
    query_new, latent_new, rope_new = decode_base(key, 0.0)
    return rope_new.astype(jnp.bfloat16)


def touch_ends(drawn, stream_key, low, top_value):
    spot = [jax.random.randint(jax.random.fold_in(stream_key, axis), (), 0, length) for axis, length in enumerate(drawn.shape)]
    main_axis = drawn.shape.index(max(drawn.shape))
    beside = spot[:main_axis] + [(spot[main_axis] + 1) % drawn.shape[main_axis]] + spot[main_axis + 1:]
    return drawn.at[tuple(spot)].set(low).at[tuple(beside)].set(top_value)


def block_scale(key, extent, cuts, smallest, top_value):
    def one(axis_at, parts):
        draws = jax.random.uniform(jax.random.fold_in(jax.random.fold_in(key, 6), axis_at), (parts,), jnp.float32, smallest / len(cuts), top_value / len(cuts))
        return jnp.repeat(jnp.exp(draws), extent[axis_at] // parts).reshape((-1,) + (1,) * (len(extent) - axis_at - 1))

    loudness = one(*cuts[0])
    for cut in cuts[1:]:
        loudness = loudness * one(*cut)
    return loudness


def length_profile(amount, total, most, slope):
    portions = [(1 << 20) // math.isqrt(standing ** slope) + 1 for standing in range(2, amount + 1)]
    rest, holding = total - most - (amount - 1), [1] * (amount - 1)
    while rest > 0:
        free = [i for i in range(amount - 1) if holding[i] < most]
        mass, remaining = sum([portions[i] for i in free]), rest
        for i in free:
            extra = min(most - holding[i], max(1, remaining * portions[i] // mass), rest)
            holding[i] = holding[i] + extra
            rest = rest - extra
    return np.array([most] + holding)


def ragged(stream_key, count, total, bound, skew):
    if count == 2:
        one = jax.random.randint(stream_key, (), max(1, total - bound), min(bound, total - 1) + 1)
        return jnp.stack([one, total - one])
    sizes = jnp.asarray(length_profile(count, total, bound, skew), jnp.int32)
    pairs = (count - 1) // 2
    giver, taker = sizes[1:1 + 2 * pairs:2], sizes[2:2 + 2 * pairs:2]
    slack = jnp.minimum(giver - 1, bound - taker)
    passed = jax.random.randint(jax.random.fold_in(stream_key, 1), (pairs,), 0, 1 << 20) % (slack + 1)
    sizes = sizes.at[1:1 + 2 * pairs:2].set(giver - passed).at[2:2 + 2 * pairs:2].set(taker + passed)
    return sizes[jax.random.permutation(jax.random.fold_in(stream_key, 2), count)]


def bell_draw(stream_key, extent, scale, bound, cuts=(), kind=jnp.bfloat16):
    factor_of = block_scale(stream_key, extent, cuts, -0.22, 0.18) if cuts else 1.0
    entries = jax.random.normal(stream_key, extent, jnp.float32) * scale * factor_of
    return jnp.minimum(jnp.maximum(entries, -bound), bound).astype(kind)


def setup_inputs(seed: int = 0) -> dict:
    streams_of = jax.random.split(jax.random.key(seed), 12)
    prefill_queries = draw_prefill_queries(jax.random.fold_in(streams_of[11], 71), 0)
    latents = draw_latents(jax.random.fold_in(streams_of[11], 71), 0)
    rope_keys = draw_rope_keys(jax.random.fold_in(streams_of[11], 71), 0)
    span_slots = jax.random.permutation(streams_of[3], SLOTS).astype(jnp.int32)
    decode_queries = draw_decode_queries(jax.random.fold_in(streams_of[11], 71), 0)
    new_latents = draw_new_latents(jax.random.fold_in(streams_of[11], 71), 0)
    new_rope = draw_new_rope(jax.random.fold_in(streams_of[11], 71), 0)
    context_lengths = ragged(streams_of[7], B, B * MAXLEN // 2, MAXLEN, 1).astype(jnp.int32)
    page_table = touch_ends(jax.random.randint(streams_of[8], (B, PAGES_ROW), 0, NPAGES), jax.random.fold_in(streams_of[8], 1), 0, NPAGES - 1).astype(jnp.int32)
    value_up = bell_draw(streams_of[9], (HEADS, LATENT, VDIM), LATENT ** -0.5, 0.375, ((0, 4),))
    out_proj = bell_draw(streams_of[10], (HEADS * VDIM, D), (HEADS * VDIM) ** -0.5, 0.046875, ((0, 4), (1, 32)))
    return {"prefill_queries": prefill_queries, "latents": latents, "rope_keys": rope_keys, "span_slots": span_slots, "decode_queries": decode_queries, "new_latents": new_latents, "new_rope": new_rope, "context_lengths": context_lengths, "page_table": page_table, "value_up": value_up, "out_proj": out_proj}


attention_score_scale = 192.0 ** -0.5


def slot_lookup(span_slots):
    slot_ids = jnp.arange(span_slots.shape[0], dtype=jnp.int32)
    matches = span_slots[:, None] == slot_ids[None, :]
    return jnp.sum(jnp.where(matches, slot_ids[:, None], 0), axis=0).astype(jnp.int32)


def reference(prefill_queries, latents, rope_keys, span_slots, decode_queries, new_latents, new_rope, context_lengths, page_table, value_up, out_proj):
    head_group = HEADS // GROUPS
    key_width = LATENT + ROPE
    row_ids = jnp.arange(SEQ, dtype=jnp.int32)
    positions = (span_slots[row_ids // SPAN] * SPAN + row_ids % SPAN).astype(jnp.int32)
    queries = prefill_queries.reshape(SEQ, HEADS, key_width)
    block_count = SEQ // TOK_DEV
    query_blocks_pos = positions.reshape(block_count, TOK_DEV)
    prefill_parts = []
    for group_id in range(GROUPS):
        latent_group = latents[:, group_id * LATENT:(group_id + 1) * LATENT]
        key_rows = jnp.concatenate([latent_group, rope_keys], axis=1).astype(jnp.float32)
        latent_float = latent_group.astype(jnp.float32)
        group_queries = queries[:, group_id * head_group:(group_id + 1) * head_group].astype(jnp.float32)
        group_queries = group_queries.reshape(block_count, TOK_DEV, head_group, key_width)
        value_map = value_up[group_id * head_group:(group_id + 1) * head_group].astype(jnp.float32)

        def one_block(block_item):
            block_queries, block_pos = block_item
            scores = jnp.einsum("qhd,kd->qhk", block_queries, key_rows) * attention_score_scale
            visible = (block_pos[:, None] >= positions[None, :])[:, None, :]
            row_max = jnp.max(jnp.where(visible, scores, -jnp.inf), axis=2, keepdims=True)
            weights = jnp.where(visible, jnp.exp(scores - row_max), 0.0)
            totals = jnp.sum(weights, axis=2)
            rounded = lax.optimization_barrier(weights.astype(jnp.bfloat16)).astype(jnp.float32)
            attended = jnp.einsum("qhk,kc->qhc", rounded, latent_float) / totals[:, :, None]
            attended = lax.optimization_barrier(attended.astype(jnp.bfloat16)).astype(jnp.float32)
            values_out = jnp.einsum("qhc,hcv->qhv", attended, value_map)
            return values_out.astype(jnp.bfloat16).reshape(TOK_DEV, head_group * VDIM)

        group_out = lax.map(one_block, (group_queries, query_blocks_pos))
        prefill_parts.append(group_out.reshape(SEQ, head_group * VDIM))
    prefill_values = jnp.concatenate(prefill_parts, axis=1)

    inverse = slot_lookup(span_slots)
    offsets = jnp.arange(MAXLEN, dtype=jnp.int32)
    token_pos = (page_table[:, offsets // PAGE] * PAGE + offsets % PAGE).astype(jnp.int32)
    storage = (inverse[token_pos // SPAN] * SPAN + token_pos % SPAN).astype(jnp.int32)
    visible_cache = (offsets[None, :] < context_lengths[:, None])[:, None, :]
    step_queries = decode_queries.reshape(STEPS, B, HEADS, key_width)
    step_values = [[] for step_id in range(STEPS)]
    for group_id in range(GROUPS):
        latent_group = latents[:, group_id * LATENT:(group_id + 1) * LATENT]
        cache_latent = latent_group[storage].astype(jnp.float32)
        cache_rope = rope_keys[storage].astype(jnp.float32)
        cached_key_rows = jnp.concatenate([cache_latent, cache_rope], axis=2)
        value_map = value_up[group_id * head_group:(group_id + 1) * head_group].astype(jnp.float32)
        for step_id in range(STEPS):
            incoming_latent_rows = new_latents[:step_id + 1, :, group_id * LATENT:(group_id + 1) * LATENT].astype(jnp.float32)
            fresh_keys = jnp.concatenate([incoming_latent_rows, new_rope[:step_id + 1].astype(jnp.float32)], axis=2)
            query_row_values = step_queries[step_id, :, group_id * head_group:(group_id + 1) * head_group].astype(jnp.float32)
            cached_score_matrix = jnp.einsum("spx,scx->spc", query_row_values, cached_key_rows) * attention_score_scale
            fresh_scores = jnp.einsum("bhd,nbd->bhn", query_row_values, fresh_keys) * attention_score_scale
            row_max = jnp.maximum(jnp.max(jnp.where(visible_cache, cached_score_matrix, -jnp.inf), axis=2), jnp.max(fresh_scores, axis=2))
            cached_weight_matrix = jnp.where(visible_cache, jnp.exp(cached_score_matrix - row_max[:, :, None]), 0.0)
            fresh_weights = jnp.exp(fresh_scores - row_max[:, :, None])
            totals = jnp.sum(cached_weight_matrix, axis=2) + jnp.sum(fresh_weights, axis=2)
            cache_round = lax.optimization_barrier(cached_weight_matrix.astype(jnp.bfloat16)).astype(jnp.float32)
            fresh_round = lax.optimization_barrier(fresh_weights.astype(jnp.bfloat16)).astype(jnp.float32)
            attended = jnp.einsum("bhk,bkc->bhc", cache_round, cache_latent) + jnp.einsum("bhn,nbc->bhc", fresh_round, incoming_latent_rows)
            attended = attended / totals[:, :, None]
            attended = lax.optimization_barrier(attended.astype(jnp.bfloat16)).astype(jnp.float32)
            values_out = jnp.einsum("bhc,hcv->bhv", attended, value_map).astype(jnp.bfloat16)
            step_values[step_id].append(values_out.reshape(B, head_group * VDIM))
    decoded_steps = []
    for step_id in range(STEPS):
        row_values = jnp.concatenate(step_values[step_id], axis=1)
        decoded_steps.append(jnp.dot(row_values, out_proj, preferred_element_type=jnp.float32).astype(jnp.bfloat16))
    decoded = jnp.stack(decoded_steps, axis=0)
    return (prefill_values, decoded)
```

```python
import functools
import itertools
import math

import jax
import jax.numpy as jnp
from jax import lax
from jax.experimental import pallas as pl
from jax.experimental.pallas import tpu as pltpu
from jax.sharding import PartitionSpec as P

SPAN = 64
LATENT = 256
ROPE = 64
KEYW = LATENT + ROPE
KPAD = 384
VDIM = 128

HEADS_TILE = 8
ROWS = HEADS_TILE * SPAN
KEYS = 512

EXP2_SCALE = 192.0 ** -0.5 * math.log2(math.e)
FAR_BELOW = -1e30
NT = (((1,), (1,)), ((), ()))
Z, X, Y = 2, 4, 4


def ctx_index(z, x, y):
    return z * (X * Y) + x * Y + y


def places():
    return [(z, x, y) for z in range(Z) for x in range(X) for y in range(Y)]


def from_other_z(value):
    pairs = [(ctx_index(z, x, y), ctx_index(1 - z, x, y)) for z, x, y in places()]
    return lax.ppermute(value, "ctx", pairs)


def gather(block, axes):
    lines = {}
    for z, x, y in places():
        at = (z, None if "x" in axes else x, None if "y" in axes else y)
        lines.setdefault(at, []).append(ctx_index(z, x, y))
    groups = list(lines.values())
    copies = jnp.broadcast_to(block[None], (len(groups[0]),) + block.shape)
    return lax.all_to_all(
        copies, "ctx", split_axis=0, concat_axis=0, axis_index_groups=groups, tiled=True
    )


def pack_kernel(latents_ref, rope_ref, out_ref):
    rope = rope_ref[...].astype(jnp.float32).T
    for span in range(2):
        rows = slice(span * SPAN, (span + 1) * SPAN)
        out_ref[span, :SPAN, :] = latents_ref[rows, :]
        parts = [rope[span * SPAN + c * 16 : span * SPAN + (c + 1) * 16] for c in range(4)]
        out_ref[span, SPAN:, :] = jnp.concatenate(parts, axis=1).astype(jnp.bfloat16)


def pack(latents, rope_keys):
    return pl.pallas_call(
        pack_kernel,
        out_shape=jax.ShapeDtypeStruct((2, SPAN + SPAN // 4, LATENT), jnp.bfloat16),
    )(latents, rope_keys.T)


def decode_kernel(
    z_ref,
    spans_ref,
    pages_ref,
    lengths_ref,
    own_first_ref,
    other_first_ref,
    second_ref,
    q_ref,
    new_latents_ref,
    new_rope_ref,
    up_hbm,
    keys_hbm,
    values_ref,
    up_ref,
    keys_ref,
    queries,
    fresh,
    cache,
    att,
    sems,
):
    low_lanes = lax.broadcasted_iota(jnp.int32, (16, 128), 1) < ROPE
    up_copy = pltpu.make_async_copy(up_hbm, up_ref, sems.at[0])
    up_copy.start()
    for half, dz, line in itertools.product(range(2), range(2), range(X * Y)):
        block = own_first_ref.at[line] if half == 0 else second_ref.at[line, dz]
        if half == 0 and dz == 1:
            block = other_first_ref.at[line]
        z = z_ref[0] if dz == 0 else 1 - z_ref[0]
        span = spans_ref[2 * (z * (X * Y) + line) + half]
        rows = pl.ds(pl.multiple_of(span * SPAN, SPAN), SPAN)
        keys_ref[rows, :LATENT] = block[:SPAN, :]
        packed = block[SPAN:, :].astype(jnp.float32)
        parts = []
        for c in range(2):
            two = packed[:, c * 128 : (c + 1) * 128]
            parts.append(jnp.where(low_lanes, two, 0.0))
            parts.append(jnp.where(low_lanes, pltpu.roll(two, 64, 1), 0.0))
        keys_ref[rows, LATENT:] = jnp.concatenate(parts, axis=0).astype(jnp.bfloat16)
    keys_copy = pltpu.make_async_copy(keys_ref, keys_hbm, sems.at[1])
    keys_copy.start()

    rows_local, pages = pages_ref.shape
    slots = pages * SPAN
    width = cache.shape[1]
    fresh[...] = jnp.zeros_like(fresh)
    for s in range(2):
        for h in range(32):
            at = h // 2 * 2 * KEYW + h % 2 * 256
            rows = q_ref[s, :, at : at + KPAD].astype(jnp.float32)
            if h % 2:
                rows = pltpu.roll(rows, KPAD - 64, 1)
            for c in range(3):
                queries[c, pl.ds(s * 32 + h, rows_local, stride=64), :] = rows[
                    :, c * 128 : (c + 1) * 128
                ]
        mine = pl.ds(s, rows_local, stride=16)
        latent_rows = new_latents_ref[s].astype(jnp.float32)
        fresh[0, mine, :] = latent_rows[:, :128]
        fresh[1, mine, :] = latent_rows[:, 128:]
        rope_rows = new_rope_ref[s].astype(jnp.float32)
        fresh[2, mine, :] = jnp.concatenate([rope_rows, jnp.zeros_like(rope_rows)], axis=1)

    def whole(ref, rows):
        return jnp.concatenate([ref[c, rows, :] for c in range(3)], axis=1).astype(jnp.bfloat16)

    cols = lax.broadcasted_iota(jnp.int32, (64, width), 1)
    step = lax.broadcasted_iota(jnp.int32, (64, width), 0) // 32
    fresh_seen = (cols >= slots) & (cols - slots <= step)
    for b in range(rows_local):
        for j in range(pages):
            page = pages_ref[b, j]
            cache[b, j * SPAN : (j + 1) * SPAN, :] = keys_ref[
                pl.ds(pl.multiple_of(page * SPAN, SPAN), SPAN), :
            ]
        cache[b, slots : slots + 16, :] = whole(fresh, slice(b * 16, (b + 1) * 16))
        cache[b, slots + 16 :, :] = jnp.zeros((width - slots - 16, KPAD), jnp.bfloat16)
        row_queries = whole(queries, slice(b * 64, (b + 1) * 64))
        scores = lax.dot_general(row_queries, cache[b], NT, preferred_element_type=jnp.float32)
        seen = (cols < lengths_ref[b]) | fresh_seen
        scores = jnp.where(seen, scores, FAR_BELOW)
        top = jnp.max(scores, axis=1, keepdims=True)
        weights = jnp.exp2(scores * EXP2_SCALE - top * EXP2_SCALE)
        total = jnp.sum(weights, axis=1, keepdims=True)
        attended = jnp.dot(
            weights.astype(jnp.bfloat16), cache[b, :, :LATENT], preferred_element_type=jnp.float32
        )
        attended = attended / total
        for s in range(2):
            for c in range(2):
                att[c, pl.ds(s * rows_local + b, 32, stride=16), :] = attended[
                    s * 32 : (s + 1) * 32, c * 128 : (c + 1) * 128
                ]
    up_copy.wait()
    for h in range(32):
        mine = slice(h * 16, (h + 1) * 16)
        attended = jnp.concatenate([att[0, mine, :], att[1, mine, :]], axis=1)
        values_ref[:, h * VDIM : (h + 1) * VDIM] = jnp.dot(
            attended.astype(jnp.bfloat16), up_ref[h], preferred_element_type=jnp.float32
        ).astype(jnp.bfloat16)
    keys_copy.wait()


def decode(
    z, spans, pages, lengths, own_first, other_first, second, queries, latents, rope, value_up
):
    smem = pl.BlockSpec(memory_space=pltpu.SMEM)
    vmem = pl.BlockSpec(memory_space=pltpu.VMEM)
    hbm = pl.BlockSpec(memory_space=pl.ANY)
    rows_local = pages.shape[0]
    heads = value_up.shape[0]
    return pl.pallas_call(
        decode_kernel,
        out_shape=(
            jax.ShapeDtypeStruct((spans.shape[0] * SPAN, KPAD), jnp.bfloat16),
            jax.ShapeDtypeStruct((2 * rows_local, heads * VDIM), jnp.bfloat16),
        ),
        in_specs=[smem] * 4 + [vmem] * 6 + [hbm],
        out_specs=(hbm, vmem),
        scratch_shapes=[
            pltpu.VMEM(value_up.shape, jnp.bfloat16),
            pltpu.VMEM((spans.shape[0] * SPAN, KPAD), jnp.bfloat16),
            pltpu.VMEM((3, 64 * rows_local, 128), jnp.float32),
            pltpu.VMEM((3, 16 * rows_local, 128), jnp.float32),
            pltpu.VMEM((rows_local, pages.shape[1] * SPAN + 128, KPAD), jnp.bfloat16),
            pltpu.VMEM((2, 16 * heads, 128), jnp.float32),
            pltpu.SemaphoreType.DMA((2,)),
        ],
        compiler_params=pltpu.CompilerParams(vmem_limit_bytes=40 << 20),
        cost_estimate=pl.CostEstimate(
            flops=2 * 8 * 64 * 1152 * 640, bytes_accessed=12 << 20, transcendentals=8 * 64 * 1152
        ),
    )(
        z, spans, pages, lengths, own_first, other_first, second, queries, latents, rope, value_up
    )


def prefill_kernel(spans_ref, q_hbm, k_hbm, up_hbm, out_ref, done_ref, *scratch):
    q_ref, k_ref, up_ref, qs, s_a, s_b, p_a, p_b, top, total, r_a, r_b, acc, sems = scratch
    q_copy = pltpu.make_async_copy(q_hbm, q_ref, sems.at[0])
    k_copy = pltpu.make_async_copy(k_hbm, k_ref, sems.at[1])
    up_copy = pltpu.make_async_copy(up_hbm, up_ref, sems.at[2])
    q_copy.start()
    k_copy.start()
    up_copy.start()
    top[...] = jnp.full(top.shape, FAR_BELOW, jnp.float32)
    total[...] = jnp.zeros_like(total)
    acc[...] = jnp.zeros_like(acc)
    p_b[...] = jnp.zeros_like(p_b)
    r_b[...] = jnp.ones_like(r_b)
    q_copy.wait()
    tiles = acc.shape[0] // 2
    span_of = [spans_ref[s] for s in range(2)]
    blocks_of = [span // (KEYS // SPAN) for span in span_of]

    for tile in range(tiles):
        for pair in range(HEADS_TILE // 2):
            at = (tile * HEADS_TILE + pair * 2) * KEYW
            for s in range(2):
                tokens = slice(s * SPAN, (s + 1) * SPAN)
                rows = qs.at[2 * tile + s]
                rows[2 * pair * SPAN : (2 * pair + 1) * SPAN, :] = q_ref[tokens, at : at + KPAD]
                odd = q_ref[tokens, at + 256 : at + 640].astype(jnp.float32)
                rows[(2 * pair + 1) * SPAN : (2 * pair + 2) * SPAN, :] = pltpu.roll(
                    odd, KPAD - 64, 1
                ).astype(jnp.bfloat16)

    def key_rows(block):
        return pl.ds(pl.multiple_of(block * KEYS, KEYS), KEYS)

    def score(unit, block, s_ref):
        s_ref[...] = lax.dot_general(
            qs[unit], k_ref[key_rows(block), :], NT, preferred_element_type=jnp.float32
        )

    lead = lax.broadcasted_iota(jnp.int32, (SPAN, 128), 1)
    lead = lead - lax.broadcasted_iota(jnp.int32, (SPAN, 128), 0)

    def weigh(unit, s_ref, p_ref, r_ref, last_key=None):
        for h in range(HEADS_TILE):
            rows = slice(h * SPAN, (h + 1) * SPAN)
            parts = [s_ref[rows, c * 128 : (c + 1) * 128] for c in range(KEYS // 128)]
            if last_key is not None:
                parts = [
                    jnp.where(lead <= last_key - c * 128, part, FAR_BELOW)
                    for c, part in enumerate(parts)
                ]
            highest = functools.reduce(jnp.maximum, parts)
            old = top[unit, rows]
            new = jnp.maximum(old, jnp.max(highest, axis=1, keepdims=True))
            top[unit, rows] = new
            scaled = new * EXP2_SCALE
            rescale = jnp.exp2(old * EXP2_SCALE - scaled)
            r_ref[rows] = rescale
            weights = [jnp.exp2(part * EXP2_SCALE - scaled) for part in parts]
            total[unit, rows] = total[unit, rows] * rescale + sum(weights)
            for c, weight in enumerate(weights):
                p_ref[rows, c * 128 : (c + 1) * 128] = weight.astype(jnp.bfloat16)

    def add_values(unit, block, p_ref, r_ref):
        product = jnp.dot(
            p_ref[...], k_ref[key_rows(block), :LATENT], preferred_element_type=jnp.float32
        )
        r = r_ref[...]
        acc[unit, :, :128] = acc[unit, :, :128] * r + product[:, :128]
        acc[unit, :, 128:] = acc[unit, :, 128:] * r + product[:, 128:]

    k_copy.wait()

    def last_item(unit):
        return unit, jnp.where(unit % 2 == 0, blocks_of[0], blocks_of[1])

    def following(item):
        unit, block = item
        ends = block + 1 >= jnp.where(unit % 2 == 0, blocks_of[0], blocks_of[1])
        other = 1 - unit % 2
        other_empty = jnp.where(other == 0, blocks_of[0], blocks_of[1]) == 0
        jump = jnp.where(other_empty, 2, 1)
        unit = jnp.where(ends, unit + jump, unit)
        return unit, jnp.where(ends, 0, block + 1)

    def two_items(i, carry):
        before, here = carry[:2], carry[2:]
        after = following(here)
        score(*after, s_b)
        weigh(here[0], s_a, p_a, r_a)
        add_values(*before, p_b, r_b)
        later = following(after)
        at_end = later[0] >= 2 * tiles
        later = tuple(jnp.where(at_end, end, value) for end, value in zip(last_item(0), later))
        score(*later, s_a)
        weigh(after[0], s_b, p_b, r_b)
        add_values(*here, p_a, r_a)
        return after + later

    all_blocks = blocks_of[0] + blocks_of[1]
    first = (jnp.where(blocks_of[0] == 0, 1, 0), jnp.int32(0))
    first = tuple(
        jnp.where(all_blocks == 0, end, value) for end, value in zip(last_item(0), first)
    )
    score(*first, s_a)
    carry = lax.fori_loop(
        0, all_blocks * (tiles // 2), two_items, (jnp.int32(0), jnp.int32(0)) + first
    )

    def two_last(i, carry):
        before = carry
        even, odd = last_item(2 * i), last_item(2 * i + 1)
        later = last_item(jnp.minimum(2 * i + 2, 2 * tiles - 1))
        offset = [(span_of[s] - blocks_of[s] * (KEYS // SPAN)) * SPAN for s in range(2)]
        score(*odd, s_b)
        weigh(even[0], s_a, p_a, r_a, offset[0])
        add_values(*before, p_b, r_b)
        score(*later, s_a)
        weigh(odd[0], s_b, p_b, r_b, offset[1])
        add_values(*even, p_a, r_a)
        return odd

    before = lax.fori_loop(0, tiles, two_last, carry[:2])
    add_values(*before, p_b, r_b)

    up_copy.wait()

    def finish(tile, carry):
        for s in range(2):
            unit = 2 * tile + s
            attended = acc[unit] / jnp.sum(total[unit], axis=1, keepdims=True)
            attended = attended.astype(jnp.bfloat16)
            values = [
                jnp.dot(
                    attended[h * SPAN : (h + 1) * SPAN],
                    up_ref[tile * HEADS_TILE + h],
                    preferred_element_type=jnp.float32,
                ).astype(jnp.bfloat16)
                for h in range(HEADS_TILE)
            ]
            columns = HEADS_TILE * VDIM
            out_ref[
                s * SPAN : (s + 1) * SPAN, pl.ds(pl.multiple_of(tile * columns, columns), columns)
            ] = jnp.concatenate(values, axis=1)
        return carry

    lax.fori_loop(0, tiles, finish, 0)
    done_ref[...] = jnp.zeros_like(done_ref)


def prefill(spans, queries, keys, value_up):
    tokens = queries.shape[0]
    heads = value_up.shape[0]
    units = 2 * heads // HEADS_TILE
    f32 = jnp.float32
    smem = pl.BlockSpec(memory_space=pltpu.SMEM)
    vmem = pl.BlockSpec(memory_space=pltpu.VMEM)
    return pl.pallas_call(
        prefill_kernel,
        out_shape=(
            jax.ShapeDtypeStruct((tokens, heads * VDIM), jnp.bfloat16),
            jax.ShapeDtypeStruct((8, 128), f32),
        ),
        in_specs=[smem] + [pl.BlockSpec(memory_space=pl.ANY)] * 3,
        out_specs=(vmem, vmem),
        scratch_shapes=[
            pltpu.VMEM(queries.shape, jnp.bfloat16),
            pltpu.VMEM(keys.shape, jnp.bfloat16),
            pltpu.VMEM(value_up.shape, jnp.bfloat16),
            pltpu.VMEM((units, ROWS, KPAD), jnp.bfloat16),
            pltpu.VMEM((ROWS, KEYS), f32),
            pltpu.VMEM((ROWS, KEYS), f32),
            pltpu.VMEM((ROWS, KEYS), jnp.bfloat16),
            pltpu.VMEM((ROWS, KEYS), jnp.bfloat16),
            pltpu.VMEM((units, ROWS, 128), f32),
            pltpu.VMEM((units, ROWS, 128), f32),
            pltpu.VMEM((ROWS, 128), f32),
            pltpu.VMEM((ROWS, 128), f32),
            pltpu.VMEM((units, ROWS, LATENT), f32),
            pltpu.SemaphoreType.DMA((3,)),
        ],
        compiler_params=pltpu.CompilerParams(vmem_limit_bytes=48 << 20),
        cost_estimate=pl.CostEstimate(
            flops=units * ROWS * keys.shape[0] * 640,
            bytes_accessed=8 << 20,
            transcendentals=units * ROWS * keys.shape[0] // 2,
        ),
    )(spans, queries, keys, value_up)


def project_kernel(place_ref, rows_ref, w_ref, other_w_ref, after_ref, *refs):
    out_refs, sums = refs[:4], refs[4]
    z, head_z, head_core = place_ref[0], place_ref[1] // 2, place_ref[1] % 2
    for side, weights in enumerate((w_ref, other_w_ref)):
        sums[side] = lax.dot_general(
            rows_ref[...], weights[...], NT, preferred_element_type=jnp.float32
        )
    share = sums.shape[1] // 2
    for k, out_ref in enumerate(out_refs):
        to_z, to_core = (head_z + k // 2) % 2, (head_core + k) % 2
        side = jnp.where(to_z == z, 0, 1)
        rows = pl.ds(pl.multiple_of(to_core * share, share), share)
        out_ref[...] = sums[side, rows, :].astype(jnp.bfloat16)


def project(place, rows, weights, other_weights, after):
    smem = pl.BlockSpec(memory_space=pltpu.SMEM)
    vmem = pl.BlockSpec(memory_space=pltpu.VMEM)
    width, depth = weights.shape
    row_count = rows.shape[0]
    return pl.pallas_call(
        project_kernel,
        out_shape=(jax.ShapeDtypeStruct((row_count // 2, width), jnp.bfloat16),) * 4,
        in_specs=[smem, vmem, vmem, vmem, pl.BlockSpec(memory_space=pl.ANY)],
        out_specs=(vmem,) * 4,
        scratch_shapes=[pltpu.VMEM((2, row_count, width), jnp.float32)],
        compiler_params=pltpu.CompilerParams(vmem_limit_bytes=24 << 20),
        cost_estimate=pl.CostEstimate(
            flops=4 * row_count * depth * 256, bytes_accessed=8 << 20, transcendentals=0
        ),
    )(place, rows, weights, other_weights, after)


def share_out(k, part):
    pairs = [
        (ctx_index(z, x, y) * 4 + 2 * a + b, ctx_index(a ^ k // 2, x, y) * 4 + 2 * z + (b ^ k % 2))
        for z, x, y in places()
        for a in range(2)
        for b in range(2)
    ]
    return lax.ppermute(part, ("ctx", "grp"), pairs)


def body(
    prefill_queries,
    latents,
    rope_keys,
    span_slots,
    decode_queries,
    new_latents,
    new_rope,
    context_lengths,
    page_table,
    value_up,
    out_proj,
):
    ctx = lax.axis_index("ctx").astype(jnp.int32)
    grp = lax.axis_index("grp").astype(jnp.int32)
    rows_local = page_table.shape[0]
    own_spans = lax.dynamic_slice_in_dim(span_slots, 2 * ctx, 2)

    z = ctx // (X * Y)
    own = pack(latents, rope_keys)
    second = jnp.stack([own[1], from_other_z(own[1])])
    own_first = gather(own[0], "xy")
    other_first = from_other_z(own_first)
    second = gather(second, "xy").reshape(X * Y, 2, *own.shape[1:])
    weights = out_proj.T
    other_weights = from_other_z(weights)
    keys, decode_values = decode(
        z.reshape(1),
        span_slots,
        page_table,
        context_lengths,
        own_first.reshape(X * Y, *own.shape[1:]),
        other_first.reshape(X * Y, *own.shape[1:]),
        second,
        decode_queries,
        new_latents,
        new_rope,
        value_up,
    )
    all_values = gather(decode_values, "xy").reshape(-1, decode_values.shape[1])
    prefill_values, prefill_done = prefill(own_spans, prefill_queries, keys, value_up)
    place = jnp.stack([z, grp])
    parts = project(place, all_values, weights, other_weights, prefill_done)
    summed = sum(share_out(k, part).astype(jnp.float32) for k, part in enumerate(parts))
    decoded = summed.astype(jnp.bfloat16).reshape(-1, 2, rows_local, summed.shape[1])
    decoded = decoded.transpose(1, 0, 2, 3).reshape(2, -1, summed.shape[1])
    return (prefill_values, decoded)


def solution(mesh):
    placed = (
        P("ctx", "grp"),
        P("ctx", "grp"),
        P("ctx", None),
        P(),
        P(None, "ctx", "grp"),
        P(None, "ctx", "grp"),
        P(None, "ctx", None),
        P("ctx"),
        P("ctx", None),
        P("grp", None, None),
        P("grp", "ctx"),
    )
    return jax.shard_map(
        body,
        mesh=mesh,
        in_specs=placed,
        out_specs=(P("ctx", "grp"), P(None, "grp", "ctx")),
        check_vma=False,
    )
```

```python
import functools
import itertools
import math

import jax
import jax.numpy as jnp
from jax import lax
from jax.experimental import pallas as pl
from jax.experimental.pallas import tpu as pltpu
from jax.sharding import PartitionSpec as P

SPAN = 64
LATENT = 256
ROPE = 64
KEYW = LATENT + ROPE
KPAD = 384
VDIM = 128

HEADS_TILE = 8
ROWS = HEADS_TILE * SPAN
KEYS = 1024

EXP2_SCALE = 192.0 ** -0.5 * math.log2(math.e)
FAR_BELOW = -1e30
NT = (((1,), (1,)), ((), ()))
Z, X, Y = 2, 4, 4


def ctx_index(z, x, y):
    return z * (X * Y) + x * Y + y


def places():
    return [(z, x, y) for z in range(Z) for x in range(X) for y in range(Y)]


def from_other_z(value):
    pairs = [(ctx_index(z, x, y), ctx_index(1 - z, x, y)) for z, x, y in places()]
    return lax.ppermute(value, "ctx", pairs)


def gather(block, axes):
    lines = {}
    for z, x, y in places():
        at = (z, None if "x" in axes else x, None if "y" in axes else y)
        lines.setdefault(at, []).append(ctx_index(z, x, y))
    groups = list(lines.values())
    copies = jnp.broadcast_to(block[None], (len(groups[0]),) + block.shape)
    return lax.all_to_all(
        copies, "ctx", split_axis=0, concat_axis=0, axis_index_groups=groups, tiled=True
    )


def pack_kernel(latents_ref, rope_ref, out_ref):
    rope = rope_ref[...].astype(jnp.float32).T
    for span in range(2):
        rows = slice(span * SPAN, (span + 1) * SPAN)
        out_ref[span, :SPAN, :] = latents_ref[rows, :]
        parts = [rope[span * SPAN + c * 16 : span * SPAN + (c + 1) * 16] for c in range(4)]
        out_ref[span, SPAN:, :] = jnp.concatenate(parts, axis=1).astype(jnp.bfloat16)


def pack(latents, rope_keys):
    return pl.pallas_call(
        pack_kernel,
        out_shape=jax.ShapeDtypeStruct((2, SPAN + SPAN // 4, LATENT), jnp.bfloat16),
    )(latents, rope_keys.T)


def decode_kernel(
    z_ref,
    spans_ref,
    pages_ref,
    lengths_ref,
    own_first_ref,
    other_first_ref,
    second_ref,
    q_ref,
    new_latents_ref,
    new_rope_ref,
    up_hbm,
    keys_hbm,
    values_ref,
    up_ref,
    keys_ref,
    queries,
    fresh,
    cache,
    att,
    sems,
):
    low_lanes = lax.broadcasted_iota(jnp.int32, (16, 128), 1) < ROPE
    up_copy = pltpu.make_async_copy(up_hbm, up_ref, sems.at[0])
    up_copy.start()
    for half, dz, line in itertools.product(range(2), range(2), range(X * Y)):
        block = own_first_ref.at[line] if half == 0 else second_ref.at[line, dz]
        if half == 0 and dz == 1:
            block = other_first_ref.at[line]
        z = z_ref[0] if dz == 0 else 1 - z_ref[0]
        span = spans_ref[2 * (z * (X * Y) + line) + half]
        rows = pl.ds(pl.multiple_of(span * SPAN, SPAN), SPAN)
        keys_ref[rows, :LATENT] = block[:SPAN, :]
        packed = block[SPAN:, :].astype(jnp.float32)
        parts = []
        for c in range(2):
            two = packed[:, c * 128 : (c + 1) * 128]
            parts.append(jnp.where(low_lanes, two, 0.0))
            parts.append(jnp.where(low_lanes, pltpu.roll(two, 64, 1), 0.0))
        keys_ref[rows, LATENT:] = jnp.concatenate(parts, axis=0).astype(jnp.bfloat16)
    keys_copy = pltpu.make_async_copy(keys_ref, keys_hbm, sems.at[1])
    keys_copy.start()

    rows_local, pages = pages_ref.shape
    slots = pages * SPAN
    width = cache.shape[1]
    fresh[...] = jnp.zeros_like(fresh)
    for s in range(2):
        for h in range(32):
            at = h // 2 * 2 * KEYW + h % 2 * 256
            rows = q_ref[s, :, at : at + KPAD].astype(jnp.float32)
            if h % 2:
                rows = pltpu.roll(rows, KPAD - 64, 1)
            for c in range(3):
                queries[c, pl.ds(s * 32 + h, rows_local, stride=64), :] = rows[
                    :, c * 128 : (c + 1) * 128
                ]
        mine = pl.ds(s, rows_local, stride=16)
        latent_rows = new_latents_ref[s].astype(jnp.float32)
        fresh[0, mine, :] = latent_rows[:, :128]
        fresh[1, mine, :] = latent_rows[:, 128:]
        rope_rows = new_rope_ref[s].astype(jnp.float32)
        fresh[2, mine, :] = jnp.concatenate([rope_rows, jnp.zeros_like(rope_rows)], axis=1)

    def whole(ref, rows):
        return jnp.concatenate([ref[c, rows, :] for c in range(3)], axis=1).astype(jnp.bfloat16)

    cols = lax.broadcasted_iota(jnp.int32, (64, width), 1)
    step = lax.broadcasted_iota(jnp.int32, (64, width), 0) // 32
    fresh_seen = (cols >= slots) & (cols - slots <= step)
    for b in range(rows_local):
        for j in range(pages):
            page = pages_ref[b, j]
            cache[b, j * SPAN : (j + 1) * SPAN, :] = keys_ref[
                pl.ds(pl.multiple_of(page * SPAN, SPAN), SPAN), :
            ]
        cache[b, slots : slots + 16, :] = whole(fresh, slice(b * 16, (b + 1) * 16))
        cache[b, slots + 16 :, :] = jnp.zeros((width - slots - 16, KPAD), jnp.bfloat16)
        row_queries = whole(queries, slice(b * 64, (b + 1) * 64))
        scores = lax.dot_general(row_queries, cache[b], NT, preferred_element_type=jnp.float32)
        seen = (cols < lengths_ref[b]) | fresh_seen
        scores = jnp.where(seen, scores, FAR_BELOW)
        top = jnp.max(scores, axis=1, keepdims=True)
        weights = jnp.exp2(scores * EXP2_SCALE - top * EXP2_SCALE)
        total = jnp.sum(weights, axis=1, keepdims=True)
        attended = jnp.dot(
            weights.astype(jnp.bfloat16), cache[b, :, :LATENT], preferred_element_type=jnp.float32
        )
        attended = attended / total
        for s in range(2):
            for c in range(2):
                att[c, pl.ds(s * rows_local + b, 32, stride=16), :] = attended[
                    s * 32 : (s + 1) * 32, c * 128 : (c + 1) * 128
                ]
    up_copy.wait()
    for h in range(32):
        mine = slice(h * 16, (h + 1) * 16)
        attended = jnp.concatenate([att[0, mine, :], att[1, mine, :]], axis=1)
        values_ref[:, h * VDIM : (h + 1) * VDIM] = jnp.dot(
            attended.astype(jnp.bfloat16), up_ref[h], preferred_element_type=jnp.float32
        ).astype(jnp.bfloat16)
    keys_copy.wait()


def decode(
    z, spans, pages, lengths, own_first, other_first, second, queries, latents, rope, value_up
):
    smem = pl.BlockSpec(memory_space=pltpu.SMEM)
    vmem = pl.BlockSpec(memory_space=pltpu.VMEM)
    hbm = pl.BlockSpec(memory_space=pltpu.HBM)
    rows_local = pages.shape[0]
    heads = value_up.shape[0]
    return pl.pallas_call(
        decode_kernel,
        out_shape=(
            jax.ShapeDtypeStruct((spans.shape[0] * SPAN, KPAD), jnp.bfloat16),
            jax.ShapeDtypeStruct((2 * rows_local, heads * VDIM), jnp.bfloat16),
        ),
        in_specs=[smem] * 4 + [vmem] * 6 + [hbm],
        out_specs=(hbm, vmem),
        scratch_shapes=[
            pltpu.VMEM(value_up.shape, jnp.bfloat16),
            pltpu.VMEM((spans.shape[0] * SPAN, KPAD), jnp.bfloat16),
            pltpu.VMEM((3, 64 * rows_local, 128), jnp.float32),
            pltpu.VMEM((3, 16 * rows_local, 128), jnp.float32),
            pltpu.VMEM((rows_local, pages.shape[1] * SPAN + 128, KPAD), jnp.bfloat16),
            pltpu.VMEM((2, 16 * heads, 128), jnp.float32),
            pltpu.SemaphoreType.DMA((2,)),
        ],
        compiler_params=pltpu.CompilerParams(vmem_limit_bytes=59 << 20),
        cost_estimate=pl.CostEstimate(
            flops=2 * 8 * 64 * 1152 * 640, bytes_accessed=12 << 20, transcendentals=8 * 64 * 1152
        ),
    )(
        z, spans, pages, lengths, own_first, other_first, second, queries, latents, rope, value_up
    )


def prefill_kernel(spans_ref, q_hbm, k_hbm, up_hbm, out_ref, done_ref, *scratch):
    q_ref, k_ref, up_ref, qs, s_a, s_b, p_a, p_b, top, total, r_a, r_b, acc, sems = scratch
    q_copy = pltpu.make_async_copy(q_hbm, q_ref, sems.at[0])
    k_copy = pltpu.make_async_copy(k_hbm, k_ref, sems.at[1])
    up_copy = pltpu.make_async_copy(up_hbm, up_ref, sems.at[2])
    q_copy.start()
    k_copy.start()
    up_copy.start()
    top[...] = jnp.full(top.shape, FAR_BELOW, jnp.float32)
    total[...] = jnp.zeros_like(total)
    acc[...] = jnp.zeros_like(acc)
    p_b[...] = jnp.zeros_like(p_b)
    r_b[...] = jnp.ones_like(r_b)
    q_copy.wait()
    tiles = acc.shape[0] // 2
    span_of = [spans_ref[s] for s in range(2)]
    blocks_of = [span // (KEYS // SPAN) for span in span_of]

    for tile in range(tiles):
        for pair in range(HEADS_TILE // 2):
            at = (tile * HEADS_TILE + pair * 2) * KEYW
            for s in range(2):
                tokens = slice(s * SPAN, (s + 1) * SPAN)
                rows = qs.at[2 * tile + s]
                rows[2 * pair * SPAN : (2 * pair + 1) * SPAN, :] = q_ref[tokens, at : at + KPAD]
                odd = q_ref[tokens, at + 256 : at + 640].astype(jnp.float32)
                rows[(2 * pair + 1) * SPAN : (2 * pair + 2) * SPAN, :] = pltpu.roll(
                    odd, KPAD - 64, 1
                ).astype(jnp.bfloat16)

    def key_rows(block):
        return pl.ds(pl.multiple_of(block * KEYS, KEYS), KEYS)

    def score(unit, block, s_ref):
        s_ref[...] = lax.dot_general(
            qs[unit], k_ref[key_rows(block), :], NT, preferred_element_type=jnp.float32
        )

    lead = lax.broadcasted_iota(jnp.int32, (SPAN, 128), 1)
    lead = lead - lax.broadcasted_iota(jnp.int32, (SPAN, 128), 0)

    def weigh(unit, s_ref, p_ref, r_ref, last_key=None):
        for h in range(HEADS_TILE):
            rows = slice(h * SPAN, (h + 1) * SPAN)
            parts = [s_ref[rows, c * 128 : (c + 1) * 128] for c in range(KEYS // 128)]
            if last_key is not None:
                parts = [
                    jnp.where(lead <= last_key - c * 128, part, FAR_BELOW)
                    for c, part in enumerate(parts)
                ]
            highest = functools.reduce(jnp.maximum, parts)
            old = top[unit, rows]
            new = jnp.maximum(old, jnp.max(highest, axis=1, keepdims=True))
            top[unit, rows] = new
            scaled = new * EXP2_SCALE
            rescale = jnp.exp2(old * EXP2_SCALE - scaled)
            r_ref[rows] = rescale
            weights = [jnp.exp2(part * EXP2_SCALE - scaled) for part in parts]
            total[unit, rows] = total[unit, rows] * rescale + sum(weights)
            for c, weight in enumerate(weights):
                p_ref[rows, c * 128 : (c + 1) * 128] = weight.astype(jnp.bfloat16)

    def add_values(unit, block, p_ref, r_ref):
        product = jnp.dot(
            p_ref[...], k_ref[key_rows(block), :LATENT], preferred_element_type=jnp.float32
        )
        r = r_ref[...]
        acc[unit, :, :128] = acc[unit, :, :128] * r + product[:, :128]
        acc[unit, :, 128:] = acc[unit, :, 128:] * r + product[:, 128:]

    k_copy.wait()

    def last_item(unit):
        return unit, jnp.where(unit % 2 == 0, blocks_of[0], blocks_of[1])

    def following(item):
        unit, block = item
        ends = block + 1 >= jnp.where(unit % 2 == 0, blocks_of[0], blocks_of[1])
        other = 1 - unit % 2
        other_empty = jnp.where(other == 0, blocks_of[0], blocks_of[1]) == 0
        jump = jnp.where(other_empty, 2, 1)
        unit = jnp.where(ends, unit + jump, unit)
        return unit, jnp.where(ends, 0, block + 1)

    def two_items(i, carry):
        before, here = carry[:2], carry[2:]
        after = following(here)
        score(*after, s_b)
        weigh(here[0], s_a, p_a, r_a)
        add_values(*before, p_b, r_b)
        later = following(after)
        at_end = later[0] >= 2 * tiles
        later = tuple(jnp.where(at_end, end, value) for end, value in zip(last_item(0), later))
        score(*later, s_a)
        weigh(after[0], s_b, p_b, r_b)
        add_values(*here, p_a, r_a)
        return after + later

    all_blocks = blocks_of[0] + blocks_of[1]
    first = (jnp.where(blocks_of[0] == 0, 1, 0), jnp.int32(0))
    first = tuple(
        jnp.where(all_blocks == 0, end, value) for end, value in zip(last_item(0), first)
    )
    score(*first, s_a)
    carry = lax.fori_loop(
        0, all_blocks * (tiles // 2), two_items, (jnp.int32(0), jnp.int32(0)) + first
    )

    def two_last(i, carry):
        before = carry
        even, odd = last_item(2 * i), last_item(2 * i + 1)
        later = last_item(jnp.minimum(2 * i + 2, 2 * tiles - 1))
        offset = [(span_of[s] - blocks_of[s] * (KEYS // SPAN)) * SPAN for s in range(2)]
        score(*odd, s_b)
        weigh(even[0], s_a, p_a, r_a, offset[0])
        add_values(*before, p_b, r_b)
        score(*later, s_a)
        weigh(odd[0], s_b, p_b, r_b, offset[1])
        add_values(*even, p_a, r_a)
        return odd

    before = lax.fori_loop(0, tiles, two_last, carry[:2])
    add_values(*before, p_b, r_b)

    up_copy.wait()

    def finish(tile, carry):
        for s in range(2):
            unit = 2 * tile + s
            attended = acc[unit] / jnp.sum(total[unit], axis=1, keepdims=True)
            attended = attended.astype(jnp.bfloat16)
            values = [
                jnp.dot(
                    attended[h * SPAN : (h + 1) * SPAN],
                    up_ref[tile * HEADS_TILE + h],
                    preferred_element_type=jnp.float32,
                ).astype(jnp.bfloat16)
                for h in range(HEADS_TILE)
            ]
            columns = HEADS_TILE * VDIM
            out_ref[
                s * SPAN : (s + 1) * SPAN, pl.ds(pl.multiple_of(tile * columns, columns), columns)
            ] = jnp.concatenate(values, axis=1)
        return carry

    lax.fori_loop(0, tiles, finish, 0)
    done_ref[...] = jnp.zeros_like(done_ref)


def prefill(spans, queries, keys, value_up):
    tokens = queries.shape[0]
    heads = value_up.shape[0]
    units = 2 * heads // HEADS_TILE
    f32 = jnp.float32
    smem = pl.BlockSpec(memory_space=pltpu.SMEM)
    vmem = pl.BlockSpec(memory_space=pltpu.VMEM)
    return pl.pallas_call(
        prefill_kernel,
        out_shape=(
            jax.ShapeDtypeStruct((tokens, heads * VDIM), jnp.bfloat16),
            jax.ShapeDtypeStruct((8, 128), f32),
        ),
        in_specs=[smem] + [pl.BlockSpec(memory_space=pltpu.HBM)] * 3,
        out_specs=(vmem, vmem),
        scratch_shapes=[
            pltpu.VMEM(queries.shape, jnp.bfloat16),
            pltpu.VMEM(keys.shape, jnp.bfloat16),
            pltpu.VMEM(value_up.shape, jnp.bfloat16),
            pltpu.VMEM((units, ROWS, KPAD), jnp.bfloat16),
            pltpu.VMEM((ROWS, KEYS), f32),
            pltpu.VMEM((ROWS, KEYS), f32),
            pltpu.VMEM((ROWS, KEYS), jnp.bfloat16),
            pltpu.VMEM((ROWS, KEYS), jnp.bfloat16),
            pltpu.VMEM((units, ROWS, 128), f32),
            pltpu.VMEM((units, ROWS, 128), f32),
            pltpu.VMEM((ROWS, 128), f32),
            pltpu.VMEM((ROWS, 128), f32),
            pltpu.VMEM((units, ROWS, LATENT), f32),
            pltpu.SemaphoreType.DMA((3,)),
        ],
        compiler_params=pltpu.CompilerParams(vmem_limit_bytes=59 << 20),
        cost_estimate=pl.CostEstimate(
            flops=units * ROWS * keys.shape[0] * 640,
            bytes_accessed=8 << 20,
            transcendentals=units * ROWS * keys.shape[0] // 2,
        ),
    )(spans, queries, keys, value_up)


def project_kernel(place_ref, rows_ref, w_hbm, other_w_hbm, after_ref, *refs):
    out_refs, (w_ref, sums, sems) = refs[:4], refs[4:]
    copies = [
        pltpu.make_async_copy(weights, w_ref.at[side], sems.at[side])
        for side, weights in enumerate((w_hbm, other_w_hbm))
    ]
    for copy in copies:
        copy.start()
    z, head_z, head_core = place_ref[0], place_ref[1] // 2, place_ref[1] % 2
    for side, copy in enumerate(copies):
        copy.wait()
        sums[side] = lax.dot_general(
            rows_ref[...], w_ref[side], NT, preferred_element_type=jnp.float32
        )
    share = sums.shape[1] // 2
    for k, out_ref in enumerate(out_refs):
        to_z, to_core = (head_z + k // 2) % 2, (head_core + k) % 2
        side = jnp.where(to_z == z, 0, 1)
        rows = pl.ds(pl.multiple_of(to_core * share, share), share)
        out_ref[...] = sums[side, rows, :].astype(jnp.bfloat16)


def project(place, rows, weights, other_weights, after):
    smem = pl.BlockSpec(memory_space=pltpu.SMEM)
    vmem = pl.BlockSpec(memory_space=pltpu.VMEM)
    hbm = pl.BlockSpec(memory_space=pltpu.HBM)
    width, depth = weights.shape
    row_count = rows.shape[0]
    return pl.pallas_call(
        project_kernel,
        out_shape=(jax.ShapeDtypeStruct((row_count // 2, width), jnp.bfloat16),) * 4,
        in_specs=[smem, vmem, hbm, hbm, pl.BlockSpec(memory_space=pl.ANY)],
        out_specs=(vmem,) * 4,
        scratch_shapes=[
            pltpu.VMEM((2, width, depth), jnp.bfloat16),
            pltpu.VMEM((2, row_count, width), jnp.float32),
            pltpu.SemaphoreType.DMA((2,)),
        ],
        compiler_params=pltpu.CompilerParams(vmem_limit_bytes=59 << 20),
        cost_estimate=pl.CostEstimate(
            flops=4 * row_count * depth * 256, bytes_accessed=8 << 20, transcendentals=0
        ),
    )(place, rows, weights, other_weights, after)


def share_out(k, part):
    pairs = [
        (ctx_index(z, x, y) * 4 + 2 * a + b, ctx_index(a ^ k // 2, x, y) * 4 + 2 * z + (b ^ k % 2))
        for z, x, y in places()
        for a in range(2)
        for b in range(2)
    ]
    return lax.ppermute(part, ("ctx", "grp"), pairs)


def body(
    prefill_queries,
    latents,
    rope_keys,
    span_slots,
    decode_queries,
    new_latents,
    new_rope,
    context_lengths,
    page_table,
    value_up,
    out_proj,
):
    ctx = lax.axis_index("ctx").astype(jnp.int32)
    grp = lax.axis_index("grp").astype(jnp.int32)
    rows_local = page_table.shape[0]
    own_spans = lax.dynamic_slice_in_dim(span_slots, 2 * ctx, 2)

    z = ctx // (X * Y)
    own = pack(latents, rope_keys)
    second = jnp.stack([own[1], from_other_z(own[1])])
    own_first = gather(own[0], "xy")
    other_first = from_other_z(own_first)
    second = gather(second, "xy").reshape(X * Y, 2, *own.shape[1:])
    weights = out_proj.T
    other_weights = from_other_z(weights)
    keys, decode_values = decode(
        z.reshape(1),
        span_slots,
        page_table,
        context_lengths,
        own_first.reshape(X * Y, *own.shape[1:]),
        other_first.reshape(X * Y, *own.shape[1:]),
        second,
        decode_queries,
        new_latents,
        new_rope,
        value_up,
    )
    all_values = gather(decode_values, "xy").reshape(-1, decode_values.shape[1])
    prefill_values, prefill_done = prefill(own_spans, prefill_queries, keys, value_up)
    place = jnp.stack([z, grp])
    parts = project(place, all_values, weights, other_weights, prefill_done)
    summed = sum(share_out(k, part).astype(jnp.float32) for k, part in enumerate(parts))
    decoded = summed.astype(jnp.bfloat16).reshape(-1, 2, rows_local, summed.shape[1])
    decoded = decoded.transpose(1, 0, 2, 3).reshape(2, -1, summed.shape[1])
    return (prefill_values, decoded)


def solution(mesh):
    placed = (
        P("ctx", "grp"),
        P("ctx", "grp"),
        P("ctx", None),
        P(),
        P(None, "ctx", "grp"),
        P(None, "ctx", "grp"),
        P(None, "ctx", None),
        P("ctx"),
        P("ctx", None),
        P("grp", None, None),
        P("grp", "ctx"),
    )
    return jax.shard_map(
        body,
        mesh=mesh,
        in_specs=placed,
        out_specs=(P("ctx", "grp"), P(None, "grp", "ctx")),
        check_vma=False,
    )
```

```python
import functools
import itertools
import math

import jax
import jax.numpy as jnp
from jax import lax
from jax.experimental import pallas as pl
from jax.experimental.pallas import tpu as pltpu
from jax.sharding import PartitionSpec as P

SPAN = 64
LATENT = 256
ROPE = 64
KEYW = LATENT + ROPE
KPAD = 384
VDIM = 128

HEADS_TILE = 8
ROWS = HEADS_TILE * SPAN
KEYS = 512

EXP2_SCALE = 192.0 ** -0.5 * math.log2(math.e)
FAR_BELOW = -1e30
NT = (((1,), (1,)), ((), ()))


def swap(value, mask):
    size = lax.axis_size("ctx")
    return lax.ppermute(value, "ctx", [(i, i ^ mask) for i in range(size)])


def gather_caches(own):
    other = swap(own, 16)
    held = [jnp.stack([own[half], other[half]]) for half in range(2)]
    for step in range(2):
        for half in range(2):
            mask = (1 << step, 4 << step)[half]
            held[half] = jnp.concatenate([held[half], swap(held[half], mask)])
    far = [[], []]
    for k in (2, 1, 3):
        for half in range(2):
            far[half].append(swap(held[half], (4 * k, k)[half]))
    return [held[0], *far[0]], [held[1], *far[1]]


def block_masks(half):
    first, last = ((1, 4), (4, 1))[half]
    near = [dz * 16 + k * first for k in range(4) for dz in range(2)]
    return [mask + k * last for k in (0, 2, 1, 3) for mask in near]


def gather_values(values):
    size = lax.axis_size("ctx")
    groups = [list(range(z * size // 2, (z + 1) * size // 2)) for z in range(2)]
    return lax.all_gather(values, "ctx", axis=0, tiled=True, axis_index_groups=groups)


def pack_kernel(latents_ref, rope_ref, out_ref):
    rope = rope_ref[...].astype(jnp.float32).T
    for span in range(2):
        rows = slice(span * SPAN, (span + 1) * SPAN)
        out_ref[span, :SPAN, :] = latents_ref[rows, :]
        parts = [rope[span * SPAN + c * 16 : span * SPAN + (c + 1) * 16] for c in range(4)]
        out_ref[span, SPAN:, :] = jnp.concatenate(parts, axis=1).astype(jnp.bfloat16)


def pack(latents, rope_keys):
    return pl.pallas_call(
        pack_kernel,
        out_shape=jax.ShapeDtypeStruct((2, SPAN + SPAN // 4, LATENT), jnp.bfloat16),
    )(latents, rope_keys.T)


def decode_kernel(
    place_ref,
    spans_ref,
    pages_ref,
    lengths_ref,
    *refs,
):
    piece_refs, refs = refs[:8], refs[8:]
    q_ref, new_latents_ref, new_rope_ref, up_hbm, keys_hbm, values_ref = refs[:6]
    up_ref, keys_ref, queries, fresh, cache, att, sems = refs[6:]
    low_lanes = lax.broadcasted_iota(jnp.int32, (16, 128), 1) < ROPE
    up_copy = pltpu.make_async_copy(up_hbm, up_ref, sems.at[0])
    up_copy.start()
    for half, n in itertools.product(range(2), range(32)):
        block = piece_refs[4 * half + n // 8].at[n % 8]
        span = spans_ref[2 * (place_ref[0] ^ block_masks(half)[n]) + half]
        rows = pl.ds(pl.multiple_of(span * SPAN, SPAN), SPAN)
        keys_ref[rows, :LATENT] = block[:SPAN, :]
        packed = block[SPAN:, :].astype(jnp.float32)
        parts = []
        for c in range(2):
            two = packed[:, c * 128 : (c + 1) * 128]
            parts.append(jnp.where(low_lanes, two, 0.0))
            parts.append(jnp.where(low_lanes, pltpu.roll(two, 64, 1), 0.0))
        keys_ref[rows, LATENT:] = jnp.concatenate(parts, axis=0).astype(jnp.bfloat16)
    keys_copy = pltpu.make_async_copy(keys_ref, keys_hbm, sems.at[1])
    keys_copy.start()

    rows_local, pages = pages_ref.shape
    slots = pages * SPAN
    width = cache.shape[1]
    fresh[...] = jnp.zeros_like(fresh)
    for s in range(2):
        for h in range(32):
            at = h // 2 * 2 * KEYW + h % 2 * 256
            rows = q_ref[s, :, at : at + KPAD].astype(jnp.float32)
            if h % 2:
                rows = pltpu.roll(rows, KPAD - 64, 1)
            for c in range(3):
                queries[c, pl.ds(s * 32 + h, rows_local, stride=64), :] = rows[
                    :, c * 128 : (c + 1) * 128
                ]
        mine = pl.ds(s, rows_local, stride=16)
        latent_rows = new_latents_ref[s].astype(jnp.float32)
        fresh[0, mine, :] = latent_rows[:, :128]
        fresh[1, mine, :] = latent_rows[:, 128:]
        rope_rows = new_rope_ref[s].astype(jnp.float32)
        fresh[2, mine, :] = jnp.concatenate([rope_rows, jnp.zeros_like(rope_rows)], axis=1)

    def whole(ref, rows):
        return jnp.concatenate([ref[c, rows, :] for c in range(3)], axis=1).astype(jnp.bfloat16)

    cols = lax.broadcasted_iota(jnp.int32, (64, width), 1)
    step = lax.broadcasted_iota(jnp.int32, (64, width), 0) // 32
    fresh_seen = (cols >= slots) & (cols - slots <= step)
    for b in range(rows_local):
        for j in range(pages):
            page = pages_ref[b, j]
            cache[b, j * SPAN : (j + 1) * SPAN, :] = keys_ref[
                pl.ds(pl.multiple_of(page * SPAN, SPAN), SPAN), :
            ]
        cache[b, slots : slots + 16, :] = whole(fresh, slice(b * 16, (b + 1) * 16))
        cache[b, slots + 16 :, :] = jnp.zeros((width - slots - 16, KPAD), jnp.bfloat16)
        row_queries = whole(queries, slice(b * 64, (b + 1) * 64))
        scores = lax.dot_general(row_queries, cache[b], NT, preferred_element_type=jnp.float32)
        seen = (cols < lengths_ref[b]) | fresh_seen
        scores = jnp.where(seen, scores, FAR_BELOW)
        top = jnp.max(scores, axis=1, keepdims=True)
        weights = jnp.exp2(scores * EXP2_SCALE - top * EXP2_SCALE)
        total = jnp.sum(weights, axis=1, keepdims=True)
        attended = jnp.dot(
            weights.astype(jnp.bfloat16), cache[b, :, :LATENT], preferred_element_type=jnp.float32
        )
        attended = attended / total
        for s in range(2):
            for c in range(2):
                att[c, pl.ds(s * rows_local + b, 32, stride=16), :] = attended[
                    s * 32 : (s + 1) * 32, c * 128 : (c + 1) * 128
                ]
    up_copy.wait()
    for h in range(32):
        mine = slice(h * 16, (h + 1) * 16)
        attended = jnp.concatenate([att[0, mine, :], att[1, mine, :]], axis=1)
        values_ref[:, h * VDIM : (h + 1) * VDIM] = jnp.dot(
            attended.astype(jnp.bfloat16), up_ref[h], preferred_element_type=jnp.float32
        ).astype(jnp.bfloat16)
    keys_copy.wait()


def decode(ctx, spans, pages, lengths, pieces, queries, latents, rope, value_up):
    smem = pl.BlockSpec(memory_space=pltpu.SMEM)
    vmem = pl.BlockSpec(memory_space=pltpu.VMEM)
    hbm = pl.BlockSpec(memory_space=pl.ANY)
    rows_local = pages.shape[0]
    heads = value_up.shape[0]
    return pl.pallas_call(
        decode_kernel,
        out_shape=(
            jax.ShapeDtypeStruct((spans.shape[0] * SPAN, KPAD), jnp.bfloat16),
            jax.ShapeDtypeStruct((2 * rows_local, heads * VDIM), jnp.bfloat16),
        ),
        in_specs=[smem] * 4 + [vmem] * 11 + [hbm],
        out_specs=(pl.BlockSpec(memory_space=pltpu.HBM), vmem),
        scratch_shapes=[
            pltpu.VMEM(value_up.shape, jnp.bfloat16),
            pltpu.VMEM((spans.shape[0] * SPAN, KPAD), jnp.bfloat16),
            pltpu.VMEM((3, 64 * rows_local, 128), jnp.float32),
            pltpu.VMEM((3, 16 * rows_local, 128), jnp.float32),
            pltpu.VMEM((rows_local, pages.shape[1] * SPAN + 128, KPAD), jnp.bfloat16),
            pltpu.VMEM((2, 16 * heads, 128), jnp.float32),
            pltpu.SemaphoreType.DMA((2,)),
        ],
        compiler_params=pltpu.CompilerParams(vmem_limit_bytes=48 << 20),
        cost_estimate=pl.CostEstimate(
            flops=2 * 8 * 64 * 1152 * 640, bytes_accessed=12 << 20, transcendentals=8 * 64 * 1152
        ),
    )(ctx, spans, pages, lengths, *pieces, queries, latents, rope, value_up)


def prefill_kernel(spans_ref, q_hbm, k_hbm, up_hbm, out_ref, done_ref, *scratch):
    q_ref, k_ref, up_ref, qs, s_a, s_b, p_a, p_b, top, total, r_a, r_b, acc, sems = scratch
    tiles = acc.shape[0] // 2
    columns, rows = q_ref.shape[1] // tiles, k_ref.shape[0] // tiles
    q_copies, k_copies = [], []
    for tile in range(tiles):
        part = (slice(None), slice(tile * columns, (tile + 1) * columns))
        q_copies.append(pltpu.make_async_copy(q_hbm.at[part], q_ref.at[part], sems.at[0, tile]))
        part = slice(tile * rows, (tile + 1) * rows)
        k_copies.append(pltpu.make_async_copy(k_hbm.at[part], k_ref.at[part], sems.at[1, tile]))
    up_copy = pltpu.make_async_copy(up_hbm, up_ref, sems.at[2, 0])
    for copy in q_copies + k_copies + [up_copy]:
        copy.start()
    top[...] = jnp.full(top.shape, FAR_BELOW, jnp.float32)
    total[...] = jnp.zeros_like(total)
    acc[...] = jnp.zeros_like(acc)
    p_b[...] = jnp.zeros_like(p_b)
    r_b[...] = jnp.ones_like(r_b)
    span_of = [spans_ref[s] for s in range(2)]
    blocks_of = [span // (KEYS // SPAN) for span in span_of]

    for tile in range(tiles):
        q_copies[tile].wait()
        for pair in range(HEADS_TILE // 2):
            at = (tile * HEADS_TILE + pair * 2) * KEYW
            for s in range(2):
                tokens = slice(s * SPAN, (s + 1) * SPAN)
                rows = qs.at[2 * tile + s]
                rows[2 * pair * SPAN : (2 * pair + 1) * SPAN, :] = q_ref[tokens, at : at + KPAD]
                odd = q_ref[tokens, at + 256 : at + 640].astype(jnp.float32)
                rows[(2 * pair + 1) * SPAN : (2 * pair + 2) * SPAN, :] = pltpu.roll(
                    odd, KPAD - 64, 1
                ).astype(jnp.bfloat16)

    def key_rows(block):
        return pl.ds(pl.multiple_of(block * KEYS, KEYS), KEYS)

    def score(unit, block, s_ref):
        s_ref[...] = lax.dot_general(
            qs[unit], k_ref[key_rows(block), :], NT, preferred_element_type=jnp.float32
        )

    lead = lax.broadcasted_iota(jnp.int32, (SPAN, 128), 1)
    lead = lead - lax.broadcasted_iota(jnp.int32, (SPAN, 128), 0)

    def weigh(unit, s_ref, p_ref, r_ref, last_key=None):
        for h in range(HEADS_TILE):
            rows = slice(h * SPAN, (h + 1) * SPAN)
            parts = [s_ref[rows, c * 128 : (c + 1) * 128] for c in range(KEYS // 128)]
            if last_key is not None:
                parts = [
                    jnp.where(lead <= last_key - c * 128, part, FAR_BELOW)
                    for c, part in enumerate(parts)
                ]
            highest = functools.reduce(jnp.maximum, parts)
            old = top[unit, rows]
            new = jnp.maximum(old, jnp.max(highest, axis=1, keepdims=True))
            top[unit, rows] = new
            scaled = new * EXP2_SCALE
            rescale = jnp.exp2(old * EXP2_SCALE - scaled)
            r_ref[rows] = rescale
            weights = [jnp.exp2(part * EXP2_SCALE - scaled) for part in parts]
            total[unit, rows] = total[unit, rows] * rescale + sum(weights)
            for c, weight in enumerate(weights):
                p_ref[rows, c * 128 : (c + 1) * 128] = weight.astype(jnp.bfloat16)

    def add_values(unit, block, p_ref, r_ref):
        product = jnp.dot(
            p_ref[...], k_ref[key_rows(block), :LATENT], preferred_element_type=jnp.float32
        )
        r = r_ref[...]
        acc[unit, :, :128] = acc[unit, :, :128] * r + product[:, :128]
        acc[unit, :, 128:] = acc[unit, :, 128:] * r + product[:, 128:]

    for copy in k_copies:
        copy.wait()

    def last_item(unit):
        return unit, jnp.where(unit % 2 == 0, blocks_of[0], blocks_of[1])

    def following(item):
        unit, block = item
        ends = block + 1 >= jnp.where(unit % 2 == 0, blocks_of[0], blocks_of[1])
        other = 1 - unit % 2
        other_empty = jnp.where(other == 0, blocks_of[0], blocks_of[1]) == 0
        jump = jnp.where(other_empty, 2, 1)
        unit = jnp.where(ends, unit + jump, unit)
        return unit, jnp.where(ends, 0, block + 1)

    def two_items(i, carry):
        before, here = carry[:2], carry[2:]
        after = following(here)
        score(*after, s_b)
        weigh(here[0], s_a, p_a, r_a)
        add_values(*before, p_b, r_b)
        later = following(after)
        at_end = later[0] >= 2 * tiles
        later = tuple(jnp.where(at_end, end, value) for end, value in zip(last_item(0), later))
        score(*later, s_a)
        weigh(after[0], s_b, p_b, r_b)
        add_values(*here, p_a, r_a)
        return after + later

    all_blocks = blocks_of[0] + blocks_of[1]
    first = (jnp.where(blocks_of[0] == 0, 1, 0), jnp.int32(0))
    first = tuple(
        jnp.where(all_blocks == 0, end, value) for end, value in zip(last_item(0), first)
    )
    score(*first, s_a)
    carry = lax.fori_loop(
        0, all_blocks * (tiles // 2), two_items, (jnp.int32(0), jnp.int32(0)) + first
    )

    def two_last(i, carry):
        before = carry
        even, odd = last_item(2 * i), last_item(2 * i + 1)
        later = last_item(jnp.minimum(2 * i + 2, 2 * tiles - 1))
        offset = [(span_of[s] - blocks_of[s] * (KEYS // SPAN)) * SPAN for s in range(2)]
        score(*odd, s_b)
        weigh(even[0], s_a, p_a, r_a, offset[0])
        add_values(*before, p_b, r_b)
        score(*later, s_a)
        weigh(odd[0], s_b, p_b, r_b, offset[1])
        add_values(*even, p_a, r_a)
        return odd

    before = lax.fori_loop(0, tiles, two_last, carry[:2])
    add_values(*before, p_b, r_b)

    up_copy.wait()

    def finish(tile, carry):
        for s in range(2):
            unit = 2 * tile + s
            attended = acc[unit] / jnp.sum(total[unit], axis=1, keepdims=True)
            attended = attended.astype(jnp.bfloat16)
            values = [
                jnp.dot(
                    attended[h * SPAN : (h + 1) * SPAN],
                    up_ref[tile * HEADS_TILE + h],
                    preferred_element_type=jnp.float32,
                ).astype(jnp.bfloat16)
                for h in range(HEADS_TILE)
            ]
            columns = HEADS_TILE * VDIM
            out_ref[
                s * SPAN : (s + 1) * SPAN, pl.ds(pl.multiple_of(tile * columns, columns), columns)
            ] = jnp.concatenate(values, axis=1)
        return carry

    lax.fori_loop(0, tiles, finish, 0)
    done_ref[...] = jnp.zeros_like(done_ref)


def prefill(spans, queries, keys, value_up):
    tokens = queries.shape[0]
    heads = value_up.shape[0]
    units = 2 * heads // HEADS_TILE
    f32 = jnp.float32
    smem = pl.BlockSpec(memory_space=pltpu.SMEM)
    vmem = pl.BlockSpec(memory_space=pltpu.VMEM)
    return pl.pallas_call(
        prefill_kernel,
        out_shape=(
            jax.ShapeDtypeStruct((tokens, heads * VDIM), jnp.bfloat16),
            jax.ShapeDtypeStruct((8, 128), f32),
        ),
        in_specs=[smem] + [pl.BlockSpec(memory_space=pltpu.HBM)] * 3,
        out_specs=(vmem, vmem),
        scratch_shapes=[
            pltpu.VMEM(queries.shape, jnp.bfloat16),
            pltpu.VMEM(keys.shape, jnp.bfloat16),
            pltpu.VMEM(value_up.shape, jnp.bfloat16),
            pltpu.VMEM((units, ROWS, KPAD), jnp.bfloat16),
            pltpu.VMEM((ROWS, KEYS), f32),
            pltpu.VMEM((ROWS, KEYS), f32),
            pltpu.VMEM((ROWS, KEYS), jnp.bfloat16),
            pltpu.VMEM((ROWS, KEYS), jnp.bfloat16),
            pltpu.VMEM((units, ROWS, 128), f32),
            pltpu.VMEM((units, ROWS, 128), f32),
            pltpu.VMEM((ROWS, 128), f32),
            pltpu.VMEM((ROWS, 128), f32),
            pltpu.VMEM((units, ROWS, LATENT), f32),
            pltpu.SemaphoreType.DMA((3, units // 2)),
        ],
        compiler_params=pltpu.CompilerParams(vmem_limit_bytes=59 << 20),
        cost_estimate=pl.CostEstimate(
            flops=units * ROWS * keys.shape[0] * 640,
            bytes_accessed=8 << 20,
            transcendentals=units * ROWS * keys.shape[0] // 2,
        ),
    )(spans, queries, keys, value_up)


def project_kernel(place_ref, rows_hbm, w_hbm, other_w_hbm, after_ref, *refs):
    out_refs, (rows_ref, w_ref, sums, sems) = refs[:4], refs[4:]
    chunks = sems.shape[1]
    width = rows_ref.shape[1] // chunks
    parts = [(slice(None), slice(c * width, (c + 1) * width)) for c in range(chunks)]
    sides = ((rows_hbm, rows_ref), (w_hbm, w_ref.at[0]), (other_w_hbm, w_ref.at[1]))
    copies = [
        [
            pltpu.make_async_copy(source.at[part], target.at[part], sems.at[i, c])
            for i, (source, target) in enumerate(sides)
        ]
        for c, part in enumerate(parts)
    ]
    for three in copies:
        for copy in three:
            copy.start()
    z, head_z, head_core = place_ref[0], place_ref[1] // 2, place_ref[1] % 2
    for c, part in enumerate(parts):
        for copy in copies[c]:
            copy.wait()
        for side in range(2):
            product = lax.dot_general(
                rows_ref[part], w_ref[side, :, part[1]], NT, preferred_element_type=jnp.float32
            )
            sums[side] = product if c == 0 else sums[side] + product
    share = sums.shape[1] // 2
    for k, out_ref in enumerate(out_refs):
        to_z, to_core = (head_z + k // 2) % 2, (head_core + k) % 2
        side = jnp.where(to_z == z, 0, 1)
        rows = pl.ds(pl.multiple_of(to_core * share, share), share)
        out_ref[...] = sums[side, rows, :].astype(jnp.bfloat16)


def project(place, rows, weights, other_weights, after):
    smem = pl.BlockSpec(memory_space=pltpu.SMEM)
    vmem = pl.BlockSpec(memory_space=pltpu.VMEM)
    hbm = pl.BlockSpec(memory_space=pltpu.HBM)
    width, depth = weights.shape
    row_count = rows.shape[0]
    return pl.pallas_call(
        project_kernel,
        out_shape=(jax.ShapeDtypeStruct((row_count // 2, width), jnp.bfloat16),) * 4,
        in_specs=[smem, hbm, hbm, hbm, pl.BlockSpec(memory_space=pl.ANY)],
        out_specs=(vmem,) * 4,
        scratch_shapes=[
            pltpu.VMEM(rows.shape, jnp.bfloat16),
            pltpu.VMEM((2, width, depth), jnp.bfloat16),
            pltpu.VMEM((2, row_count, width), jnp.float32),
            pltpu.SemaphoreType.DMA((3, 4)),
        ],
        compiler_params=pltpu.CompilerParams(vmem_limit_bytes=59 << 20),
        cost_estimate=pl.CostEstimate(
            flops=4 * row_count * depth * 256, bytes_accessed=8 << 20, transcendentals=0
        ),
    )(place, rows, weights, other_weights, after)


def share_out(k, part):
    pairs = []
    for ctx in range(lax.axis_size("ctx")):
        z, line = divmod(ctx, 16)
        for a in range(2):
            for b in range(2):
                to = ((a ^ k // 2) * 16 + line) * 4 + 2 * z + (b ^ k % 2)
                pairs.append((ctx * 4 + 2 * a + b, to))
    return lax.ppermute(part, ("ctx", "grp"), pairs)


def body(
    prefill_queries,
    latents,
    rope_keys,
    span_slots,
    decode_queries,
    new_latents,
    new_rope,
    context_lengths,
    page_table,
    value_up,
    out_proj,
):
    ctx = lax.axis_index("ctx").astype(jnp.int32)
    grp = lax.axis_index("grp").astype(jnp.int32)
    rows_local = page_table.shape[0]
    own_spans = lax.dynamic_slice_in_dim(span_slots, 2 * ctx, 2)

    first, second = gather_caches(pack(latents, rope_keys))
    keys, decode_values = decode(
        ctx.reshape(1),
        span_slots,
        page_table,
        context_lengths,
        first + second,
        decode_queries,
        new_latents,
        new_rope,
        value_up,
    )
    weights = out_proj.T
    other_weights = swap(weights, 16)
    all_values = gather_values(decode_values)
    prefill_values, prefill_done = prefill(own_spans, prefill_queries, keys, value_up)
    place = jnp.stack([ctx // 16, grp])
    parts = project(place, all_values, weights, other_weights, prefill_done)
    summed = sum(share_out(k, part).astype(jnp.float32) for k, part in enumerate(parts))
    decoded = summed.astype(jnp.bfloat16).reshape(-1, 2, rows_local, summed.shape[1])
    decoded = decoded.transpose(1, 0, 2, 3).reshape(2, -1, summed.shape[1])
    return (prefill_values, decoded)


def solution(mesh):
    placed = (
        P("ctx", "grp"),
        P("ctx", "grp"),
        P("ctx", None),
        P(),
        P(None, "ctx", "grp"),
        P(None, "ctx", "grp"),
        P(None, "ctx", None),
        P("ctx"),
        P("ctx", None),
        P("grp", None, None),
        P("grp", "ctx"),
    )
    return jax.shard_map(
        body,
        mesh=mesh,
        in_specs=placed,
        out_specs=(P("ctx", "grp"), P(None, "grp", "ctx")),
        check_vma=False,
    )
```

```python
import functools
import math

import jax
import jax.numpy as jnp
from jax import lax
from jax.experimental import pallas as pl
from jax.experimental.pallas import tpu as pltpu
from jax.sharding import PartitionSpec as P

SPAN = 64
LATENT = 256
ROPE = 64
KEYW = LATENT + ROPE
KPAD = 384
VDIM = 128

HEADS_TILE = 8
ROWS = HEADS_TILE * SPAN
KEYS = 512

EXP2_SCALE = 192.0 ** -0.5 * math.log2(math.e)
FAR_BELOW = -1e30
NT = (((1,), (1,)), ((), ()))


def swap(value, mask):
    size = lax.axis_size("ctx")
    return lax.ppermute(value, "ctx", [(i, i ^ mask) for i in range(size)])


def gather_caches(own):
    def copies(block):
        return jnp.broadcast_to(block[None], (lax.axis_size("ctx"),) + block.shape)

    def exchange(blocks):
        return lax.all_to_all(blocks, "ctx", split_axis=0, concat_axis=0, tiled=True)

    first, second = lax.optimization_barrier((copies(own[0]), own[1]))
    return exchange(first), exchange(copies(second))


def gather_values(values):
    size = lax.axis_size("ctx")
    groups = [list(range(z * size // 2, (z + 1) * size // 2)) for z in range(2)]
    copies = jnp.broadcast_to(values[None], (size // 2,) + values.shape)
    gathered = lax.all_to_all(
        copies, "ctx", split_axis=0, concat_axis=0, axis_index_groups=groups, tiled=True
    )
    return gathered.reshape(-1, values.shape[1])


def pack_kernel(latents_ref, rope_ref, out_ref):
    rope = rope_ref[...].astype(jnp.float32).T
    for span in range(2):
        rows = slice(span * SPAN, (span + 1) * SPAN)
        out_ref[span, :SPAN, :] = latents_ref[rows, :]
        parts = [rope[span * SPAN + c * 16 : span * SPAN + (c + 1) * 16] for c in range(4)]
        out_ref[span, SPAN:, :] = jnp.concatenate(parts, axis=1).astype(jnp.bfloat16)


def pack(latents, rope_keys):
    return pl.pallas_call(
        pack_kernel,
        out_shape=jax.ShapeDtypeStruct((2, SPAN + SPAN // 4, LATENT), jnp.bfloat16),
    )(latents, rope_keys.T)


def copies_in_parts(source, target, sems, axis=0):
    parts = sems.shape[0]
    size = source.shape[axis] // parts
    where = [(slice(None),) * axis + (slice(i * size, (i + 1) * size),) for i in range(parts)]
    return [
        pltpu.make_async_copy(source.at[at], target.at[at], sems.at[i])
        for i, at in enumerate(where)
    ]


def start(copies):
    for copy in copies:
        copy.start()


def wait(copies):
    for copy in copies:
        copy.wait()


def unpack(block, keys_ref, place):
    rows = pl.ds(pl.multiple_of(place * SPAN, SPAN), SPAN)
    keys_ref[rows, :LATENT] = block[:SPAN, :]
    packed = block[SPAN:, :].astype(jnp.float32)
    low_lanes = lax.broadcasted_iota(jnp.int32, (16, 128), 1) < ROPE
    parts = []
    for c in range(2):
        two = packed[:, c * 128 : (c + 1) * 128]
        parts.append(jnp.where(low_lanes, two, 0.0))
        parts.append(jnp.where(low_lanes, pltpu.roll(two, 64, 1), 0.0))
    keys_ref[rows, LATENT:] = jnp.concatenate(parts, axis=0).astype(jnp.bfloat16)


def decode_kernel(spans_ref, places_ref, pages_ref, lengths_ref, *refs):
    q_ref, new_latents_ref, new_rope_ref, blocks_hbm, first_hbm, up_hbm = refs[:6]
    second_hbm, values_ref = refs[6:8]
    blocks_ref, up_ref, keys_ref, queries, fresh, cache, att, sems = refs[8:]
    half_rows = first_hbm.shape[0]
    blocks_copies = copies_in_parts(blocks_hbm, blocks_ref, sems.at[0])
    first_copies = copies_in_parts(first_hbm, keys_ref.at[:half_rows], sems.at[1])
    up_copies = copies_in_parts(up_hbm, up_ref, sems.at[2])
    start(blocks_copies + first_copies + up_copies)

    rows_local, pages = pages_ref.shape
    slots = pages * SPAN
    width = cache.shape[1]
    fresh[...] = jnp.zeros_like(fresh)
    for s in range(2):
        for h in range(32):
            at = h // 2 * 2 * KEYW + h % 2 * 256
            rows = q_ref[s, :, at : at + KPAD].astype(jnp.float32)
            if h % 2:
                rows = pltpu.roll(rows, KPAD - 64, 1)
            for c in range(3):
                queries[c, pl.ds(s * 32 + h, rows_local, stride=64), :] = rows[
                    :, c * 128 : (c + 1) * 128
                ]
        mine = pl.ds(s, rows_local, stride=16)
        latent_rows = new_latents_ref[s].astype(jnp.float32)
        fresh[0, mine, :] = latent_rows[:, :128]
        fresh[1, mine, :] = latent_rows[:, 128:]
        rope_rows = new_rope_ref[s].astype(jnp.float32)
        fresh[2, mine, :] = jnp.concatenate([rope_rows, jnp.zeros_like(rope_rows)], axis=1)

    wait(blocks_copies)
    for n in range(blocks_ref.shape[0]):
        unpack(blocks_ref.at[n], keys_ref, places_ref[spans_ref[2 * n + 1]])
    second_copies = copies_in_parts(keys_ref.at[half_rows:], second_hbm, sems.at[3])
    start(second_copies)
    wait(first_copies)

    def whole(ref, rows):
        return jnp.concatenate([ref[c, rows, :] for c in range(3)], axis=1).astype(jnp.bfloat16)

    cols = lax.broadcasted_iota(jnp.int32, (64, width), 1)
    step = lax.broadcasted_iota(jnp.int32, (64, width), 0) // 32
    fresh_seen = (cols >= slots) & (cols - slots <= step)
    for b in range(rows_local):
        for j in range(pages):
            page = places_ref[pages_ref[b, j]]
            cache[b, j * SPAN : (j + 1) * SPAN, :] = keys_ref[
                pl.ds(pl.multiple_of(page * SPAN, SPAN), SPAN), :
            ]
        cache[b, slots : slots + 16, :] = whole(fresh, slice(b * 16, (b + 1) * 16))
        cache[b, slots + 16 :, :] = jnp.zeros((width - slots - 16, KPAD), jnp.bfloat16)
        row_queries = whole(queries, slice(b * 64, (b + 1) * 64))
        scores = lax.dot_general(row_queries, cache[b], NT, preferred_element_type=jnp.float32)
        seen = (cols < lengths_ref[b]) | fresh_seen
        scores = jnp.where(seen, scores, FAR_BELOW)
        top = jnp.max(scores, axis=1, keepdims=True)
        weights = jnp.exp2(scores * EXP2_SCALE - top * EXP2_SCALE)
        total = jnp.sum(weights, axis=1, keepdims=True)
        attended = jnp.dot(
            weights.astype(jnp.bfloat16), cache[b, :, :LATENT], preferred_element_type=jnp.float32
        )
        attended = attended / total
        for s in range(2):
            for c in range(2):
                att[c, pl.ds(s * rows_local + b, 32, stride=16), :] = attended[
                    s * 32 : (s + 1) * 32, c * 128 : (c + 1) * 128
                ]
    wait(up_copies)
    for h in range(32):
        mine = slice(h * 16, (h + 1) * 16)
        attended = jnp.concatenate([att[0, mine, :], att[1, mine, :]], axis=1)
        values_ref[:, h * VDIM : (h + 1) * VDIM] = jnp.dot(
            attended.astype(jnp.bfloat16), up_ref[h], preferred_element_type=jnp.float32
        ).astype(jnp.bfloat16)
    wait(second_copies)


def decode(spans, places, pages, lengths, queries, latents, rope, blocks, first_keys, value_up):
    smem = pl.BlockSpec(memory_space=pltpu.SMEM)
    vmem = pl.BlockSpec(memory_space=pltpu.VMEM)
    hbm = pl.BlockSpec(memory_space=pltpu.HBM)
    rows_local = pages.shape[0]
    heads = value_up.shape[0]
    half_rows = first_keys.shape[0]
    return pl.pallas_call(
        decode_kernel,
        out_shape=(
            jax.ShapeDtypeStruct((half_rows, KPAD), jnp.bfloat16),
            jax.ShapeDtypeStruct((2 * rows_local, heads * VDIM), jnp.bfloat16),
        ),
        in_specs=[smem] * 4 + [vmem] * 3 + [hbm] * 3,
        out_specs=(hbm, vmem),
        scratch_shapes=[
            pltpu.VMEM(blocks.shape, jnp.bfloat16),
            pltpu.VMEM(value_up.shape, jnp.bfloat16),
            pltpu.VMEM((2 * half_rows, KPAD), jnp.bfloat16),
            pltpu.VMEM((3, 64 * rows_local, 128), jnp.float32),
            pltpu.VMEM((3, 16 * rows_local, 128), jnp.float32),
            pltpu.VMEM((rows_local, pages.shape[1] * SPAN + 128, KPAD), jnp.bfloat16),
            pltpu.VMEM((2, 16 * heads, 128), jnp.float32),
            pltpu.SemaphoreType.DMA((4, 4)),
        ],
        compiler_params=pltpu.CompilerParams(vmem_limit_bytes=59 << 20),
        cost_estimate=pl.CostEstimate(
            flops=2 * 8 * 64 * 1152 * 640, bytes_accessed=12 << 20, transcendentals=8 * 64 * 1152
        ),
    )(spans, places, pages, lengths, queries, latents, rope, blocks, first_keys, value_up)


def split_queries(q_ref, qs, tile):
    for pair in range(HEADS_TILE // 2):
        at = (tile * HEADS_TILE + pair * 2) * KEYW
        for s in range(2):
            tokens = slice(s * SPAN, (s + 1) * SPAN)
            rows = qs.at[2 * tile + s]
            rows[2 * pair * SPAN : (2 * pair + 1) * SPAN, :] = q_ref[tokens, at : at + KPAD]
            odd = q_ref[tokens, at + 256 : at + 640].astype(jnp.float32)
            rows[(2 * pair + 1) * SPAN : (2 * pair + 2) * SPAN, :] = pltpu.roll(
                odd, KPAD - 64, 1
            ).astype(jnp.bfloat16)


def clear(top, total, acc, p_b, r_b):
    top[...] = jnp.full(top.shape, FAR_BELOW, jnp.float32)
    total[...] = jnp.zeros_like(total)
    acc[...] = jnp.zeros_like(acc)
    p_b[...] = jnp.zeros_like(p_b)
    r_b[...] = jnp.ones_like(r_b)


def sweep(half, ctx_ref, spans_ref, places_ref, k_ref, qs, work, unit_weighed, unit_added):
    s_a, s_b, p_a, p_b, top, total, r_a, r_b, acc = work
    tiles = acc.shape[0] // 2
    half_spans = spans_ref.shape[0] // 2
    per_block = KEYS // SPAN
    blocks_of, offset_of = [], []
    for s in range(2):
        span = spans_ref[2 * ctx_ref[0] + s]
        rank = places_ref[span] - s * half_spans
        before = rank if s == half else span - rank
        blocks_of.append(jnp.minimum(before // per_block, half_spans // per_block - 1))
        last_seen = before * SPAN - (0 if s == half else 1)
        offset_of.append(last_seen - blocks_of[s] * KEYS)

    def key_rows(block):
        return pl.ds(pl.multiple_of(block * KEYS, KEYS), KEYS)

    def score(unit, block, s_ref):
        s_ref[...] = lax.dot_general(
            qs[unit], k_ref[key_rows(block), :], NT, preferred_element_type=jnp.float32
        )

    lane = lax.broadcasted_iota(jnp.int32, (SPAN, 128), 1)
    lead_of = [lane, lane]
    lead_of[half] = lane - lax.broadcasted_iota(jnp.int32, (SPAN, 128), 0)

    def weigh(unit, s_ref, p_ref, r_ref, s=None):
        for h in range(HEADS_TILE):
            rows = slice(h * SPAN, (h + 1) * SPAN)
            parts = [s_ref[rows, c * 128 : (c + 1) * 128] for c in range(KEYS // 128)]
            if s is not None:
                parts = [
                    jnp.where(lead_of[s] <= offset_of[s] - c * 128, part, FAR_BELOW)
                    for c, part in enumerate(parts)
                ]
            highest = functools.reduce(jnp.maximum, parts)
            old = top[unit, rows]
            new = jnp.maximum(old, jnp.max(highest, axis=1, keepdims=True))
            top[unit, rows] = new
            scaled = new * EXP2_SCALE
            rescale = jnp.exp2(old * EXP2_SCALE - scaled)
            r_ref[rows] = rescale
            weights = [jnp.exp2(part * EXP2_SCALE - scaled) for part in parts]
            total[unit, rows] = total[unit, rows] * rescale + sum(weights)
            for c, weight in enumerate(weights):
                p_ref[rows, c * 128 : (c + 1) * 128] = weight.astype(jnp.bfloat16)

    def add_values(unit, block, p_ref, r_ref):
        product = jnp.dot(
            p_ref[...], k_ref[key_rows(block), :LATENT], preferred_element_type=jnp.float32
        )
        r = r_ref[...]
        acc[unit, :, :128] = acc[unit, :, :128] * r + product[:, :128]
        acc[unit, :, 128:] = acc[unit, :, 128:] * r + product[:, 128:]

    def last_item(unit):
        return unit, jnp.where(unit % 2 == 0, blocks_of[0], blocks_of[1])

    def following(item):
        unit, block = item
        ends = block + 1 >= jnp.where(unit % 2 == 0, blocks_of[0], blocks_of[1])
        other = 1 - unit % 2
        other_empty = jnp.where(other == 0, blocks_of[0], blocks_of[1]) == 0
        jump = jnp.where(other_empty, 2, 1)
        unit = jnp.where(ends, unit + jump, unit)
        return unit, jnp.where(ends, 0, block + 1)

    def two_items(i, carry):
        before, here = carry[:2], carry[2:]
        after = following(here)
        score(*after, s_b)
        weigh(here[0], s_a, p_a, r_a)
        add_values(*before, p_b, r_b)
        later = following(after)
        at_end = later[0] >= 2 * tiles
        later = tuple(jnp.where(at_end, end, value) for end, value in zip(last_item(0), later))
        score(*later, s_a)
        weigh(after[0], s_b, p_b, r_b)
        add_values(*here, p_a, r_a)
        return after + later

    all_blocks = blocks_of[0] + blocks_of[1]
    first = (jnp.where(blocks_of[0] == 0, 1, 0), jnp.int32(0))
    first = tuple(
        jnp.where(all_blocks == 0, end, value) for end, value in zip(last_item(0), first)
    )
    score(*first, s_a)
    carry = lax.fori_loop(
        0, all_blocks * (tiles // 2), two_items, (jnp.int32(0), jnp.int32(0)) + first
    )

    def two_last(i, carry):
        before = carry
        even, odd = last_item(2 * i), last_item(2 * i + 1)
        later = last_item(jnp.minimum(2 * i + 2, 2 * tiles - 1))
        score(*odd, s_b)
        weigh(even[0], s_a, p_a, r_a, 0)
        unit_weighed(even[0])
        add_values(*before, p_b, r_b)

        @pl.when(i > 0)
        def _():
            unit_added(before[0])

        score(*later, s_a)
        weigh(odd[0], s_b, p_b, r_b, 1)
        unit_weighed(odd[0])
        add_values(*even, p_a, r_a)
        unit_added(even[0])
        return odd

    before = lax.fori_loop(0, tiles, two_last, carry[:2])
    add_values(*before, p_b, r_b)
    unit_added(before[0])


def first_prefill_kernel(ctx_ref, spans_ref, q_hbm, blocks_hbm, *refs):
    places_ref, keys_hbm, acc_hbm, state_hbm = refs[:4]
    q_ref, blocks_ref, k_ref, qs, state, *work = refs[4:-3]
    slots_ref, sems, out_sems = refs[-3:]
    p_b, top, total, r_b, acc = work[3], work[4], work[5], work[7], work[8]
    blocks_copies = copies_in_parts(blocks_hbm, blocks_ref, sems.at[0])
    q_copies = copies_in_parts(q_hbm, q_ref, sems.at[1], axis=1)
    start(blocks_copies + q_copies)
    slots = spans_ref.shape[0]
    for slot in range(slots):
        slots_ref[spans_ref[slot]] = slot
    counts = [jnp.int32(0), jnp.int32(slots // 2)]
    for span in range(slots):
        odd = slots_ref[span] % 2
        places_ref[span] = jnp.where(odd == 0, counts[0], counts[1])
        counts = [counts[0] + 1 - odd, counts[1] + odd]
    clear(top, total, acc, p_b, r_b)
    wait(blocks_copies)
    for n in range(slots // 2):
        unpack(blocks_ref.at[n], k_ref, places_ref[spans_ref[2 * n]])
    keys_copies = copies_in_parts(k_ref, keys_hbm, sems.at[2])
    start(keys_copies)
    for tile, copy in enumerate(q_copies):
        copy.wait()
        split_queries(q_ref, qs, tile)
    low_lanes = lax.broadcasted_iota(jnp.int32, (ROWS, 128), 1) < 64

    def state_copy(unit):
        return pltpu.make_async_copy(state.at[unit], state_hbm.at[unit], out_sems.at[0, unit])

    def acc_copy(unit):
        return pltpu.make_async_copy(acc.at[unit], acc_hbm.at[unit], out_sems.at[1, unit])

    def unit_weighed(unit):
        sums = jnp.sum(total[unit], axis=1, keepdims=True)
        state[unit] = jnp.where(low_lanes, top[unit], sums)
        state_copy(unit).start()

    sweep(
        0,
        ctx_ref,
        spans_ref,
        places_ref,
        k_ref,
        qs,
        work,
        unit_weighed,
        lambda unit: acc_copy(unit).start(),
    )
    wait(keys_copies)
    for unit in range(acc.shape[0]):
        state_copy(unit).wait()
        acc_copy(unit).wait()


def second_prefill_kernel(ctx_ref, spans_ref, places_ref, q_hbm, keys_hbm, *refs):
    up_hbm, acc_hbm, state_hbm, out_ref, done_ref = refs[:5]
    q_ref, k_ref, up_ref, first_acc, first_state, qs, *work = refs[5:-1]
    sems = refs[-1]
    p_b, top, total, r_b, acc = work[3], work[4], work[5], work[7], work[8]
    tiles = acc.shape[0] // 2
    q_copies = copies_in_parts(q_hbm, q_ref, sems.at[0], axis=1)
    keys_copies = copies_in_parts(keys_hbm, k_ref, sems.at[1])
    late_copies = copies_in_parts(up_hbm, up_ref, sems.at[2])
    late_copies += copies_in_parts(acc_hbm, first_acc, sems.at[3])
    late_copies += copies_in_parts(state_hbm, first_state, sems.at[4])
    start(q_copies + keys_copies + late_copies)
    clear(top, total, acc, p_b, r_b)
    for tile, copy in enumerate(q_copies):
        copy.wait()
        split_queries(q_ref, qs, tile)
    wait(keys_copies)
    sweep(
        1,
        ctx_ref,
        spans_ref,
        places_ref,
        k_ref,
        qs,
        work,
        lambda unit: None,
        lambda unit: None,
    )
    wait(late_copies)

    def finish(tile, carry):
        for s in range(2):
            unit = 2 * tile + s
            first_top = first_state[unit, :, :1]
            first_total = first_state[unit, :, 64:65]
            highest = jnp.maximum(top[unit], first_top)
            first_scale = jnp.exp2((first_top - highest) * EXP2_SCALE)
            second_scale = jnp.exp2((top[unit] - highest) * EXP2_SCALE)
            second_total = jnp.sum(total[unit], axis=1, keepdims=True)
            whole = first_scale * first_total + second_scale * second_total
            first_scale, second_scale = first_scale / whole, second_scale / whole
            attended = [
                acc[unit, :, cols] * second_scale + first_acc[unit, :, cols] * first_scale
                for cols in (slice(0, 128), slice(128, 256))
            ]
            attended = jnp.concatenate(attended, axis=1).astype(jnp.bfloat16)
            values = [
                jnp.dot(
                    attended[h * SPAN : (h + 1) * SPAN],
                    up_ref[tile * HEADS_TILE + h],
                    preferred_element_type=jnp.float32,
                ).astype(jnp.bfloat16)
                for h in range(HEADS_TILE)
            ]
            columns = HEADS_TILE * VDIM
            out_ref[
                s * SPAN : (s + 1) * SPAN, pl.ds(pl.multiple_of(tile * columns, columns), columns)
            ] = jnp.concatenate(values, axis=1)
        return carry

    lax.fori_loop(0, tiles, finish, 0)
    done_ref[...] = jnp.zeros_like(done_ref)


def work_shapes(units):
    f32 = jnp.float32
    return [
        pltpu.VMEM((ROWS, KEYS), f32),
        pltpu.VMEM((ROWS, KEYS), f32),
        pltpu.VMEM((ROWS, KEYS), jnp.bfloat16),
        pltpu.VMEM((ROWS, KEYS), jnp.bfloat16),
        pltpu.VMEM((units, ROWS, 128), f32),
        pltpu.VMEM((units, ROWS, 128), f32),
        pltpu.VMEM((ROWS, 128), f32),
        pltpu.VMEM((ROWS, 128), f32),
        pltpu.VMEM((units, ROWS, LATENT), f32),
    ]


def prefill_cost(units, key_rows):
    return pl.CostEstimate(
        flops=2 * units * ROWS * key_rows * 640,
        bytes_accessed=16 << 20,
        transcendentals=units * ROWS * key_rows,
    )


def first_prefill(ctx, spans, queries, blocks, heads):
    units = 2 * heads // HEADS_TILE
    half_rows = blocks.shape[0] * SPAN
    f32 = jnp.float32
    smem = pl.BlockSpec(memory_space=pltpu.SMEM)
    hbm = pl.BlockSpec(memory_space=pltpu.HBM)
    return pl.pallas_call(
        first_prefill_kernel,
        out_shape=(
            jax.ShapeDtypeStruct(spans.shape, jnp.int32),
            jax.ShapeDtypeStruct((half_rows, KPAD), jnp.bfloat16),
            jax.ShapeDtypeStruct((units, ROWS, LATENT), f32),
            jax.ShapeDtypeStruct((units, ROWS, 128), f32),
        ),
        in_specs=[smem, smem, hbm, hbm],
        out_specs=(smem, hbm, hbm, hbm),
        scratch_shapes=[
            pltpu.VMEM(queries.shape, jnp.bfloat16),
            pltpu.VMEM(blocks.shape, jnp.bfloat16),
            pltpu.VMEM((half_rows, KPAD), jnp.bfloat16),
            pltpu.VMEM((units, ROWS, KPAD), jnp.bfloat16),
            pltpu.VMEM((units, ROWS, 128), f32),
        ]
        + work_shapes(units)
        + [
            pltpu.SMEM(spans.shape, jnp.int32),
            pltpu.SemaphoreType.DMA((3, units // 2)),
            pltpu.SemaphoreType.DMA((2, units)),
        ],
        compiler_params=pltpu.CompilerParams(vmem_limit_bytes=59 << 20),
        cost_estimate=prefill_cost(units, half_rows),
    )(ctx, spans, queries, blocks)


def second_prefill(ctx, spans, places, queries, keys, value_up, first_acc, first_state):
    tokens = queries.shape[0]
    heads = value_up.shape[0]
    units = first_acc.shape[0]
    f32 = jnp.float32
    smem = pl.BlockSpec(memory_space=pltpu.SMEM)
    vmem = pl.BlockSpec(memory_space=pltpu.VMEM)
    hbm = pl.BlockSpec(memory_space=pltpu.HBM)
    return pl.pallas_call(
        second_prefill_kernel,
        out_shape=(
            jax.ShapeDtypeStruct((tokens, heads * VDIM), jnp.bfloat16),
            jax.ShapeDtypeStruct((8, 128), f32),
        ),
        in_specs=[smem] * 3 + [hbm] * 5,
        out_specs=(vmem, vmem),
        scratch_shapes=[
            pltpu.VMEM(queries.shape, jnp.bfloat16),
            pltpu.VMEM(keys.shape, jnp.bfloat16),
            pltpu.VMEM(value_up.shape, jnp.bfloat16),
            pltpu.VMEM(first_acc.shape, f32),
            pltpu.VMEM(first_state.shape, f32),
            pltpu.VMEM((units, ROWS, KPAD), jnp.bfloat16),
        ]
        + work_shapes(units)
        + [pltpu.SemaphoreType.DMA((5, units // 2))],
        compiler_params=pltpu.CompilerParams(vmem_limit_bytes=59 << 20),
        cost_estimate=prefill_cost(units, keys.shape[0]),
    )(ctx, spans, places, queries, keys, value_up, first_acc, first_state)


def project_kernel(ctx_ref, grp_ref, rows_hbm, w_hbm, other_w_hbm, after_ref, *refs):
    out_refs, (rows_ref, w_ref, sums, sems) = refs[:4], refs[4:]
    chunks = sems.shape[1]
    width = rows_ref.shape[1] // chunks
    parts = [(slice(None), slice(c * width, (c + 1) * width)) for c in range(chunks)]
    sides = ((rows_hbm, rows_ref), (w_hbm, w_ref.at[0]), (other_w_hbm, w_ref.at[1]))
    copies = [
        [
            pltpu.make_async_copy(source.at[part], target.at[part], sems.at[i, c])
            for i, (source, target) in enumerate(sides)
        ]
        for c, part in enumerate(parts)
    ]
    for three in copies:
        for copy in three:
            copy.start()
    z, head_z, head_core = ctx_ref[0] // 16, grp_ref[0] // 2, grp_ref[0] % 2
    for c, part in enumerate(parts):
        for copy in copies[c]:
            copy.wait()
        for side in range(2):
            product = lax.dot_general(
                rows_ref[part], w_ref[side, :, part[1]], NT, preferred_element_type=jnp.float32
            )
            sums[side] = product if c == 0 else sums[side] + product
    share = sums.shape[1] // 2
    for k, out_ref in enumerate(out_refs):
        to_z, to_core = (head_z + k // 2) % 2, (head_core + k) % 2
        side = jnp.where(to_z == z, 0, 1)
        rows = pl.ds(pl.multiple_of(to_core * share, share), share)
        out_ref[...] = sums[side, rows, :].astype(jnp.bfloat16)


def project(ctx, grp, rows, weights, other_weights, after):
    smem = pl.BlockSpec(memory_space=pltpu.SMEM)
    vmem = pl.BlockSpec(memory_space=pltpu.VMEM)
    hbm = pl.BlockSpec(memory_space=pltpu.HBM)
    width, depth = weights.shape
    row_count = rows.shape[0]
    return pl.pallas_call(
        project_kernel,
        out_shape=(jax.ShapeDtypeStruct((row_count // 2, width), jnp.bfloat16),) * 4,
        in_specs=[smem, smem, hbm, hbm, hbm, pl.BlockSpec(memory_space=pl.ANY)],
        out_specs=(vmem,) * 4,
        scratch_shapes=[
            pltpu.VMEM(rows.shape, jnp.bfloat16),
            pltpu.VMEM((2, width, depth), jnp.bfloat16),
            pltpu.VMEM((2, row_count, width), jnp.float32),
            pltpu.SemaphoreType.DMA((3, 4)),
        ],
        compiler_params=pltpu.CompilerParams(vmem_limit_bytes=59 << 20),
        cost_estimate=pl.CostEstimate(
            flops=4 * row_count * depth * 256, bytes_accessed=8 << 20, transcendentals=0
        ),
    )(ctx, grp, rows, weights, other_weights, after)


def share_out(k, part):
    pairs = []
    for ctx in range(lax.axis_size("ctx")):
        z, line = divmod(ctx, 16)
        for a in range(2):
            for b in range(2):
                to = ((a ^ k // 2) * 16 + line) * 4 + 2 * z + (b ^ k % 2)
                pairs.append((ctx * 4 + 2 * a + b, to))
    return lax.ppermute(part, ("ctx", "grp"), pairs)


def body(
    prefill_queries,
    latents,
    rope_keys,
    span_slots,
    decode_queries,
    new_latents,
    new_rope,
    context_lengths,
    page_table,
    value_up,
    out_proj,
):
    ctx = lax.axis_index("ctx").astype(jnp.int32).reshape(1)
    grp = lax.axis_index("grp").astype(jnp.int32).reshape(1)
    heads = value_up.shape[0]
    rows_local = page_table.shape[0]

    own = pack(latents, rope_keys)
    first_blocks, second_blocks = gather_caches(own)
    weights, first_blocks = lax.optimization_barrier((out_proj.T, first_blocks))
    other_weights = swap(weights, 16)
    places, first_keys, first_acc, first_state = first_prefill(
        ctx, span_slots, prefill_queries, first_blocks, heads
    )
    second_keys, decode_values = decode(
        span_slots,
        places,
        page_table,
        context_lengths,
        decode_queries,
        new_latents,
        new_rope,
        second_blocks,
        first_keys,
        value_up,
    )
    all_values = gather_values(decode_values)
    prefill_values, prefill_done = second_prefill(
        ctx, span_slots, places, prefill_queries, second_keys, value_up, first_acc, first_state
    )
    parts = project(ctx, grp, all_values, weights, other_weights, prefill_done)
    summed = sum(share_out(k, part).astype(jnp.float32) for k, part in enumerate(parts))
    decoded = summed.astype(jnp.bfloat16).reshape(-1, 2, rows_local, summed.shape[1])
    decoded = decoded.transpose(1, 0, 2, 3).reshape(2, -1, summed.shape[1])
    return (prefill_values, decoded)


def solution(mesh):
    placed = (
        P("ctx", "grp"),
        P("ctx", "grp"),
        P("ctx", None),
        P(),
        P(None, "ctx", "grp"),
        P(None, "ctx", "grp"),
        P(None, "ctx", None),
        P("ctx"),
        P("ctx", None),
        P("grp", None, None),
        P("grp", "ctx"),
    )
    return jax.shard_map(
        body,
        mesh=mesh,
        in_specs=placed,
        out_specs=(P("ctx", "grp"), P(None, "grp", "ctx")),
        check_vma=False,
    )
```

```python
import functools
import math

import jax
import jax.numpy as jnp
from jax import lax
from jax.experimental import pallas as pl
from jax.experimental.pallas import tpu as pltpu
from jax.sharding import PartitionSpec as P

SPAN = 64
LATENT = 256
ROPE = 64
KEYW = LATENT + ROPE
KPAD = 384
VDIM = 128

HEADS_TILE = 8
ROWS = HEADS_TILE * SPAN
KEYS = 512

EXP2_SCALE = 192.0 ** -0.5 * math.log2(math.e)
FAR_BELOW = -1e30
NT = (((1,), (1,)), ((), ()))


def swap(value, mask):
    size = lax.axis_size("ctx")
    return lax.ppermute(value, "ctx", [(i, i ^ mask) for i in range(size)])


def exchange(block):
    size = lax.axis_size("ctx")
    groups = [list(range(z * size // 2, (z + 1) * size // 2)) for z in range(2)]
    copies = jnp.broadcast_to(block[None], (size // 2,) + block.shape)
    return lax.all_to_all(
        copies, "ctx", split_axis=0, concat_axis=0, axis_index_groups=groups, tiled=True
    )


def gather_caches(own):
    second = jnp.stack([own[1], swap(own[1], 16)])
    own_first = exchange(own[0])
    return own_first, swap(own_first, 16), exchange(second)


def pack_kernel(latents_ref, rope_ref, out_ref):
    rope = rope_ref[...].astype(jnp.float32).T
    for span in range(2):
        rows = slice(span * SPAN, (span + 1) * SPAN)
        out_ref[span, :SPAN, :] = latents_ref[rows, :]
        parts = [rope[span * SPAN + c * 16 : span * SPAN + (c + 1) * 16] for c in range(4)]
        out_ref[span, SPAN:, :] = jnp.concatenate(parts, axis=1).astype(jnp.bfloat16)


def pack(latents, rope_keys):
    return pl.pallas_call(
        pack_kernel,
        out_shape=jax.ShapeDtypeStruct((2, SPAN + SPAN // 4, LATENT), jnp.bfloat16),
    )(latents, rope_keys.T)


def copies_in_parts(source, target, sems, axis=0):
    parts = sems.shape[0]
    size = source.shape[axis] // parts
    where = [(slice(None),) * axis + (slice(i * size, (i + 1) * size),) for i in range(parts)]
    return [
        pltpu.make_async_copy(source.at[at], target.at[at], sems.at[i])
        for i, at in enumerate(where)
    ]


def start(copies):
    for copy in copies:
        copy.start()


def wait(copies):
    for copy in copies:
        copy.wait()


def unpack(block, keys_ref, place):
    rows = pl.ds(pl.multiple_of(place * SPAN, SPAN), SPAN)
    keys_ref[rows, :LATENT] = block[:SPAN, :]
    packed = block[SPAN:, :].astype(jnp.float32)
    low_lanes = lax.broadcasted_iota(jnp.int32, (16, 128), 1) < ROPE
    parts = []
    for c in range(2):
        two = packed[:, c * 128 : (c + 1) * 128]
        parts.append(jnp.where(low_lanes, two, 0.0))
        parts.append(jnp.where(low_lanes, pltpu.roll(two, 64, 1), 0.0))
    keys_ref[rows, LATENT:] = jnp.concatenate(parts, axis=0).astype(jnp.bfloat16)


def decode_kernel(ctx_ref, spans_ref, pages_ref, lengths_ref, *refs):
    q_ref, fresh_ref, *block_hbms, up_hbm, keys_hbm, values_ref = refs[:8]
    own_ref, other_ref, second_ref, up_ref, keys_ref, cache, att, sems = refs[8:]
    block_refs = own_ref, other_ref, second_ref
    block_copies = [
        copies_in_parts(source, target, sems.at[i])
        for i, (source, target) in enumerate(zip(block_hbms, block_refs))
    ]
    up_copies = copies_in_parts(up_hbm, up_ref, sems.at[3])
    start(sum(block_copies, []) + up_copies)
    rows_local, pages = pages_ref.shape
    slots = pages * SPAN
    width = cache.shape[1]
    for b in range(rows_local):
        cache[b, slots : slots + 16, :] = fresh_ref[b]
        cache[b, slots + 16 :, :] = jnp.zeros((width - slots - 16, KPAD), jnp.bfloat16)
    half = spans_ref.shape[0] // 2
    own_z = ctx_ref[0] // 16
    for i, copies in enumerate(block_copies):
        wait(copies)
        for n in range(block_refs[i].shape[0]):
            line = n % 16 if i < 2 else n // 2
            z = own_z if (i == 0 or (i == 2 and n % 2 == 0)) else 1 - own_z
            unpack(block_refs[i].at[n], keys_ref, spans_ref[2 * (z * 16 + line) + i // 2])
    keys_copies = copies_in_parts(keys_ref, keys_hbm, sems.at[4])
    start(keys_copies)

    cols = lax.broadcasted_iota(jnp.int32, (64, width), 1)
    step = lax.broadcasted_iota(jnp.int32, (64, width), 0) // 32
    fresh_seen = (cols >= slots) & (cols - slots <= step)
    for b in range(rows_local):
        for j in range(pages):
            page = pages_ref[b, j]
            cache[b, j * SPAN : (j + 1) * SPAN, :] = keys_ref[
                pl.ds(pl.multiple_of(page * SPAN, SPAN), SPAN), :
            ]
        scores = lax.dot_general(q_ref[b], cache[b], NT, preferred_element_type=jnp.float32)
        seen = (cols < lengths_ref[b]) | fresh_seen
        scores = jnp.where(seen, scores, FAR_BELOW)
        top = jnp.max(scores, axis=1, keepdims=True)
        weights = jnp.exp2(scores * EXP2_SCALE - top * EXP2_SCALE)
        total = jnp.sum(weights, axis=1, keepdims=True)
        attended = jnp.dot(
            weights.astype(jnp.bfloat16), cache[b, :, :LATENT], preferred_element_type=jnp.float32
        )
        attended = attended / total
        for s in range(2):
            for c in range(2):
                att[c, pl.ds(s * rows_local + b, 32, stride=16), :] = attended[
                    s * 32 : (s + 1) * 32, c * 128 : (c + 1) * 128
                ]
    wait(up_copies)
    for h in range(32):
        mine = slice(h * 16, (h + 1) * 16)
        attended = jnp.concatenate([att[0, mine, :], att[1, mine, :]], axis=1)
        values_ref[:, h * VDIM : (h + 1) * VDIM] = jnp.dot(
            attended.astype(jnp.bfloat16), up_ref[h], preferred_element_type=jnp.float32
        ).astype(jnp.bfloat16)
    wait(keys_copies)


def decode(ctx, spans, pages, lengths, queries, fresh, blocks, value_up):
    smem = pl.BlockSpec(memory_space=pltpu.SMEM)
    vmem = pl.BlockSpec(memory_space=pltpu.VMEM)
    hbm = pl.BlockSpec(memory_space=pltpu.HBM)
    rows_local = pages.shape[0]
    heads = value_up.shape[0]
    key_rows = spans.shape[0] * SPAN
    return pl.pallas_call(
        decode_kernel,
        out_shape=(
            jax.ShapeDtypeStruct((key_rows, KPAD), jnp.bfloat16),
            jax.ShapeDtypeStruct((2 * rows_local, heads * VDIM), jnp.bfloat16),
        ),
        in_specs=[smem] * 4 + [vmem] * 2 + [hbm] * 4,
        out_specs=(hbm, vmem),
        scratch_shapes=[pltpu.VMEM(block.shape, jnp.bfloat16) for block in blocks]
        + [
            pltpu.VMEM(value_up.shape, jnp.bfloat16),
            pltpu.VMEM((key_rows, KPAD), jnp.bfloat16),
            pltpu.VMEM((rows_local, pages.shape[1] * SPAN + 128, KPAD), jnp.bfloat16),
            pltpu.VMEM((2, 16 * heads, 128), jnp.float32),
            pltpu.SemaphoreType.DMA((5, 4)),
        ],
        compiler_params=pltpu.CompilerParams(vmem_limit_bytes=59 << 20),
        cost_estimate=pl.CostEstimate(
            flops=2 * 8 * 64 * 1152 * 640, bytes_accessed=12 << 20, transcendentals=8 * 64 * 1152
        ),
    )(ctx, spans, pages, lengths, queries, fresh, *blocks, value_up)


def arrange_kernel(q_ref, dq_ref, new_latents_ref, new_rope_ref, *refs):
    out_ref, decode_out_ref, fresh_out_ref, decode_rows, fresh = refs
    for pair in range(HEADS_TILE // 2):
        at = pair * 2 * KEYW
        for s in range(2):
            tokens = slice(s * SPAN, (s + 1) * SPAN)
            out_ref[s, 2 * pair * SPAN : (2 * pair + 1) * SPAN, :] = q_ref[tokens, at : at + KPAD]
            odd = q_ref[tokens, at + 256 : at + 640].astype(jnp.float32)
            out_ref[s, (2 * pair + 1) * SPAN : (2 * pair + 2) * SPAN, :] = pltpu.roll(
                odd, KPAD - 64, 1
            ).astype(jnp.bfloat16)

    @pl.when(pl.program_id(0) == 0)
    def _():
        rows_local = dq_ref.shape[1]
        fresh[...] = jnp.zeros_like(fresh)
        for s in range(2):
            for h in range(32):
                at = h // 2 * 2 * KEYW + h % 2 * 256
                rows = dq_ref[s, :, at : at + KPAD].astype(jnp.float32)
                if h % 2:
                    rows = pltpu.roll(rows, KPAD - 64, 1)
                for c in range(3):
                    decode_rows[c, pl.ds(s * 32 + h, rows_local, stride=64), :] = rows[
                        :, c * 128 : (c + 1) * 128
                    ]
            mine = pl.ds(s, rows_local, stride=16)
            latent_rows = new_latents_ref[s].astype(jnp.float32)
            fresh[0, mine, :] = latent_rows[:, :128]
            fresh[1, mine, :] = latent_rows[:, 128:]
            rope_rows = new_rope_ref[s].astype(jnp.float32)
            fresh[2, mine, :] = jnp.concatenate([rope_rows, jnp.zeros_like(rope_rows)], axis=1)
        for b in range(rows_local):
            for rows_ref, out, size in ((decode_rows, decode_out_ref, 64), (fresh, fresh_out_ref, 16)):
                rows = slice(b * size, (b + 1) * size)
                parts = [rows_ref[c, rows, :] for c in range(3)]
                out[b] = jnp.concatenate(parts, axis=1).astype(jnp.bfloat16)


def arrange(queries, decode_queries, latents, rope):
    vmem = pl.BlockSpec(memory_space=pltpu.VMEM)
    rows_local = decode_queries.shape[1]
    tiles = queries.shape[1] // (HEADS_TILE * KEYW)
    bf16 = jnp.bfloat16
    whole = [(rows_local, 64, KPAD), (rows_local, 16, KPAD)]
    return pl.pallas_call(
        arrange_kernel,
        grid=(tiles,),
        out_shape=[jax.ShapeDtypeStruct((2 * tiles, ROWS, KPAD), bf16)]
        + [jax.ShapeDtypeStruct(shape, bf16) for shape in whole],
        in_specs=[pl.BlockSpec((2 * SPAN, HEADS_TILE * KEYW), lambda i: (0, i))] + [vmem] * 3,
        out_specs=[pl.BlockSpec((2, ROWS, KPAD), lambda i: (i, 0, 0))]
        + [pl.BlockSpec(shape, lambda i: (0, 0, 0)) for shape in whole],
        scratch_shapes=[
            pltpu.VMEM((3, 64 * rows_local, 128), jnp.float32),
            pltpu.VMEM((3, 16 * rows_local, 128), jnp.float32),
        ],
        compiler_params=pltpu.CompilerParams(vmem_limit_bytes=24 << 20),
        cost_estimate=pl.CostEstimate(flops=0, bytes_accessed=12 << 20, transcendentals=0),
    )(queries, decode_queries, latents, rope)


def clear(top, total, acc, p_b, r_b):
    top[...] = jnp.full(top.shape, FAR_BELOW, jnp.float32)
    total[...] = jnp.zeros_like(total)
    acc[...] = jnp.zeros_like(acc)
    p_b[...] = jnp.zeros_like(p_b)
    r_b[...] = jnp.ones_like(r_b)


def prefill_kernel(ctx_ref, spans_ref, qs_hbm, k_hbm, up_hbm, out_ref, done_ref, *scratch):
    qs, k_ref, up_ref, s_a, s_b, p_a, p_b, top, total, r_a, r_b, acc, sems = scratch
    tiles = acc.shape[0] // 2
    copies = copies_in_parts(qs_hbm, qs, sems.at[0]) + copies_in_parts(k_hbm, k_ref, sems.at[1])
    up_copies = copies_in_parts(up_hbm, up_ref, sems.at[2])
    start(copies + up_copies)
    clear(top, total, acc, p_b, r_b)
    span_of = [spans_ref[2 * ctx_ref[0] + s] for s in range(2)]
    blocks_of = [span // (KEYS // SPAN) for span in span_of]
    offset_of = [(span_of[s] - blocks_of[s] * (KEYS // SPAN)) * SPAN for s in range(2)]
    wait(copies)

    def key_rows(block):
        return pl.ds(pl.multiple_of(block * KEYS, KEYS), KEYS)

    def score_part(unit, block, s_ref, part):
        cols = slice(part * KEYS // 2, (part + 1) * KEYS // 2)
        keys = pl.ds(pl.multiple_of(block * KEYS + part * KEYS // 2, KEYS // 2), KEYS // 2)
        s_ref[:, cols] = lax.dot_general(
            qs[unit], k_ref[keys, :], NT, preferred_element_type=jnp.float32
        )

    lead = lax.broadcasted_iota(jnp.int32, (SPAN, 128), 1)
    lead = lead - lax.broadcasted_iota(jnp.int32, (SPAN, 128), 0)

    def weigh_part(unit, s_ref, p_ref, r_ref, offset, part):
        for h in range(part * HEADS_TILE // 4, (part + 1) * HEADS_TILE // 4):
            rows = slice(h * SPAN, (h + 1) * SPAN)
            parts = [s_ref[rows, c * 128 : (c + 1) * 128] for c in range(KEYS // 128)]
            if offset is not None:
                parts = [
                    jnp.where(lead <= offset - c * 128, part, FAR_BELOW)
                    for c, part in enumerate(parts)
                ]
            highest = functools.reduce(jnp.maximum, parts)
            old = top[unit, rows]
            new = jnp.maximum(old, jnp.max(highest, axis=1, keepdims=True))
            top[unit, rows] = new
            scaled = new * EXP2_SCALE
            rescale = jnp.exp2(old * EXP2_SCALE - scaled)
            r_ref[rows] = rescale
            weights = [jnp.exp2(part * EXP2_SCALE - scaled) for part in parts]
            total[unit, rows] = total[unit, rows] * rescale + sum(weights)
            for c, weight in enumerate(weights):
                p_ref[rows, c * 128 : (c + 1) * 128] = weight.astype(jnp.bfloat16)

    def add_part(unit, block, p_ref, r_ref, part):
        rows = slice(part * ROWS // 2, (part + 1) * ROWS // 2)
        product = jnp.dot(
            p_ref[rows, :], k_ref[key_rows(block), :LATENT], preferred_element_type=jnp.float32
        )
        r = r_ref[rows]
        acc[unit, rows, :128] = acc[unit, rows, :128] * r + product[:, :128]
        acc[unit, rows, 128:] = acc[unit, rows, 128:] * r + product[:, 128:]

    def step(later, here, before, s_later, s_here, p_here, r_here, p_before, r_before, offset=None):
        score_part(*later, s_later, 0)
        weigh_part(here[0], s_here, p_here, r_here, offset, 0)
        score_part(*later, s_later, 1)
        weigh_part(here[0], s_here, p_here, r_here, offset, 1)
        add_part(*before, p_before, r_before, 0)
        weigh_part(here[0], s_here, p_here, r_here, offset, 2)
        add_part(*before, p_before, r_before, 1)
        weigh_part(here[0], s_here, p_here, r_here, offset, 3)

    def last_item(unit):
        return unit, jnp.where(unit % 2 == 0, blocks_of[0], blocks_of[1])

    def following(item):
        unit, block = item
        ends = block + 1 >= jnp.where(unit % 2 == 0, blocks_of[0], blocks_of[1])
        other = 1 - unit % 2
        other_empty = jnp.where(other == 0, blocks_of[0], blocks_of[1]) == 0
        jump = jnp.where(other_empty, 2, 1)
        unit = jnp.where(ends, unit + jump, unit)
        return unit, jnp.where(ends, 0, block + 1)

    def two_items(i, carry):
        before, here = carry[:2], carry[2:]
        after = following(here)
        step(after, here, before, s_b, s_a, p_a, r_a, p_b, r_b)
        later = following(after)
        at_end = later[0] >= 2 * tiles
        later = tuple(jnp.where(at_end, end, value) for end, value in zip(last_item(0), later))
        step(later, after, here, s_a, s_b, p_b, r_b, p_a, r_a)
        return after + later

    all_blocks = blocks_of[0] + blocks_of[1]
    first = (jnp.where(blocks_of[0] == 0, 1, 0), jnp.int32(0))
    first = tuple(
        jnp.where(all_blocks == 0, end, value) for end, value in zip(last_item(0), first)
    )
    for part in range(2):
        score_part(*first, s_a, part)
    carry = lax.fori_loop(
        0, all_blocks * (tiles // 2), two_items, (jnp.int32(0), jnp.int32(0)) + first
    )

    def two_last(i, carry):
        before = carry
        even, odd = last_item(2 * i), last_item(2 * i + 1)
        later = last_item(jnp.minimum(2 * i + 2, 2 * tiles - 1))
        step(odd, even, before, s_b, s_a, p_a, r_a, p_b, r_b, offset_of[0])
        step(later, odd, even, s_a, s_b, p_b, r_b, p_a, r_a, offset_of[1])
        return odd

    before = lax.fori_loop(0, tiles, two_last, carry[:2])
    for part in range(2):
        add_part(*before, p_b, r_b, part)
    wait(up_copies)

    def finish(tile, carry):
        attended = []
        for s in range(2):
            unit = 2 * tile + s
            share = 1.0 / jnp.sum(total[unit], axis=1, keepdims=True)
            attended.append((acc[unit] * share).astype(jnp.bfloat16))
        values = []
        for h in range(HEADS_TILE):
            rows = slice(h * SPAN, (h + 1) * SPAN)
            both = jnp.concatenate([attended[0][rows], attended[1][rows]], axis=0)
            values.append(
                jnp.dot(
                    both, up_ref[tile * HEADS_TILE + h], preferred_element_type=jnp.float32
                ).astype(jnp.bfloat16)
            )
        columns = HEADS_TILE * VDIM
        out_ref[:, pl.ds(pl.multiple_of(tile * columns, columns), columns)] = jnp.concatenate(
            values, axis=1
        )
        return carry

    lax.fori_loop(0, tiles, finish, 0)
    done_ref[...] = jnp.zeros_like(done_ref)


def prefill(ctx, spans, queries, keys, value_up):
    units = queries.shape[0]
    heads = value_up.shape[0]
    f32 = jnp.float32
    smem = pl.BlockSpec(memory_space=pltpu.SMEM)
    vmem = pl.BlockSpec(memory_space=pltpu.VMEM)
    hbm = pl.BlockSpec(memory_space=pltpu.HBM)
    return pl.pallas_call(
        prefill_kernel,
        out_shape=(
            jax.ShapeDtypeStruct((2 * SPAN, heads * VDIM), jnp.bfloat16),
            jax.ShapeDtypeStruct((8, 128), f32),
        ),
        in_specs=[smem] * 2 + [hbm] * 3,
        out_specs=(vmem, vmem),
        scratch_shapes=[
            pltpu.VMEM(queries.shape, jnp.bfloat16),
            pltpu.VMEM(keys.shape, jnp.bfloat16),
            pltpu.VMEM(value_up.shape, jnp.bfloat16),
            pltpu.VMEM((ROWS, KEYS), f32),
            pltpu.VMEM((ROWS, KEYS), f32),
            pltpu.VMEM((ROWS, KEYS), jnp.bfloat16),
            pltpu.VMEM((ROWS, KEYS), jnp.bfloat16),
            pltpu.VMEM((units, ROWS, 128), f32),
            pltpu.VMEM((units, ROWS, 128), f32),
            pltpu.VMEM((ROWS, 128), f32),
            pltpu.VMEM((ROWS, 128), f32),
            pltpu.VMEM((units, ROWS, LATENT), f32),
            pltpu.SemaphoreType.DMA((3, 4)),
        ],
        compiler_params=pltpu.CompilerParams(vmem_limit_bytes=59 << 20),
        cost_estimate=pl.CostEstimate(
            flops=units * ROWS * keys.shape[0] * 640,
            bytes_accessed=8 << 20,
            transcendentals=units * ROWS * keys.shape[0] // 2,
        ),
    )(ctx, spans, queries, keys, value_up)


def project_kernel(ctx_ref, grp_ref, rows_hbm, w_hbm, other_w_hbm, after_ref, *refs):
    out_refs, (rows_ref, w_ref, sums, sems) = refs[:4], refs[4:]
    chunks = sems.shape[1]
    width = rows_ref.shape[1] // chunks
    parts = [(slice(None), slice(c * width, (c + 1) * width)) for c in range(chunks)]
    sides = ((rows_hbm, rows_ref), (w_hbm, w_ref.at[0]), (other_w_hbm, w_ref.at[1]))
    copies = [
        [
            pltpu.make_async_copy(source.at[part], target.at[part], sems.at[i, c])
            for i, (source, target) in enumerate(sides)
        ]
        for c, part in enumerate(parts)
    ]
    for three in copies:
        for copy in three:
            copy.start()
    z, head_z, head_core = ctx_ref[0] // 16, grp_ref[0] // 2, grp_ref[0] % 2
    for c, part in enumerate(parts):
        for copy in copies[c]:
            copy.wait()
        for side in range(2):
            product = lax.dot_general(
                rows_ref[part], w_ref[side, :, part[1]], NT, preferred_element_type=jnp.float32
            )
            sums[side] = product if c == 0 else sums[side] + product
    share = sums.shape[1] // 2
    for k, out_ref in enumerate(out_refs):
        to_z, to_core = (head_z + k // 2) % 2, (head_core + k) % 2
        side = jnp.where(to_z == z, 0, 1)
        rows = pl.ds(pl.multiple_of(to_core * share, share), share)
        out_ref[...] = sums[side, rows, :].astype(jnp.bfloat16)


def project(ctx, grp, rows, weights, other_weights, after):
    smem = pl.BlockSpec(memory_space=pltpu.SMEM)
    vmem = pl.BlockSpec(memory_space=pltpu.VMEM)
    hbm = pl.BlockSpec(memory_space=pltpu.HBM)
    width, depth = weights.shape
    row_count = rows.shape[0]
    return pl.pallas_call(
        project_kernel,
        out_shape=(jax.ShapeDtypeStruct((row_count // 2, width), jnp.bfloat16),) * 4,
        in_specs=[smem, smem, hbm, hbm, hbm, pl.BlockSpec(memory_space=pl.ANY)],
        out_specs=(vmem,) * 4,
        scratch_shapes=[
            pltpu.VMEM(rows.shape, jnp.bfloat16),
            pltpu.VMEM((2, width, depth), jnp.bfloat16),
            pltpu.VMEM((2, row_count, width), jnp.float32),
            pltpu.SemaphoreType.DMA((3, 4)),
        ],
        compiler_params=pltpu.CompilerParams(vmem_limit_bytes=59 << 20),
        cost_estimate=pl.CostEstimate(
            flops=4 * row_count * depth * 256, bytes_accessed=8 << 20, transcendentals=0
        ),
    )(ctx, grp, rows, weights, other_weights, after)


def share_out(k, part):
    pairs = []
    for ctx in range(lax.axis_size("ctx")):
        z, line = divmod(ctx, 16)
        for a in range(2):
            for b in range(2):
                to = ((a ^ k // 2) * 16 + line) * 4 + 2 * z + (b ^ k % 2)
                pairs.append((ctx * 4 + 2 * a + b, to))
    return lax.ppermute(part, ("ctx", "grp"), pairs)


def body(
    prefill_queries,
    latents,
    rope_keys,
    span_slots,
    decode_queries,
    new_latents,
    new_rope,
    context_lengths,
    page_table,
    value_up,
    out_proj,
):
    ctx = lax.axis_index("ctx").astype(jnp.int32).reshape(1)
    grp = lax.axis_index("grp").astype(jnp.int32).reshape(1)
    rows_local = page_table.shape[0]

    own_first, other_first, second = gather_caches(pack(latents, rope_keys))
    queries, row_queries, fresh = arrange(prefill_queries, decode_queries, new_latents, new_rope)
    weights, other_first = lax.optimization_barrier((out_proj.T, other_first))
    other_weights = swap(weights, 16)
    blocks = own_first, other_first, second.reshape(-1, *second.shape[2:])
    keys, decode_values = decode(
        ctx, span_slots, page_table, context_lengths, row_queries, fresh, blocks, value_up
    )
    all_values = exchange(decode_values).reshape(-1, decode_values.shape[1])
    prefill_values, prefill_done = prefill(ctx, span_slots, queries, keys, value_up)
    parts = project(ctx, grp, all_values, weights, other_weights, prefill_done)
    summed = sum(share_out(k, part).astype(jnp.float32) for k, part in enumerate(parts))
    decoded = summed.astype(jnp.bfloat16).reshape(-1, 2, rows_local, summed.shape[1])
    decoded = decoded.transpose(1, 0, 2, 3).reshape(2, -1, summed.shape[1])
    return (prefill_values, decoded)


def solution(mesh):
    placed = (
        P("ctx", "grp"),
        P("ctx", "grp"),
        P("ctx", None),
        P(),
        P(None, "ctx", "grp"),
        P(None, "ctx", "grp"),
        P(None, "ctx", None),
        P("ctx"),
        P("ctx", None),
        P("grp", None, None),
        P("grp", "ctx"),
    )
    return jax.shard_map(
        body,
        mesh=mesh,
        in_specs=placed,
        out_specs=(P("ctx", "grp"), P(None, "grp", "ctx")),
        check_vma=False,
    )
```

```python
import functools
import math

import jax
import jax.numpy as jnp
from jax import lax
from jax.experimental import pallas as pl
from jax.experimental.pallas import tpu as pltpu
from jax.sharding import PartitionSpec as P

SPAN = 64
LATENT = 256
ROPE = 64
KEYW = LATENT + ROPE
KPAD = 384
VDIM = 128

HEADS_TILE = 8
ROWS = HEADS_TILE * SPAN
KEYS = 512

EXP2_SCALE = 192.0 ** -0.5 * math.log2(math.e)
FAR_BELOW = -1e30
NT = (((1,), (1,)), ((), ()))


def swap(value, mask):
    size = lax.axis_size("ctx")
    return lax.ppermute(value, "ctx", [(i, i ^ mask) for i in range(size)])


def exchange(block):
    size = lax.axis_size("ctx")
    groups = [list(range(z * size // 2, (z + 1) * size // 2)) for z in range(2)]
    copies = jnp.broadcast_to(block[None], (size // 2,) + block.shape)
    return lax.all_to_all(
        copies, "ctx", split_axis=0, concat_axis=0, axis_index_groups=groups, tiled=True
    )


def gather_caches(own):
    second = jnp.stack([own[1], swap(own[1], 16)])
    own_first = exchange(own[0])
    return own_first, swap(own_first, 16), exchange(second)


def pack_kernel(latents_ref, rope_ref, out_ref):
    rope = rope_ref[...].astype(jnp.float32).T
    for span in range(2):
        rows = slice(span * SPAN, (span + 1) * SPAN)
        out_ref[span, :SPAN, :] = latents_ref[rows, :]
        parts = [rope[span * SPAN + c * 16 : span * SPAN + (c + 1) * 16] for c in range(4)]
        out_ref[span, SPAN:, :] = jnp.concatenate(parts, axis=1).astype(jnp.bfloat16)


def pack(latents, rope_keys):
    return pl.pallas_call(
        pack_kernel,
        out_shape=jax.ShapeDtypeStruct((2, SPAN + SPAN // 4, LATENT), jnp.bfloat16),
    )(latents, rope_keys.T)


def copies_in_parts(source, target, sems, axis=0):
    parts = sems.shape[0]
    size = source.shape[axis] // parts
    where = [(slice(None),) * axis + (slice(i * size, (i + 1) * size),) for i in range(parts)]
    return [
        pltpu.make_async_copy(source.at[at], target.at[at], sems.at[i])
        for i, at in enumerate(where)
    ]


def start(copies):
    for copy in copies:
        copy.start()


def wait(copies):
    for copy in copies:
        copy.wait()


def unpack(block, keys_ref, place):
    rows = pl.ds(pl.multiple_of(place * SPAN, SPAN), SPAN)
    keys_ref[rows, :LATENT] = block[:SPAN, :]
    packed = block[SPAN:, :].astype(jnp.float32)
    low_lanes = lax.broadcasted_iota(jnp.int32, (16, 128), 1) < ROPE
    parts = []
    for c in range(2):
        two = packed[:, c * 128 : (c + 1) * 128]
        parts.append(jnp.where(low_lanes, two, 0.0))
        parts.append(jnp.where(low_lanes, pltpu.roll(two, 64, 1), 0.0))
    keys_ref[rows, LATENT:] = jnp.concatenate(parts, axis=0).astype(jnp.bfloat16)


def decode_kernel(ctx_ref, spans_ref, pages_ref, lengths_ref, *refs):
    q_ref, fresh_ref, *block_hbms, up_hbm, keys_hbm, values_ref = refs[:8]
    own_ref, other_ref, second_ref, up_ref, keys_ref, cache, att, sems = refs[8:]
    block_refs = own_ref, other_ref, second_ref
    block_copies = [
        copies_in_parts(source, target, sems.at[i])
        for i, (source, target) in enumerate(zip(block_hbms, block_refs))
    ]
    up_copies = copies_in_parts(up_hbm, up_ref, sems.at[3])
    start(sum(block_copies, []) + up_copies)
    rows_local, pages = pages_ref.shape
    slots = pages * SPAN
    width = cache.shape[1]
    for b in range(rows_local):
        cache[b, slots : slots + 16, :] = fresh_ref[b]
        cache[b, slots + 16 :, :] = jnp.zeros((width - slots - 16, KPAD), jnp.bfloat16)
    half = spans_ref.shape[0] // 2
    own_z = ctx_ref[0] // 16
    for i, copies in enumerate(block_copies):
        wait(copies)
        for n in range(block_refs[i].shape[0]):
            line = n % 16 if i < 2 else n // 2
            z = own_z if (i == 0 or (i == 2 and n % 2 == 0)) else 1 - own_z
            unpack(block_refs[i].at[n], keys_ref, spans_ref[2 * (z * 16 + line) + i // 2])
    keys_copies = copies_in_parts(keys_ref, keys_hbm, sems.at[4])
    start(keys_copies)

    cols = lax.broadcasted_iota(jnp.int32, (64, width), 1)
    step = lax.broadcasted_iota(jnp.int32, (64, width), 0) // 32
    fresh_seen = (cols >= slots) & (cols - slots <= step)
    for b in range(rows_local):
        for j in range(pages):
            page = pages_ref[b, j]
            cache[b, j * SPAN : (j + 1) * SPAN, :] = keys_ref[
                pl.ds(pl.multiple_of(page * SPAN, SPAN), SPAN), :
            ]
        scores = lax.dot_general(q_ref[b], cache[b], NT, preferred_element_type=jnp.float32)
        seen = (cols < lengths_ref[b]) | fresh_seen
        scores = jnp.where(seen, scores, FAR_BELOW)
        top = jnp.max(scores, axis=1, keepdims=True)
        weights = jnp.exp2(scores * EXP2_SCALE - top * EXP2_SCALE)
        total = jnp.sum(weights, axis=1, keepdims=True)
        attended = jnp.dot(
            weights.astype(jnp.bfloat16), cache[b, :, :LATENT], preferred_element_type=jnp.float32
        )
        attended = attended / total
        for s in range(2):
            for c in range(2):
                att[c, pl.ds(s * rows_local + b, 32, stride=16), :] = attended[
                    s * 32 : (s + 1) * 32, c * 128 : (c + 1) * 128
                ]
    wait(up_copies)
    for h in range(32):
        mine = slice(h * 16, (h + 1) * 16)
        attended = jnp.concatenate([att[0, mine, :], att[1, mine, :]], axis=1)
        values_ref[:, h * VDIM : (h + 1) * VDIM] = jnp.dot(
            attended.astype(jnp.bfloat16), up_ref[h], preferred_element_type=jnp.float32
        ).astype(jnp.bfloat16)
    wait(keys_copies)


def decode(ctx, spans, pages, lengths, queries, fresh, blocks, value_up):
    smem = pl.BlockSpec(memory_space=pltpu.SMEM)
    vmem = pl.BlockSpec(memory_space=pltpu.VMEM)
    hbm = pl.BlockSpec(memory_space=pltpu.HBM)
    rows_local = pages.shape[0]
    heads = value_up.shape[0]
    key_rows = spans.shape[0] * SPAN
    return pl.pallas_call(
        decode_kernel,
        out_shape=(
            jax.ShapeDtypeStruct((key_rows, KPAD), jnp.bfloat16),
            jax.ShapeDtypeStruct((2 * rows_local, heads * VDIM), jnp.bfloat16),
        ),
        in_specs=[smem] * 4 + [vmem] * 2 + [hbm] * 4,
        out_specs=(hbm, vmem),
        scratch_shapes=[pltpu.VMEM(block.shape, jnp.bfloat16) for block in blocks]
        + [
            pltpu.VMEM(value_up.shape, jnp.bfloat16),
            pltpu.VMEM((key_rows, KPAD), jnp.bfloat16),
            pltpu.VMEM((rows_local, pages.shape[1] * SPAN + 128, KPAD), jnp.bfloat16),
            pltpu.VMEM((2, 16 * heads, 128), jnp.float32),
            pltpu.SemaphoreType.DMA((5, 4)),
        ],
        compiler_params=pltpu.CompilerParams(vmem_limit_bytes=59 << 20),
        cost_estimate=pl.CostEstimate(
            flops=2 * 8 * 64 * 1152 * 640, bytes_accessed=12 << 20, transcendentals=8 * 64 * 1152
        ),
    )(ctx, spans, pages, lengths, queries, fresh, *blocks, value_up)


def arrange_kernel(q_ref, dq_ref, new_latents_ref, new_rope_ref, *refs):
    out_ref, decode_out_ref, fresh_out_ref, decode_rows, fresh = refs
    for pair in range(HEADS_TILE // 2):
        at = pair * 2 * KEYW
        for s in range(2):
            tokens = slice(s * SPAN, (s + 1) * SPAN)
            out_ref[s, 2 * pair * SPAN : (2 * pair + 1) * SPAN, :] = q_ref[tokens, at : at + KPAD]
            odd = q_ref[tokens, at + 256 : at + 640].astype(jnp.float32)
            out_ref[s, (2 * pair + 1) * SPAN : (2 * pair + 2) * SPAN, :] = pltpu.roll(
                odd, KPAD - 64, 1
            ).astype(jnp.bfloat16)

    @pl.when(pl.program_id(0) == 0)
    def _():
        rows_local = dq_ref.shape[1]
        fresh[...] = jnp.zeros_like(fresh)
        for s in range(2):
            for h in range(32):
                at = h // 2 * 2 * KEYW + h % 2 * 256
                rows = dq_ref[s, :, at : at + KPAD].astype(jnp.float32)
                if h % 2:
                    rows = pltpu.roll(rows, KPAD - 64, 1)
                for c in range(3):
                    decode_rows[c, pl.ds(s * 32 + h, rows_local, stride=64), :] = rows[
                        :, c * 128 : (c + 1) * 128
                    ]
            mine = pl.ds(s, rows_local, stride=16)
            latent_rows = new_latents_ref[s].astype(jnp.float32)
            fresh[0, mine, :] = latent_rows[:, :128]
            fresh[1, mine, :] = latent_rows[:, 128:]
            rope_rows = new_rope_ref[s].astype(jnp.float32)
            fresh[2, mine, :] = jnp.concatenate([rope_rows, jnp.zeros_like(rope_rows)], axis=1)
        for b in range(rows_local):
            for rows_ref, out, size in ((decode_rows, decode_out_ref, 64), (fresh, fresh_out_ref, 16)):
                rows = slice(b * size, (b + 1) * size)
                parts = [rows_ref[c, rows, :] for c in range(3)]
                out[b] = jnp.concatenate(parts, axis=1).astype(jnp.bfloat16)


def arrange(queries, decode_queries, latents, rope):
    vmem = pl.BlockSpec(memory_space=pltpu.VMEM)
    rows_local = decode_queries.shape[1]
    tiles = queries.shape[1] // (HEADS_TILE * KEYW)
    bf16 = jnp.bfloat16
    whole = [(rows_local, 64, KPAD), (rows_local, 16, KPAD)]
    return pl.pallas_call(
        arrange_kernel,
        grid=(tiles,),
        out_shape=[jax.ShapeDtypeStruct((2 * tiles, ROWS, KPAD), bf16)]
        + [jax.ShapeDtypeStruct(shape, bf16) for shape in whole],
        in_specs=[pl.BlockSpec((2 * SPAN, HEADS_TILE * KEYW), lambda i: (0, i))] + [vmem] * 3,
        out_specs=[pl.BlockSpec((2, ROWS, KPAD), lambda i: (i, 0, 0))]
        + [pl.BlockSpec(shape, lambda i: (0, 0, 0)) for shape in whole],
        scratch_shapes=[
            pltpu.VMEM((3, 64 * rows_local, 128), jnp.float32),
            pltpu.VMEM((3, 16 * rows_local, 128), jnp.float32),
        ],
        compiler_params=pltpu.CompilerParams(vmem_limit_bytes=24 << 20),
        cost_estimate=pl.CostEstimate(flops=0, bytes_accessed=12 << 20, transcendentals=0),
    )(queries, decode_queries, latents, rope)


def clear(top, total, acc, p_b, r_b):
    top[...] = jnp.full(top.shape, FAR_BELOW, jnp.float32)
    total[...] = jnp.zeros_like(total)
    acc[...] = jnp.zeros_like(acc)
    p_b[...] = jnp.zeros_like(p_b)
    r_b[...] = jnp.ones_like(r_b)


def prefill_kernel(ctx_ref, spans_ref, qs_hbm, k_hbm, up_hbm, out_ref, done_ref, *scratch):
    qs, k_ref, kt_ref, up_ref, s_a, s_b, p_a, p_b, top, total, r_a, r_b, acc, sems = scratch
    tiles = acc.shape[0] // 2
    k_copies = copies_in_parts(k_hbm, k_ref, sems.at[0])
    q_copies = copies_in_parts(qs_hbm, qs, sems.at[1])
    up_copies = copies_in_parts(up_hbm, up_ref, sems.at[2])
    start(k_copies + q_copies + up_copies)
    clear(top, total, acc, p_b, r_b)
    pieces = kt_ref.shape[0]
    for n in range(pieces):
        if n % (pieces // len(k_copies)) == 0:
            k_copies[n // (pieces // len(k_copies))].wait()
        kt_ref[n] = k_ref[n * KEYS // 2 : (n + 1) * KEYS // 2, :].T
    span_of = [spans_ref[2 * ctx_ref[0] + s] for s in range(2)]
    blocks_of = [span // (KEYS // SPAN) for span in span_of]
    offset_of = [(span_of[s] - blocks_of[s] * (KEYS // SPAN)) * SPAN for s in range(2)]
    wait(q_copies)

    def key_rows(block):
        return pl.ds(pl.multiple_of(block * KEYS, KEYS), KEYS)

    def score_part(unit, block, s_ref, part):
        cols = slice(part * KEYS // 2, (part + 1) * KEYS // 2)
        s_ref[:, cols] = jnp.dot(
            qs[unit], kt_ref[2 * block + part], preferred_element_type=jnp.float32
        )

    lead = lax.broadcasted_iota(jnp.int32, (SPAN, 128), 1)
    lead = lead - lax.broadcasted_iota(jnp.int32, (SPAN, 128), 0)

    def weigh_part(unit, s_ref, p_ref, r_ref, offset, part):
        for h in range(part * HEADS_TILE // 4, (part + 1) * HEADS_TILE // 4):
            rows = slice(h * SPAN, (h + 1) * SPAN)
            parts = [s_ref[rows, c * 128 : (c + 1) * 128] for c in range(KEYS // 128)]
            if offset is not None:
                parts = [
                    jnp.where(lead <= offset - c * 128, part, FAR_BELOW)
                    for c, part in enumerate(parts)
                ]
            highest = functools.reduce(jnp.maximum, parts)
            old = top[unit, rows]
            new = jnp.maximum(old, jnp.max(highest, axis=1, keepdims=True))
            top[unit, rows] = new
            scaled = new * EXP2_SCALE
            rescale = jnp.exp2(old * EXP2_SCALE - scaled)
            r_ref[rows] = rescale
            weights = [jnp.exp2(part * EXP2_SCALE - scaled) for part in parts]
            total[unit, rows] = total[unit, rows] * rescale + sum(weights)
            for c, weight in enumerate(weights):
                p_ref[rows, c * 128 : (c + 1) * 128] = weight.astype(jnp.bfloat16)

    def add_part(unit, block, p_ref, r_ref, part):
        rows = slice(part * ROWS // 2, (part + 1) * ROWS // 2)
        product = jnp.dot(
            p_ref[rows, :], k_ref[key_rows(block), :LATENT], preferred_element_type=jnp.float32
        )
        r = r_ref[rows]
        acc[unit, rows, :128] = acc[unit, rows, :128] * r + product[:, :128]
        acc[unit, rows, 128:] = acc[unit, rows, 128:] * r + product[:, 128:]

    def step(later, here, before, s_later, s_here, p_here, r_here, p_before, r_before, offset=None):
        score_part(*later, s_later, 0)
        weigh_part(here[0], s_here, p_here, r_here, offset, 0)
        score_part(*later, s_later, 1)
        weigh_part(here[0], s_here, p_here, r_here, offset, 1)
        add_part(*before, p_before, r_before, 0)
        weigh_part(here[0], s_here, p_here, r_here, offset, 2)
        add_part(*before, p_before, r_before, 1)
        weigh_part(here[0], s_here, p_here, r_here, offset, 3)

    def last_item(unit):
        return unit, jnp.where(unit % 2 == 0, blocks_of[0], blocks_of[1])

    def following(item):
        unit, block = item
        ends = block + 1 >= jnp.where(unit % 2 == 0, blocks_of[0], blocks_of[1])
        other = 1 - unit % 2
        other_empty = jnp.where(other == 0, blocks_of[0], blocks_of[1]) == 0
        jump = jnp.where(other_empty, 2, 1)
        unit = jnp.where(ends, unit + jump, unit)
        return unit, jnp.where(ends, 0, block + 1)

    def two_items(i, carry):
        before, here = carry[:2], carry[2:]
        after = following(here)
        step(after, here, before, s_b, s_a, p_a, r_a, p_b, r_b)
        later = following(after)
        at_end = later[0] >= 2 * tiles
        later = tuple(jnp.where(at_end, end, value) for end, value in zip(last_item(0), later))
        step(later, after, here, s_a, s_b, p_b, r_b, p_a, r_a)
        return after + later

    all_blocks = blocks_of[0] + blocks_of[1]
    first = (jnp.where(blocks_of[0] == 0, 1, 0), jnp.int32(0))
    first = tuple(
        jnp.where(all_blocks == 0, end, value) for end, value in zip(last_item(0), first)
    )
    for part in range(2):
        score_part(*first, s_a, part)
    carry = lax.fori_loop(
        0, all_blocks * (tiles // 2), two_items, (jnp.int32(0), jnp.int32(0)) + first
    )

    def two_last(i, carry):
        before = carry
        even, odd = last_item(2 * i), last_item(2 * i + 1)
        later = last_item(jnp.minimum(2 * i + 2, 2 * tiles - 1))
        step(odd, even, before, s_b, s_a, p_a, r_a, p_b, r_b, offset_of[0])
        step(later, odd, even, s_a, s_b, p_b, r_b, p_a, r_a, offset_of[1])
        return odd

    before = lax.fori_loop(0, tiles, two_last, carry[:2])
    for part in range(2):
        add_part(*before, p_b, r_b, part)
    wait(up_copies)

    def finish(tile, carry):
        attended = []
        for s in range(2):
            unit = 2 * tile + s
            share = 1.0 / jnp.sum(total[unit], axis=1, keepdims=True)
            attended.append((acc[unit] * share).astype(jnp.bfloat16))
        values = []
        for h in range(HEADS_TILE):
            rows = slice(h * SPAN, (h + 1) * SPAN)
            both = jnp.concatenate([attended[0][rows], attended[1][rows]], axis=0)
            values.append(
                jnp.dot(
                    both, up_ref[tile * HEADS_TILE + h], preferred_element_type=jnp.float32
                ).astype(jnp.bfloat16)
            )
        columns = HEADS_TILE * VDIM
        out_ref[:, pl.ds(pl.multiple_of(tile * columns, columns), columns)] = jnp.concatenate(
            values, axis=1
        )
        return carry

    lax.fori_loop(0, tiles, finish, 0)
    done_ref[...] = jnp.zeros_like(done_ref)


def prefill(ctx, spans, queries, keys, value_up):
    units = queries.shape[0]
    heads = value_up.shape[0]
    f32 = jnp.float32
    smem = pl.BlockSpec(memory_space=pltpu.SMEM)
    vmem = pl.BlockSpec(memory_space=pltpu.VMEM)
    hbm = pl.BlockSpec(memory_space=pltpu.HBM)
    return pl.pallas_call(
        prefill_kernel,
        out_shape=(
            jax.ShapeDtypeStruct((2 * SPAN, heads * VDIM), jnp.bfloat16),
            jax.ShapeDtypeStruct((8, 128), f32),
        ),
        in_specs=[smem] * 2 + [hbm] * 3,
        out_specs=(vmem, vmem),
        scratch_shapes=[
            pltpu.VMEM(queries.shape, jnp.bfloat16),
            pltpu.VMEM(keys.shape, jnp.bfloat16),
            pltpu.VMEM((2 * keys.shape[0] // KEYS, KPAD, KEYS // 2), jnp.bfloat16),
            pltpu.VMEM(value_up.shape, jnp.bfloat16),
            pltpu.VMEM((ROWS, KEYS), f32),
            pltpu.VMEM((ROWS, KEYS), f32),
            pltpu.VMEM((ROWS, KEYS), jnp.bfloat16),
            pltpu.VMEM((ROWS, KEYS), jnp.bfloat16),
            pltpu.VMEM((units, ROWS, 128), f32),
            pltpu.VMEM((units, ROWS, 128), f32),
            pltpu.VMEM((ROWS, 128), f32),
            pltpu.VMEM((ROWS, 128), f32),
            pltpu.VMEM((units, ROWS, LATENT), f32),
            pltpu.SemaphoreType.DMA((3, 4)),
        ],
        compiler_params=pltpu.CompilerParams(vmem_limit_bytes=59 << 20),
        cost_estimate=pl.CostEstimate(
            flops=units * ROWS * keys.shape[0] * 640,
            bytes_accessed=8 << 20,
            transcendentals=units * ROWS * keys.shape[0] // 2,
        ),
    )(ctx, spans, queries, keys, value_up)


def project_kernel(ctx_ref, grp_ref, rows_hbm, w_hbm, other_w_hbm, after_ref, *refs):
    out_refs, (rows_ref, w_ref, sums, sems) = refs[:4], refs[4:]
    chunks = sems.shape[1]
    width = rows_ref.shape[1] // chunks
    parts = [(slice(None), slice(c * width, (c + 1) * width)) for c in range(chunks)]
    sides = ((rows_hbm, rows_ref), (w_hbm, w_ref.at[0]), (other_w_hbm, w_ref.at[1]))
    copies = [
        [
            pltpu.make_async_copy(source.at[part], target.at[part], sems.at[i, c])
            for i, (source, target) in enumerate(sides)
        ]
        for c, part in enumerate(parts)
    ]
    for three in copies:
        for copy in three:
            copy.start()
    z, head_z, head_core = ctx_ref[0] // 16, grp_ref[0] // 2, grp_ref[0] % 2
    for c, part in enumerate(parts):
        for copy in copies[c]:
            copy.wait()
        for side in range(2):
            product = lax.dot_general(
                rows_ref[part], w_ref[side, :, part[1]], NT, preferred_element_type=jnp.float32
            )
            sums[side] = product if c == 0 else sums[side] + product
    share = sums.shape[1] // 2
    for k, out_ref in enumerate(out_refs):
        to_z, to_core = (head_z + k // 2) % 2, (head_core + k) % 2
        side = jnp.where(to_z == z, 0, 1)
        rows = pl.ds(pl.multiple_of(to_core * share, share), share)
        out_ref[...] = sums[side, rows, :].astype(jnp.bfloat16)


def project(ctx, grp, rows, weights, other_weights, after):
    smem = pl.BlockSpec(memory_space=pltpu.SMEM)
    vmem = pl.BlockSpec(memory_space=pltpu.VMEM)
    hbm = pl.BlockSpec(memory_space=pltpu.HBM)
    width, depth = weights.shape
    row_count = rows.shape[0]
    return pl.pallas_call(
        project_kernel,
        out_shape=(jax.ShapeDtypeStruct((row_count // 2, width), jnp.bfloat16),) * 4,
        in_specs=[smem, smem, hbm, hbm, hbm, pl.BlockSpec(memory_space=pl.ANY)],
        out_specs=(vmem,) * 4,
        scratch_shapes=[
            pltpu.VMEM(rows.shape, jnp.bfloat16),
            pltpu.VMEM((2, width, depth), jnp.bfloat16),
            pltpu.VMEM((2, row_count, width), jnp.float32),
            pltpu.SemaphoreType.DMA((3, 4)),
        ],
        compiler_params=pltpu.CompilerParams(vmem_limit_bytes=59 << 20),
        cost_estimate=pl.CostEstimate(
            flops=4 * row_count * depth * 256, bytes_accessed=8 << 20, transcendentals=0
        ),
    )(ctx, grp, rows, weights, other_weights, after)


def share_out(k, part):
    pairs = []
    for ctx in range(lax.axis_size("ctx")):
        z, line = divmod(ctx, 16)
        for a in range(2):
            for b in range(2):
                to = ((a ^ k // 2) * 16 + line) * 4 + 2 * z + (b ^ k % 2)
                pairs.append((ctx * 4 + 2 * a + b, to))
    return lax.ppermute(part, ("ctx", "grp"), pairs)


def body(
    prefill_queries,
    latents,
    rope_keys,
    span_slots,
    decode_queries,
    new_latents,
    new_rope,
    context_lengths,
    page_table,
    value_up,
    out_proj,
):
    ctx = lax.axis_index("ctx").astype(jnp.int32).reshape(1)
    grp = lax.axis_index("grp").astype(jnp.int32).reshape(1)
    rows_local = page_table.shape[0]

    own_first, other_first, second = gather_caches(pack(latents, rope_keys))
    queries, row_queries, fresh = arrange(prefill_queries, decode_queries, new_latents, new_rope)
    weights, other_first = lax.optimization_barrier((out_proj.T, other_first))
    other_weights = swap(weights, 16)
    blocks = own_first, other_first, second.reshape(-1, *second.shape[2:])
    keys, decode_values = decode(
        ctx, span_slots, page_table, context_lengths, row_queries, fresh, blocks, value_up
    )
    all_values = exchange(decode_values).reshape(-1, decode_values.shape[1])
    prefill_values, prefill_done = prefill(ctx, span_slots, queries, keys, value_up)
    parts = project(ctx, grp, all_values, weights, other_weights, prefill_done)
    summed = sum(share_out(k, part).astype(jnp.float32) for k, part in enumerate(parts))
    decoded = summed.astype(jnp.bfloat16).reshape(-1, 2, rows_local, summed.shape[1])
    decoded = decoded.transpose(1, 0, 2, 3).reshape(2, -1, summed.shape[1])
    return (prefill_values, decoded)


def solution(mesh):
    placed = (
        P("ctx", "grp"),
        P("ctx", "grp"),
        P("ctx", None),
        P(),
        P(None, "ctx", "grp"),
        P(None, "ctx", "grp"),
        P(None, "ctx", None),
        P("ctx"),
        P("ctx", None),
        P("grp", None, None),
        P("grp", "ctx"),
    )
    return jax.shard_map(
        body,
        mesh=mesh,
        in_specs=placed,
        out_specs=(P("ctx", "grp"), P(None, "grp", "ctx")),
        check_vma=False,
    )
```

```python
import functools
import math

import jax
import jax.numpy as jnp
from jax import lax
from jax.experimental import pallas as pl
from jax.experimental.pallas import tpu as pltpu
from jax.sharding import PartitionSpec as P

SPAN = 64
LATENT = 256
ROPE = 64
KEYW = LATENT + ROPE
KPAD = 384
VDIM = 128

HEADS_TILE = 8
ROWS = HEADS_TILE * SPAN
KEYS = 512

EXP2_SCALE = 192.0 ** -0.5 * math.log2(math.e)
FAR_BELOW = -1e30
NT = (((1,), (1,)), ((), ()))


def swap(value, mask):
    size = lax.axis_size("ctx")
    return lax.ppermute(value, "ctx", [(i, i ^ mask) for i in range(size)])


def exchange(copies):
    size = lax.axis_size("ctx")
    groups = [list(range(z * size // 2, (z + 1) * size // 2)) for z in range(2)]
    return lax.all_to_all(
        copies, "ctx", split_axis=0, concat_axis=0, axis_index_groups=groups, tiled=True
    )


def gather_caches(first, second):
    first_copies, second_copies = spread(first, second, swap(second, 16))
    return exchange(first_copies), exchange(second_copies)


def copies_in_parts(source, target, sems, axis=0):
    parts = sems.shape[0]
    size = source.shape[axis] // parts
    where = [(slice(None),) * axis + (slice(i * size, (i + 1) * size),) for i in range(parts)]
    return [
        pltpu.make_async_copy(source.at[at], target.at[at], sems.at[i])
        for i, at in enumerate(where)
    ]


def start(copies):
    for copy in copies:
        copy.start()


def wait(copies):
    for copy in copies:
        copy.wait()


def pack_kernel(latents_ref, rope_ref, *out_refs):
    rope = rope_ref[...].astype(jnp.float32).T
    for span, out_ref in enumerate(out_refs):
        rows = slice(span * SPAN, (span + 1) * SPAN)
        out_ref[:SPAN, :] = latents_ref[rows, :]
        parts = [rope[span * SPAN + c * 16 : span * SPAN + (c + 1) * 16] for c in range(4)]
        out_ref[SPAN:, :] = jnp.concatenate(parts, axis=1).astype(jnp.bfloat16)


def pack(latents, rope_keys):
    block = jax.ShapeDtypeStruct((SPAN + SPAN // 4, LATENT), jnp.bfloat16)
    return pl.pallas_call(pack_kernel, out_shape=(block, block))(latents, rope_keys.T)


def repeat_to(source, target, sems):
    size = source.shape[0]
    return [
        pltpu.make_async_copy(source, target.at[i * size : (i + 1) * size], sems.at[i])
        for i in range(target.shape[0] // size)
    ]


def spread_kernel(first_ref, second_ref, other_ref, first_hbm, second_hbm, firsts, seconds, sems):
    for i in range(firsts.shape[0]):
        firsts[i] = first_ref[...]
    first_copies = repeat_to(firsts, first_hbm, sems.at[0])
    start(first_copies)
    for i in range(seconds.shape[0]):
        seconds[i, 0] = second_ref[...]
        seconds[i, 1] = other_ref[...]
    second_copies = repeat_to(seconds, second_hbm, sems.at[1])
    start(second_copies)
    wait(first_copies + second_copies)


def spread(first, second, other):
    shape = first.shape
    hbm = pl.BlockSpec(memory_space=pltpu.HBM)
    return pl.pallas_call(
        spread_kernel,
        out_shape=(
            jax.ShapeDtypeStruct((16, *shape), jnp.bfloat16),
            jax.ShapeDtypeStruct((16, 2, *shape), jnp.bfloat16),
        ),
        out_specs=(hbm, hbm),
        scratch_shapes=[
            pltpu.VMEM((4, *shape), jnp.bfloat16),
            pltpu.VMEM((4, 2, *shape), jnp.bfloat16),
            pltpu.SemaphoreType.DMA((2, 4)),
        ],
    )(first, second, other)


def unpack(block, keys_ref, place):
    rows = pl.ds(pl.multiple_of(place * SPAN, SPAN), SPAN)
    keys_ref[rows, :LATENT] = block[:SPAN, :]
    packed = block[SPAN:, :].astype(jnp.float32)
    low_lanes = lax.broadcasted_iota(jnp.int32, (16, 128), 1) < ROPE
    parts = []
    for c in range(2):
        two = packed[:, c * 128 : (c + 1) * 128]
        parts.append(jnp.where(low_lanes, two, 0.0))
        parts.append(jnp.where(low_lanes, pltpu.roll(two, 64, 1), 0.0))
    keys_ref[rows, LATENT:] = jnp.concatenate(parts, axis=0).astype(jnp.bfloat16)


def decode_kernel(ctx_ref, spans_ref, pages_ref, lengths_ref, *refs):
    q_ref, fresh_ref, *block_hbms, up_hbm, keys_hbm, values_hbm = refs[:8]
    own_ref, other_ref, second_ref, up_ref, keys_ref, cache, att, values, sems = refs[8:]
    block_refs = own_ref, other_ref, second_ref
    block_copies = [
        copies_in_parts(source, target, sems.at[i])
        for i, (source, target) in enumerate(zip(block_hbms, block_refs))
    ]
    up_copies = copies_in_parts(up_hbm, up_ref, sems.at[3])
    start(sum(block_copies, []) + up_copies)
    rows_local, pages = pages_ref.shape
    slots = pages * SPAN
    width = cache.shape[1]
    for b in range(rows_local):
        cache[b, slots : slots + 16, :] = fresh_ref[b]
        cache[b, slots + 16 :, :] = jnp.zeros((width - slots - 16, KPAD), jnp.bfloat16)
    half = spans_ref.shape[0] // 2
    own_z = ctx_ref[0] // 16
    for i, copies in enumerate(block_copies):
        wait(copies)
        for n in range(block_refs[i].shape[0]):
            line = n % 16 if i < 2 else n // 2
            z = own_z if (i == 0 or (i == 2 and n % 2 == 0)) else 1 - own_z
            unpack(block_refs[i].at[n], keys_ref, spans_ref[2 * (z * 16 + line) + i // 2])
    keys_copies = copies_in_parts(keys_ref, keys_hbm, sems.at[4])
    start(keys_copies)

    cols = lax.broadcasted_iota(jnp.int32, (64, width), 1)
    step = lax.broadcasted_iota(jnp.int32, (64, width), 0) // 32
    fresh_seen = (cols >= slots) & (cols - slots <= step)
    for b in range(rows_local):
        for j in range(pages):
            page = pages_ref[b, j]
            cache[b, j * SPAN : (j + 1) * SPAN, :] = keys_ref[
                pl.ds(pl.multiple_of(page * SPAN, SPAN), SPAN), :
            ]
        scores = lax.dot_general(q_ref[b], cache[b], NT, preferred_element_type=jnp.float32)
        seen = (cols < lengths_ref[b]) | fresh_seen
        scores = jnp.where(seen, scores, FAR_BELOW)
        top = jnp.max(scores, axis=1, keepdims=True)
        weights = jnp.exp2(scores * EXP2_SCALE - top * EXP2_SCALE)
        total = jnp.sum(weights, axis=1, keepdims=True)
        attended = jnp.dot(
            weights.astype(jnp.bfloat16), cache[b, :, :LATENT], preferred_element_type=jnp.float32
        )
        attended = attended / total
        for s in range(2):
            for c in range(2):
                att[c, pl.ds(s * rows_local + b, 32, stride=16), :] = attended[
                    s * 32 : (s + 1) * 32, c * 128 : (c + 1) * 128
                ]
    wait(up_copies)
    for h in range(32):
        mine = slice(h * 16, (h + 1) * 16)
        attended = jnp.concatenate([att[0, mine, :], att[1, mine, :]], axis=1)
        head_values = jnp.dot(
            attended.astype(jnp.bfloat16), up_ref[h], preferred_element_type=jnp.float32
        ).astype(jnp.bfloat16)
        for i in range(values.shape[0]):
            values[i, :, h * VDIM : (h + 1) * VDIM] = head_values
    values_copies = repeat_to(values, values_hbm, sems.at[5])
    start(values_copies)
    wait(values_copies)
    wait(keys_copies)


def decode(ctx, spans, pages, lengths, queries, fresh, blocks, value_up):
    smem = pl.BlockSpec(memory_space=pltpu.SMEM)
    vmem = pl.BlockSpec(memory_space=pltpu.VMEM)
    hbm = pl.BlockSpec(memory_space=pltpu.HBM)
    rows_local = pages.shape[0]
    heads = value_up.shape[0]
    key_rows = spans.shape[0] * SPAN
    return pl.pallas_call(
        decode_kernel,
        out_shape=(
            jax.ShapeDtypeStruct((key_rows, KPAD), jnp.bfloat16),
            jax.ShapeDtypeStruct((16, 2 * rows_local, heads * VDIM), jnp.bfloat16),
        ),
        in_specs=[smem] * 4 + [vmem] * 2 + [hbm] * 4,
        out_specs=(hbm, hbm),
        scratch_shapes=[pltpu.VMEM(block.shape, jnp.bfloat16) for block in blocks]
        + [
            pltpu.VMEM(value_up.shape, jnp.bfloat16),
            pltpu.VMEM((key_rows, KPAD), jnp.bfloat16),
            pltpu.VMEM((rows_local, pages.shape[1] * SPAN + 128, KPAD), jnp.bfloat16),
            pltpu.VMEM((2, 16 * heads, 128), jnp.float32),
            pltpu.VMEM((4, 2 * rows_local, heads * VDIM), jnp.bfloat16),
            pltpu.SemaphoreType.DMA((6, 4)),
        ],
        compiler_params=pltpu.CompilerParams(vmem_limit_bytes=59 << 20),
        cost_estimate=pl.CostEstimate(
            flops=2 * 8 * 64 * 1152 * 640, bytes_accessed=12 << 20, transcendentals=8 * 64 * 1152
        ),
    )(ctx, spans, pages, lengths, queries, fresh, *blocks, value_up)


def arrange_kernel(q_ref, dq_ref, new_latents_ref, new_rope_ref, *refs):
    out_ref, decode_out_ref, fresh_out_ref, decode_rows, fresh = refs
    for pair in range(HEADS_TILE // 2):
        at = pair * 2 * KEYW
        for s in range(2):
            tokens = slice(s * SPAN, (s + 1) * SPAN)
            out_ref[s, 2 * pair * SPAN : (2 * pair + 1) * SPAN, :] = q_ref[tokens, at : at + KPAD]
            odd = q_ref[tokens, at + 256 : at + 640].astype(jnp.float32)
            out_ref[s, (2 * pair + 1) * SPAN : (2 * pair + 2) * SPAN, :] = pltpu.roll(
                odd, KPAD - 64, 1
            ).astype(jnp.bfloat16)

    @pl.when(pl.program_id(0) == 0)
    def _():
        rows_local = dq_ref.shape[1]
        fresh[...] = jnp.zeros_like(fresh)
        for s in range(2):
            for h in range(32):
                at = h // 2 * 2 * KEYW + h % 2 * 256
                rows = dq_ref[s, :, at : at + KPAD].astype(jnp.float32)
                if h % 2:
                    rows = pltpu.roll(rows, KPAD - 64, 1)
                for c in range(3):
                    decode_rows[c, pl.ds(s * 32 + h, rows_local, stride=64), :] = rows[
                        :, c * 128 : (c + 1) * 128
                    ]
            mine = pl.ds(s, rows_local, stride=16)
            latent_rows = new_latents_ref[s].astype(jnp.float32)
            fresh[0, mine, :] = latent_rows[:, :128]
            fresh[1, mine, :] = latent_rows[:, 128:]
            rope_rows = new_rope_ref[s].astype(jnp.float32)
            fresh[2, mine, :] = jnp.concatenate([rope_rows, jnp.zeros_like(rope_rows)], axis=1)
        for b in range(rows_local):
            for rows_ref, out, size in ((decode_rows, decode_out_ref, 64), (fresh, fresh_out_ref, 16)):
                rows = slice(b * size, (b + 1) * size)
                parts = [rows_ref[c, rows, :] for c in range(3)]
                out[b] = jnp.concatenate(parts, axis=1).astype(jnp.bfloat16)


def arrange(queries, decode_queries, latents, rope):
    vmem = pl.BlockSpec(memory_space=pltpu.VMEM)
    rows_local = decode_queries.shape[1]
    tiles = queries.shape[1] // (HEADS_TILE * KEYW)
    bf16 = jnp.bfloat16
    whole = [(rows_local, 64, KPAD), (rows_local, 16, KPAD)]
    return pl.pallas_call(
        arrange_kernel,
        grid=(tiles,),
        out_shape=[jax.ShapeDtypeStruct((2 * tiles, ROWS, KPAD), bf16)]
        + [jax.ShapeDtypeStruct(shape, bf16) for shape in whole],
        in_specs=[pl.BlockSpec((2 * SPAN, HEADS_TILE * KEYW), lambda i: (0, i))] + [vmem] * 3,
        out_specs=[pl.BlockSpec((2, ROWS, KPAD), lambda i: (i, 0, 0))]
        + [pl.BlockSpec(shape, lambda i: (0, 0, 0)) for shape in whole],
        scratch_shapes=[
            pltpu.VMEM((3, 64 * rows_local, 128), jnp.float32),
            pltpu.VMEM((3, 16 * rows_local, 128), jnp.float32),
        ],
        compiler_params=pltpu.CompilerParams(vmem_limit_bytes=59 << 20),
        cost_estimate=pl.CostEstimate(flops=0, bytes_accessed=12 << 20, transcendentals=0),
    )(queries, decode_queries, latents, rope)


def clear(top, total, acc, p_b, r_b):
    top[...] = jnp.full(top.shape, FAR_BELOW, jnp.float32)
    total[...] = jnp.zeros_like(total)
    acc[...] = jnp.zeros_like(acc)
    p_b[...] = jnp.zeros_like(p_b)
    r_b[...] = jnp.ones_like(r_b)


def prefill_kernel(ctx_ref, spans_ref, qs_hbm, k_hbm, up_hbm, out_ref, done_ref, *scratch):
    qs, k_ref, kt_ref, up_ref, s_a, s_b, p_a, p_b, top, total, r_a, r_b, acc, sems = scratch
    tiles = acc.shape[0] // 2
    k_copies = copies_in_parts(k_hbm, k_ref, sems.at[0])
    q_copies = copies_in_parts(qs_hbm, qs, sems.at[1])
    up_copies = copies_in_parts(up_hbm, up_ref, sems.at[2])
    start(k_copies + q_copies)
    clear(top, total, acc, p_b, r_b)
    pieces = kt_ref.shape[0]
    for n in range(pieces):
        if n % (pieces // len(k_copies)) == 0:
            k_copies[n // (pieces // len(k_copies))].wait()
        kt_ref[n] = k_ref[n * KEYS // 2 : (n + 1) * KEYS // 2, :].T
    span_of = [spans_ref[2 * ctx_ref[0] + s] for s in range(2)]
    blocks_of = [span // (KEYS // SPAN) for span in span_of]
    offset_of = [(span_of[s] - blocks_of[s] * (KEYS // SPAN)) * SPAN for s in range(2)]
    wait(q_copies)
    start(up_copies)

    def key_rows(block):
        return pl.ds(pl.multiple_of(block * KEYS, KEYS), KEYS)

    def score_part(unit, block, s_ref, part):
        cols = slice(part * KEYS // 2, (part + 1) * KEYS // 2)
        s_ref[:, cols] = jnp.dot(
            qs[unit], kt_ref[2 * block + part], preferred_element_type=jnp.float32
        )

    lead = lax.broadcasted_iota(jnp.int32, (SPAN, 128), 1)
    lead = lead - lax.broadcasted_iota(jnp.int32, (SPAN, 128), 0)

    def weigh_part(unit, s_ref, p_ref, r_ref, offset, part):
        for h in range(part * HEADS_TILE // 4, (part + 1) * HEADS_TILE // 4):
            rows = slice(h * SPAN, (h + 1) * SPAN)
            parts = [s_ref[rows, c * 128 : (c + 1) * 128] for c in range(KEYS // 128)]
            if offset is not None:
                parts = [
                    jnp.where(lead <= offset - c * 128, part, FAR_BELOW)
                    for c, part in enumerate(parts)
                ]
            highest = functools.reduce(jnp.maximum, parts)
            old = top[unit, rows]
            new = jnp.maximum(old, jnp.max(highest, axis=1, keepdims=True))
            top[unit, rows] = new
            scaled = new * EXP2_SCALE
            rescale = jnp.exp2(old * EXP2_SCALE - scaled)
            r_ref[rows] = rescale
            weights = [jnp.exp2(part * EXP2_SCALE - scaled) for part in parts]
            total[unit, rows] = total[unit, rows] * rescale + sum(weights)
            for c, weight in enumerate(weights):
                p_ref[rows, c * 128 : (c + 1) * 128] = weight.astype(jnp.bfloat16)

    def add_part(unit, block, p_ref, r_ref, part):
        rows = slice(part * ROWS // 2, (part + 1) * ROWS // 2)
        product = jnp.dot(
            p_ref[rows, :], k_ref[key_rows(block), :LATENT], preferred_element_type=jnp.float32
        )
        r = r_ref[rows]
        acc[unit, rows, :128] = acc[unit, rows, :128] * r + product[:, :128]
        acc[unit, rows, 128:] = acc[unit, rows, 128:] * r + product[:, 128:]

    def step(later, here, before, s_later, s_here, p_here, r_here, p_before, r_before, offset=None):
        score_part(*later, s_later, 0)
        weigh_part(here[0], s_here, p_here, r_here, offset, 0)
        score_part(*later, s_later, 1)
        weigh_part(here[0], s_here, p_here, r_here, offset, 1)
        add_part(*before, p_before, r_before, 0)
        weigh_part(here[0], s_here, p_here, r_here, offset, 2)
        add_part(*before, p_before, r_before, 1)
        weigh_part(here[0], s_here, p_here, r_here, offset, 3)

    def last_item(unit):
        return unit, jnp.where(unit % 2 == 0, blocks_of[0], blocks_of[1])

    def following(item):
        unit, block = item
        ends = block + 1 >= jnp.where(unit % 2 == 0, blocks_of[0], blocks_of[1])
        other = 1 - unit % 2
        other_empty = jnp.where(other == 0, blocks_of[0], blocks_of[1]) == 0
        jump = jnp.where(other_empty, 2, 1)
        unit = jnp.where(ends, unit + jump, unit)
        return unit, jnp.where(ends, 0, block + 1)

    def two_items(i, carry):
        before, here = carry[:2], carry[2:]
        after = following(here)
        step(after, here, before, s_b, s_a, p_a, r_a, p_b, r_b)
        later = following(after)
        at_end = later[0] >= 2 * tiles
        later = tuple(jnp.where(at_end, end, value) for end, value in zip(last_item(0), later))
        step(later, after, here, s_a, s_b, p_b, r_b, p_a, r_a)
        return after + later

    all_blocks = blocks_of[0] + blocks_of[1]
    first = (jnp.where(blocks_of[0] == 0, 1, 0), jnp.int32(0))
    first = tuple(
        jnp.where(all_blocks == 0, end, value) for end, value in zip(last_item(0), first)
    )
    for part in range(2):
        score_part(*first, s_a, part)
    carry = lax.fori_loop(
        0, all_blocks * (tiles // 2), two_items, (jnp.int32(0), jnp.int32(0)) + first
    )

    def two_last(i, carry):
        before = carry
        even, odd = last_item(2 * i), last_item(2 * i + 1)
        later = last_item(jnp.minimum(2 * i + 2, 2 * tiles - 1))
        step(odd, even, before, s_b, s_a, p_a, r_a, p_b, r_b, offset_of[0])
        step(later, odd, even, s_a, s_b, p_b, r_b, p_a, r_a, offset_of[1])
        return odd

    before = lax.fori_loop(0, tiles, two_last, carry[:2])
    for part in range(2):
        add_part(*before, p_b, r_b, part)
    wait(up_copies)

    def finish(tile, carry):
        attended = []
        for s in range(2):
            unit = 2 * tile + s
            share = 1.0 / jnp.sum(total[unit], axis=1, keepdims=True)
            attended.append((acc[unit] * share).astype(jnp.bfloat16))
        values = []
        for h in range(HEADS_TILE):
            rows = slice(h * SPAN, (h + 1) * SPAN)
            both = jnp.concatenate([attended[0][rows], attended[1][rows]], axis=0)
            values.append(
                jnp.dot(
                    both, up_ref[tile * HEADS_TILE + h], preferred_element_type=jnp.float32
                ).astype(jnp.bfloat16)
            )
        columns = HEADS_TILE * VDIM
        out_ref[:, pl.ds(pl.multiple_of(tile * columns, columns), columns)] = jnp.concatenate(
            values, axis=1
        )
        return carry

    lax.fori_loop(0, tiles, finish, 0)
    done_ref[...] = jnp.zeros_like(done_ref)


def prefill(ctx, spans, queries, keys, value_up):
    units = queries.shape[0]
    heads = value_up.shape[0]
    f32 = jnp.float32
    smem = pl.BlockSpec(memory_space=pltpu.SMEM)
    vmem = pl.BlockSpec(memory_space=pltpu.VMEM)
    hbm = pl.BlockSpec(memory_space=pltpu.HBM)
    return pl.pallas_call(
        prefill_kernel,
        out_shape=(
            jax.ShapeDtypeStruct((2 * SPAN, heads * VDIM), jnp.bfloat16),
            jax.ShapeDtypeStruct((8, 128), f32),
        ),
        in_specs=[smem] * 2 + [hbm] * 3,
        out_specs=(vmem, vmem),
        scratch_shapes=[
            pltpu.VMEM(queries.shape, jnp.bfloat16),
            pltpu.VMEM(keys.shape, jnp.bfloat16),
            pltpu.VMEM((2 * keys.shape[0] // KEYS, KPAD, KEYS // 2), jnp.bfloat16),
            pltpu.VMEM(value_up.shape, jnp.bfloat16),
            pltpu.VMEM((ROWS, KEYS), f32),
            pltpu.VMEM((ROWS, KEYS), f32),
            pltpu.VMEM((ROWS, KEYS), jnp.bfloat16),
            pltpu.VMEM((ROWS, KEYS), jnp.bfloat16),
            pltpu.VMEM((units, ROWS, 128), f32),
            pltpu.VMEM((units, ROWS, 128), f32),
            pltpu.VMEM((ROWS, 128), f32),
            pltpu.VMEM((ROWS, 128), f32),
            pltpu.VMEM((units, ROWS, LATENT), f32),
            pltpu.SemaphoreType.DMA((3, 4)),
        ],
        compiler_params=pltpu.CompilerParams(vmem_limit_bytes=59 << 20),
        cost_estimate=pl.CostEstimate(
            flops=units * ROWS * keys.shape[0] * 640,
            bytes_accessed=8 << 20,
            transcendentals=units * ROWS * keys.shape[0] // 2,
        ),
    )(ctx, spans, queries, keys, value_up)


def project_kernel(ctx_ref, grp_ref, rows_hbm, w_hbm, other_w_hbm, after_ref, *refs):
    out_refs, (rows_ref, w_ref, sums, sems) = refs[:4], refs[4:]
    chunks = sems.shape[1]
    width = rows_ref.shape[1] // chunks
    parts = [(slice(None), slice(c * width, (c + 1) * width)) for c in range(chunks)]
    sides = ((rows_hbm, rows_ref), (w_hbm, w_ref.at[0]), (other_w_hbm, w_ref.at[1]))
    copies = [
        [
            pltpu.make_async_copy(source.at[part], target.at[part], sems.at[i, c])
            for i, (source, target) in enumerate(sides)
        ]
        for c, part in enumerate(parts)
    ]
    for three in copies:
        for copy in three:
            copy.start()
    z, head_z, head_core = ctx_ref[0] // 16, grp_ref[0] // 2, grp_ref[0] % 2
    for c, part in enumerate(parts):
        for copy in copies[c]:
            copy.wait()
        for side in range(2):
            product = lax.dot_general(
                rows_ref[part], w_ref[side, :, part[1]], NT, preferred_element_type=jnp.float32
            )
            sums[side] = product if c == 0 else sums[side] + product
    share = sums.shape[1] // 2
    for k, out_ref in enumerate(out_refs):
        to_z, to_core = (head_z + k // 2) % 2, (head_core + k) % 2
        side = jnp.where(to_z == z, 0, 1)
        rows = pl.ds(pl.multiple_of(to_core * share, share), share)
        out_ref[...] = sums[side, rows, :].astype(jnp.bfloat16)


def project(ctx, grp, rows, weights, other_weights, after):
    smem = pl.BlockSpec(memory_space=pltpu.SMEM)
    vmem = pl.BlockSpec(memory_space=pltpu.VMEM)
    hbm = pl.BlockSpec(memory_space=pltpu.HBM)
    width, depth = weights.shape
    row_count = rows.shape[0]
    return pl.pallas_call(
        project_kernel,
        out_shape=(jax.ShapeDtypeStruct((row_count // 2, width), jnp.bfloat16),) * 4,
        in_specs=[smem, smem, hbm, hbm, hbm, pl.BlockSpec(memory_space=pl.ANY)],
        out_specs=(vmem,) * 4,
        scratch_shapes=[
            pltpu.VMEM(rows.shape, jnp.bfloat16),
            pltpu.VMEM((2, width, depth), jnp.bfloat16),
            pltpu.VMEM((2, row_count, width), jnp.float32),
            pltpu.SemaphoreType.DMA((3, 4)),
        ],
        compiler_params=pltpu.CompilerParams(vmem_limit_bytes=32 << 20),
        cost_estimate=pl.CostEstimate(
            flops=4 * row_count * depth * 256, bytes_accessed=8 << 20, transcendentals=0
        ),
    )(ctx, grp, rows, weights, other_weights, after)


def share_out(k, part):
    pairs = []
    for ctx in range(lax.axis_size("ctx")):
        z, line = divmod(ctx, 16)
        for a in range(2):
            for b in range(2):
                to = ((a ^ k // 2) * 16 + line) * 4 + 2 * z + (b ^ k % 2)
                pairs.append((ctx * 4 + 2 * a + b, to))
    return lax.ppermute(part, ("ctx", "grp"), pairs)


def body(
    prefill_queries,
    latents,
    rope_keys,
    span_slots,
    decode_queries,
    new_latents,
    new_rope,
    context_lengths,
    page_table,
    value_up,
    out_proj,
):
    ctx = lax.axis_index("ctx").astype(jnp.int32).reshape(1)
    grp = lax.axis_index("grp").astype(jnp.int32).reshape(1)
    rows_local = page_table.shape[0]

    own_first, second = gather_caches(*pack(latents, rope_keys))
    own_first, prefill_queries = lax.optimization_barrier((own_first, prefill_queries))
    other_first = swap(own_first, 16)
    queries, row_queries, fresh = arrange(prefill_queries, decode_queries, new_latents, new_rope)
    weights, other_first = lax.optimization_barrier((out_proj.T, other_first))
    other_weights = swap(weights, 16)
    blocks = own_first, other_first, second.reshape(-1, *second.shape[2:])
    keys, decode_values = decode(
        ctx, span_slots, page_table, context_lengths, row_queries, fresh, blocks, value_up
    )
    all_values = exchange(decode_values).reshape(-1, decode_values.shape[2])
    prefill_values, prefill_done = prefill(ctx, span_slots, queries, keys, value_up)
    parts = project(ctx, grp, all_values, weights, other_weights, prefill_done)
    summed = sum(share_out(k, part).astype(jnp.float32) for k, part in enumerate(parts))
    decoded = summed.astype(jnp.bfloat16).reshape(-1, 2, rows_local, summed.shape[1])
    decoded = decoded.transpose(1, 0, 2, 3).reshape(2, -1, summed.shape[1])
    return (prefill_values, decoded)


def solution(mesh):
    placed = (
        P("ctx", "grp"),
        P("ctx", "grp"),
        P("ctx", None),
        P(),
        P(None, "ctx", "grp"),
        P(None, "ctx", "grp"),
        P(None, "ctx", None),
        P("ctx"),
        P("ctx", None),
        P("grp", None, None),
        P("grp", "ctx"),
    )
    return jax.shard_map(
        body,
        mesh=mesh,
        in_specs=placed,
        out_specs=(P("ctx", "grp"), P(None, "grp", "ctx")),
        check_vma=False,
    )
```

```python
import functools
import math

import jax
import jax.numpy as jnp
from jax import lax
from jax.experimental import pallas as pl
from jax.experimental.pallas import tpu as pltpu
from jax.sharding import PartitionSpec as P

SPAN = 64
LATENT = 256
ROPE = 64
KEYW = LATENT + ROPE
KPAD = 384
VDIM = 128

HEADS_TILE = 8
ROWS = HEADS_TILE * SPAN
KEYS = 512

EXP2_SCALE = 192.0 ** -0.5 * math.log2(math.e)
FAR_BELOW = -1e30
NT = (((1,), (1,)), ((), ()))
RING = (0, -1, 1, 2)


def exchange(copies):
    size = lax.axis_size("ctx")
    groups = [list(range(z * size // 2, (z + 1) * size // 2)) for z in range(2)]
    return lax.all_to_all(
        copies, "ctx", split_axis=0, concat_axis=0, axis_index_groups=groups, tiled=True
    )


def shift(value, dz, dx, dy):
    pairs = []
    for ctx in range(lax.axis_size("ctx")):
        z, x, y = ctx // 16, ctx // 4 % 4, ctx % 4
        pairs.append((ctx, (z + dz) % 2 * 16 + (x + dx) % 4 * 4 + (y + dy) % 4))
    return lax.ppermute(value, "ctx", pairs)


def along(axis, steps):
    return (0, steps, 0) if axis == "x" else (0, 0, steps)


def gather_caches(own):
    other = shift(own, 1, 0, 0)
    axes = ("yx", "xy")
    held = [jnp.stack([own[half], other[half]]) for half in range(2)]
    for half in range(2):
        ring = [shift(held[half], *along(axes[half][0], -off)) for off in RING[1:]]
        held[half] = jnp.concatenate([held[half]] + ring)
    near = [
        [shift(held[half], *along(axes[half][1], -off)) for off in RING[1:3]] for half in range(2)
    ]
    cut = held[0].shape[0] // 2
    pieces = []
    for half in range(2):
        after, before = near[half]
        far_first = shift(after[:cut], *along(axes[half][1], 1))
        far_second = shift(before[cut:], *along(axes[half][1], -1))
        pieces += [held[half], after, before, far_first, far_second]
    return pieces


def block_offsets(half):
    places = []
    for last in RING:
        for first in RING:
            for dz in range(2):
                places.append((dz, last, first) if half == 0 else (dz, first, last))
    return places


def pack_kernel(latents_ref, rope_ref, out_ref):
    rope = rope_ref[...].astype(jnp.float32).T
    for span in range(2):
        rows = slice(span * SPAN, (span + 1) * SPAN)
        out_ref[span, :SPAN, :] = latents_ref[rows, :]
        parts = [rope[span * SPAN + c * 16 : span * SPAN + (c + 1) * 16] for c in range(4)]
        out_ref[span, SPAN:, :] = jnp.concatenate(parts, axis=1).astype(jnp.bfloat16)


def pack(latents, rope_keys):
    return pl.pallas_call(
        pack_kernel,
        out_shape=jax.ShapeDtypeStruct((2, SPAN + SPAN // 4, LATENT), jnp.bfloat16),
    )(latents, rope_keys.T)


def copies_in_parts(source, target, sems, axis=0):
    parts = sems.shape[0]
    size = source.shape[axis] // parts
    where = [(slice(None),) * axis + (slice(i * size, (i + 1) * size),) for i in range(parts)]
    return [
        pltpu.make_async_copy(source.at[at], target.at[at], sems.at[i])
        for i, at in enumerate(where)
    ]


def start(copies):
    for copy in copies:
        copy.start()


def wait(copies):
    for copy in copies:
        copy.wait()


def repeat_to(source, target, sems):
    size = source.shape[0]
    return [
        pltpu.make_async_copy(source, target.at[i * size : (i + 1) * size], sems.at[i])
        for i in range(target.shape[0] // size)
    ]


def unpack(block, keys_ref, place):
    rows = pl.ds(pl.multiple_of(place * SPAN, SPAN), SPAN)
    keys_ref[rows, :LATENT] = block[:SPAN, :]
    packed = block[SPAN:, :].astype(jnp.float32)
    low_lanes = lax.broadcasted_iota(jnp.int32, (16, 128), 1) < ROPE
    parts = []
    for c in range(2):
        two = packed[:, c * 128 : (c + 1) * 128]
        parts.append(jnp.where(low_lanes, two, 0.0))
        parts.append(jnp.where(low_lanes, pltpu.roll(two, 64, 1), 0.0))
    keys_ref[rows, LATENT:] = jnp.concatenate(parts, axis=0).astype(jnp.bfloat16)


def decode_kernel(ctx_ref, spans_ref, pages_ref, lengths_ref, *refs):
    q_ref, fresh_ref, *piece_refs, up_hbm, keys_hbm, values_hbm = refs[:15]
    up_ref, keys_ref, cache, att, values, sems = refs[15:]
    up_copies = copies_in_parts(up_hbm, up_ref, sems.at[0])
    start(up_copies)
    rows_local, pages = pages_ref.shape
    slots = pages * SPAN
    width = cache.shape[1]
    z, x, y = ctx_ref[0] // 16, ctx_ref[0] // 4 % 4, ctx_ref[0] % 4
    for half in range(2):
        blocks = [ref.at[i] for ref in piece_refs[5 * half : 5 * half + 5] for i in range(ref.shape[0])]
        for block, (dz, dx, dy) in zip(blocks, block_offsets(half)):
            source = (z + dz) % 2 * 16 + (x + dx + 4) % 4 * 4 + (y + dy + 4) % 4
            unpack(block, keys_ref, spans_ref[2 * source + half])
    keys_copies = copies_in_parts(keys_ref, keys_hbm, sems.at[1])
    start(keys_copies)
    for b in range(rows_local):
        cache[b, slots : slots + 16, :] = fresh_ref[b]
        cache[b, slots + 16 :, :] = jnp.zeros((width - slots - 16, KPAD), jnp.bfloat16)

    cols = lax.broadcasted_iota(jnp.int32, (64, width), 1)
    step = lax.broadcasted_iota(jnp.int32, (64, width), 0) // 32
    fresh_seen = (cols >= slots) & (cols - slots <= step)
    for b in range(rows_local):
        for j in range(pages):
            page = pages_ref[b, j]
            cache[b, j * SPAN : (j + 1) * SPAN, :] = keys_ref[
                pl.ds(pl.multiple_of(page * SPAN, SPAN), SPAN), :
            ]
        scores = lax.dot_general(q_ref[b], cache[b], NT, preferred_element_type=jnp.float32)
        seen = (cols < lengths_ref[b]) | fresh_seen
        scores = jnp.where(seen, scores, FAR_BELOW)
        top = jnp.max(scores, axis=1, keepdims=True)
        weights = jnp.exp2(scores * EXP2_SCALE - top * EXP2_SCALE)
        total = jnp.sum(weights, axis=1, keepdims=True)
        attended = jnp.dot(
            weights.astype(jnp.bfloat16), cache[b, :, :LATENT], preferred_element_type=jnp.float32
        )
        attended = attended / total
        for s in range(2):
            for c in range(2):
                att[c, pl.ds(s * rows_local + b, 32, stride=16), :] = attended[
                    s * 32 : (s + 1) * 32, c * 128 : (c + 1) * 128
                ]
    wait(up_copies)
    for h in range(32):
        mine = slice(h * 16, (h + 1) * 16)
        attended = jnp.concatenate([att[0, mine, :], att[1, mine, :]], axis=1)
        head_values = jnp.dot(
            attended.astype(jnp.bfloat16), up_ref[h], preferred_element_type=jnp.float32
        ).astype(jnp.bfloat16)
        for i in range(values.shape[0]):
            values[i, :, h * VDIM : (h + 1) * VDIM] = head_values
    values_copies = repeat_to(values, values_hbm, sems.at[2])
    start(values_copies)
    wait(values_copies)
    wait(keys_copies)


def decode(ctx, spans, pages, lengths, queries, fresh, pieces, value_up):
    smem = pl.BlockSpec(memory_space=pltpu.SMEM)
    vmem = pl.BlockSpec(memory_space=pltpu.VMEM)
    hbm = pl.BlockSpec(memory_space=pltpu.HBM)
    rows_local = pages.shape[0]
    heads = value_up.shape[0]
    key_rows = spans.shape[0] * SPAN
    return pl.pallas_call(
        decode_kernel,
        out_shape=(
            jax.ShapeDtypeStruct((key_rows, KPAD), jnp.bfloat16),
            jax.ShapeDtypeStruct((16, 2 * rows_local, heads * VDIM), jnp.bfloat16),
        ),
        in_specs=[smem] * 4 + [vmem] * 12 + [hbm],
        out_specs=(hbm, hbm),
        scratch_shapes=[
            pltpu.VMEM(value_up.shape, jnp.bfloat16),
            pltpu.VMEM((key_rows, KPAD), jnp.bfloat16),
            pltpu.VMEM((rows_local, pages.shape[1] * SPAN + 128, KPAD), jnp.bfloat16),
            pltpu.VMEM((2, 16 * heads, 128), jnp.float32),
            pltpu.VMEM((4, 2 * rows_local, heads * VDIM), jnp.bfloat16),
            pltpu.SemaphoreType.DMA((3, 4)),
        ],
        compiler_params=pltpu.CompilerParams(vmem_limit_bytes=48 << 20),
        cost_estimate=pl.CostEstimate(
            flops=2 * 8 * 64 * 1152 * 640, bytes_accessed=12 << 20, transcendentals=8 * 64 * 1152
        ),
    )(ctx, spans, pages, lengths, queries, fresh, *pieces, value_up)


def arrange_kernel(q_ref, dq_ref, new_latents_ref, new_rope_ref, *refs):
    out_ref, decode_out_ref, fresh_out_ref, decode_rows, fresh = refs
    for pair in range(HEADS_TILE // 2):
        at = pair * 2 * KEYW
        for s in range(2):
            tokens = slice(s * SPAN, (s + 1) * SPAN)
            out_ref[s, 2 * pair * SPAN : (2 * pair + 1) * SPAN, :] = q_ref[tokens, at : at + KPAD]
            odd = q_ref[tokens, at + 256 : at + 640].astype(jnp.float32)
            out_ref[s, (2 * pair + 1) * SPAN : (2 * pair + 2) * SPAN, :] = pltpu.roll(
                odd, KPAD - 64, 1
            ).astype(jnp.bfloat16)

    @pl.when(pl.program_id(0) == 0)
    def _():
        rows_local = dq_ref.shape[1]
        fresh[...] = jnp.zeros_like(fresh)
        for s in range(2):
            for h in range(32):
                at = h // 2 * 2 * KEYW + h % 2 * 256
                rows = dq_ref[s, :, at : at + KPAD].astype(jnp.float32)
                if h % 2:
                    rows = pltpu.roll(rows, KPAD - 64, 1)
                for c in range(3):
                    decode_rows[c, pl.ds(s * 32 + h, rows_local, stride=64), :] = rows[
                        :, c * 128 : (c + 1) * 128
                    ]
            mine = pl.ds(s, rows_local, stride=16)
            latent_rows = new_latents_ref[s].astype(jnp.float32)
            fresh[0, mine, :] = latent_rows[:, :128]
            fresh[1, mine, :] = latent_rows[:, 128:]
            rope_rows = new_rope_ref[s].astype(jnp.float32)
            fresh[2, mine, :] = jnp.concatenate([rope_rows, jnp.zeros_like(rope_rows)], axis=1)
        for b in range(rows_local):
            for rows_ref, out, size in ((decode_rows, decode_out_ref, 64), (fresh, fresh_out_ref, 16)):
                rows = slice(b * size, (b + 1) * size)
                parts = [rows_ref[c, rows, :] for c in range(3)]
                out[b] = jnp.concatenate(parts, axis=1).astype(jnp.bfloat16)


def arrange(queries, decode_queries, latents, rope):
    vmem = pl.BlockSpec(memory_space=pltpu.VMEM)
    rows_local = decode_queries.shape[1]
    tiles = queries.shape[1] // (HEADS_TILE * KEYW)
    bf16 = jnp.bfloat16
    whole = [(rows_local, 64, KPAD), (rows_local, 16, KPAD)]
    return pl.pallas_call(
        arrange_kernel,
        grid=(tiles,),
        out_shape=[jax.ShapeDtypeStruct((2 * tiles, ROWS, KPAD), bf16)]
        + [jax.ShapeDtypeStruct(shape, bf16) for shape in whole],
        in_specs=[pl.BlockSpec((2 * SPAN, HEADS_TILE * KEYW), lambda i: (0, i))] + [vmem] * 3,
        out_specs=[pl.BlockSpec((2, ROWS, KPAD), lambda i: (i, 0, 0))]
        + [pl.BlockSpec(shape, lambda i: (0, 0, 0)) for shape in whole],
        scratch_shapes=[
            pltpu.VMEM((3, 64 * rows_local, 128), jnp.float32),
            pltpu.VMEM((3, 16 * rows_local, 128), jnp.float32),
        ],
        compiler_params=pltpu.CompilerParams(vmem_limit_bytes=48 << 20),
        cost_estimate=pl.CostEstimate(flops=0, bytes_accessed=12 << 20, transcendentals=0),
    )(queries, decode_queries, latents, rope)


def clear(top, total, acc, p_b, r_b):
    top[...] = jnp.full(top.shape, FAR_BELOW, jnp.float32)
    total[...] = jnp.zeros_like(total)
    acc[...] = jnp.zeros_like(acc)
    p_b[...] = jnp.zeros_like(p_b)
    r_b[...] = jnp.ones_like(r_b)


def prefill_kernel(ctx_ref, spans_ref, qs_hbm, k_hbm, up_hbm, out_hbm, done_ref, *scratch):
    out_ref, qs, k_ref, kt_ref, up_ref, s_a, s_b, p_a, p_b, top, total, r_a, r_b, acc, sems = scratch
    tiles = acc.shape[0] // 2
    k_copies = copies_in_parts(k_hbm, k_ref, sems.at[0])
    q_copies = copies_in_parts(qs_hbm, qs, sems.at[1])
    up_copies = copies_in_parts(up_hbm, up_ref, sems.at[2])
    start(k_copies + q_copies)
    clear(top, total, acc, p_b, r_b)
    pieces = kt_ref.shape[0]
    for n in range(pieces):
        if n % (pieces // len(k_copies)) == 0:
            k_copies[n // (pieces // len(k_copies))].wait()
        kt_ref[n] = k_ref[n * KEYS // 2 : (n + 1) * KEYS // 2, :].T
    span_of = [spans_ref[2 * ctx_ref[0] + s] for s in range(2)]
    blocks_of = [span // (KEYS // SPAN) for span in span_of]
    offset_of = [(span_of[s] - blocks_of[s] * (KEYS // SPAN)) * SPAN for s in range(2)]
    wait(q_copies)
    start(up_copies)

    def key_rows(block):
        return pl.ds(pl.multiple_of(block * KEYS, KEYS), KEYS)

    def score_part(unit, block, s_ref, part):
        cols = slice(part * KEYS // 2, (part + 1) * KEYS // 2)
        s_ref[:, cols] = jnp.dot(
            qs[unit], kt_ref[2 * block + part], preferred_element_type=jnp.float32
        )

    lead = lax.broadcasted_iota(jnp.int32, (SPAN, 128), 1)
    lead = lead - lax.broadcasted_iota(jnp.int32, (SPAN, 128), 0)

    def weigh_part(unit, s_ref, p_ref, r_ref, offset, part):
        for h in range(part * HEADS_TILE // 4, (part + 1) * HEADS_TILE // 4):
            rows = slice(h * SPAN, (h + 1) * SPAN)
            parts = [s_ref[rows, c * 128 : (c + 1) * 128] for c in range(KEYS // 128)]
            if offset is not None:
                parts = [
                    jnp.where(lead <= offset - c * 128, part, FAR_BELOW)
                    for c, part in enumerate(parts)
                ]
            highest = functools.reduce(jnp.maximum, parts)
            old = top[unit, rows]
            new = jnp.maximum(old, jnp.max(highest, axis=1, keepdims=True))
            top[unit, rows] = new
            scaled = new * EXP2_SCALE
            rescale = jnp.exp2(old * EXP2_SCALE - scaled)
            r_ref[rows] = rescale
            weights = [jnp.exp2(part * EXP2_SCALE - scaled) for part in parts]
            total[unit, rows] = total[unit, rows] * rescale + sum(weights)
            for c, weight in enumerate(weights):
                p_ref[rows, c * 128 : (c + 1) * 128] = weight.astype(jnp.bfloat16)

    def add_part(unit, block, p_ref, r_ref, part):
        rows = slice(part * ROWS // 2, (part + 1) * ROWS // 2)
        product = jnp.dot(
            p_ref[rows, :], k_ref[key_rows(block), :LATENT], preferred_element_type=jnp.float32
        )
        r = r_ref[rows]
        acc[unit, rows, :128] = acc[unit, rows, :128] * r + product[:, :128]
        acc[unit, rows, 128:] = acc[unit, rows, 128:] * r + product[:, 128:]

    def step(later, here, before, s_later, s_here, p_here, r_here, p_before, r_before, offset=None):
        score_part(*later, s_later, 0)
        weigh_part(here[0], s_here, p_here, r_here, offset, 0)
        score_part(*later, s_later, 1)
        weigh_part(here[0], s_here, p_here, r_here, offset, 1)
        add_part(*before, p_before, r_before, 0)
        weigh_part(here[0], s_here, p_here, r_here, offset, 2)
        add_part(*before, p_before, r_before, 1)
        weigh_part(here[0], s_here, p_here, r_here, offset, 3)

    def last_item(unit):
        return unit, jnp.where(unit % 2 == 0, blocks_of[0], blocks_of[1])

    def following(item):
        unit, block = item
        ends = block + 1 >= jnp.where(unit % 2 == 0, blocks_of[0], blocks_of[1])
        other = 1 - unit % 2
        other_empty = jnp.where(other == 0, blocks_of[0], blocks_of[1]) == 0
        jump = jnp.where(other_empty, 2, 1)
        unit = jnp.where(ends, unit + jump, unit)
        return unit, jnp.where(ends, 0, block + 1)

    def two_items(i, carry):
        before, here = carry[:2], carry[2:]
        after = following(here)
        step(after, here, before, s_b, s_a, p_a, r_a, p_b, r_b)
        later = following(after)
        at_end = later[0] >= 2 * tiles
        later = tuple(jnp.where(at_end, end, value) for end, value in zip(last_item(0), later))
        step(later, after, here, s_a, s_b, p_b, r_b, p_a, r_a)
        return after + later

    all_blocks = blocks_of[0] + blocks_of[1]
    first = (jnp.where(blocks_of[0] == 0, 1, 0), jnp.int32(0))
    first = tuple(
        jnp.where(all_blocks == 0, end, value) for end, value in zip(last_item(0), first)
    )
    for part in range(2):
        score_part(*first, s_a, part)
    carry = lax.fori_loop(
        0, all_blocks * (tiles // 2), two_items, (jnp.int32(0), jnp.int32(0)) + first
    )

    def two_last(i, carry):
        before = carry
        even, odd = last_item(2 * i), last_item(2 * i + 1)
        later = last_item(jnp.minimum(2 * i + 2, 2 * tiles - 1))
        step(odd, even, before, s_b, s_a, p_a, r_a, p_b, r_b, offset_of[0])
        step(later, odd, even, s_a, s_b, p_b, r_b, p_a, r_a, offset_of[1])
        return odd

    before = lax.fori_loop(0, tiles, two_last, carry[:2])
    for part in range(2):
        add_part(*before, p_b, r_b, part)
    wait(up_copies)

    out_copies = copies_in_parts(out_ref, out_hbm, sems.at[3], axis=1)
    for tile in range(tiles):
        attended = []
        for s in range(2):
            unit = 2 * tile + s
            share = 1.0 / jnp.sum(total[unit], axis=1, keepdims=True)
            attended.append((acc[unit] * share).astype(jnp.bfloat16))
        for h in range(HEADS_TILE):
            rows = slice(h * SPAN, (h + 1) * SPAN)
            both = jnp.concatenate([attended[0][rows], attended[1][rows]], axis=0)
            head = tile * HEADS_TILE + h
            out_ref[:, head * VDIM : (head + 1) * VDIM] = jnp.dot(
                both, up_ref[head], preferred_element_type=jnp.float32
            ).astype(jnp.bfloat16)
        out_copies[tile].start()
    wait(out_copies)
    done_ref[...] = jnp.zeros_like(done_ref)


def prefill(ctx, spans, queries, keys, value_up):
    units = queries.shape[0]
    heads = value_up.shape[0]
    f32 = jnp.float32
    smem = pl.BlockSpec(memory_space=pltpu.SMEM)
    vmem = pl.BlockSpec(memory_space=pltpu.VMEM)
    hbm = pl.BlockSpec(memory_space=pltpu.HBM)
    return pl.pallas_call(
        prefill_kernel,
        out_shape=(
            jax.ShapeDtypeStruct((2 * SPAN, heads * VDIM), jnp.bfloat16),
            jax.ShapeDtypeStruct((8, 128), f32),
        ),
        in_specs=[smem] * 2 + [hbm] * 3,
        out_specs=(hbm, vmem),
        scratch_shapes=[
            pltpu.VMEM((2 * SPAN, heads * VDIM), jnp.bfloat16),
            pltpu.VMEM(queries.shape, jnp.bfloat16),
            pltpu.VMEM(keys.shape, jnp.bfloat16),
            pltpu.VMEM((2 * keys.shape[0] // KEYS, KPAD, KEYS // 2), jnp.bfloat16),
            pltpu.VMEM(value_up.shape, jnp.bfloat16),
            pltpu.VMEM((ROWS, KEYS), f32),
            pltpu.VMEM((ROWS, KEYS), f32),
            pltpu.VMEM((ROWS, KEYS), jnp.bfloat16),
            pltpu.VMEM((ROWS, KEYS), jnp.bfloat16),
            pltpu.VMEM((units, ROWS, 128), f32),
            pltpu.VMEM((units, ROWS, 128), f32),
            pltpu.VMEM((ROWS, 128), f32),
            pltpu.VMEM((ROWS, 128), f32),
            pltpu.VMEM((units, ROWS, LATENT), f32),
            pltpu.SemaphoreType.DMA((4, 4)),
        ],
        compiler_params=pltpu.CompilerParams(vmem_limit_bytes=59 << 20),
        cost_estimate=pl.CostEstimate(
            flops=units * ROWS * keys.shape[0] * 640,
            bytes_accessed=8 << 20,
            transcendentals=units * ROWS * keys.shape[0] // 2,
        ),
    )(ctx, spans, queries, keys, value_up)


def project_kernel(ctx_ref, grp_ref, rows_hbm, w_hbm, other_w_hbm, after_ref, *refs):
    out_refs, (rows_ref, w_ref, sums, sems) = refs[:4], refs[4:]
    chunks = sems.shape[1]
    width = rows_ref.shape[1] // chunks
    parts = [(slice(None), slice(c * width, (c + 1) * width)) for c in range(chunks)]
    sides = ((rows_hbm, rows_ref), (w_hbm, w_ref.at[0]), (other_w_hbm, w_ref.at[1]))
    copies = [
        [
            pltpu.make_async_copy(source.at[part], target.at[part], sems.at[i, c])
            for i, (source, target) in enumerate(sides)
        ]
        for c, part in enumerate(parts)
    ]
    for three in copies:
        for copy in three:
            copy.start()
    z, head_z, head_core = ctx_ref[0] // 16, grp_ref[0] // 2, grp_ref[0] % 2
    for c, part in enumerate(parts):
        for copy in copies[c]:
            copy.wait()
        for side in range(2):
            product = lax.dot_general(
                rows_ref[part], w_ref[side, :, part[1]], NT, preferred_element_type=jnp.float32
            )
            sums[side] = product if c == 0 else sums[side] + product
    share = sums.shape[1] // 2
    for k, out_ref in enumerate(out_refs):
        to_z, to_core = (head_z + k // 2) % 2, (head_core + k) % 2
        side = jnp.where(to_z == z, 0, 1)
        rows = pl.ds(pl.multiple_of(to_core * share, share), share)
        out_ref[...] = sums[side, rows, :].astype(jnp.bfloat16)


def project(ctx, grp, rows, weights, other_weights, after):
    smem = pl.BlockSpec(memory_space=pltpu.SMEM)
    vmem = pl.BlockSpec(memory_space=pltpu.VMEM)
    hbm = pl.BlockSpec(memory_space=pltpu.HBM)
    width, depth = weights.shape
    row_count = rows.shape[0]
    return pl.pallas_call(
        project_kernel,
        out_shape=(jax.ShapeDtypeStruct((row_count // 2, width), jnp.bfloat16),) * 4,
        in_specs=[smem, smem, hbm, hbm, hbm, pl.BlockSpec(memory_space=pl.ANY)],
        out_specs=(vmem,) * 4,
        scratch_shapes=[
            pltpu.VMEM(rows.shape, jnp.bfloat16),
            pltpu.VMEM((2, width, depth), jnp.bfloat16),
            pltpu.VMEM((2, row_count, width), jnp.float32),
            pltpu.SemaphoreType.DMA((3, 4)),
        ],
        compiler_params=pltpu.CompilerParams(vmem_limit_bytes=32 << 20),
        cost_estimate=pl.CostEstimate(
            flops=4 * row_count * depth * 256, bytes_accessed=8 << 20, transcendentals=0
        ),
    )(ctx, grp, rows, weights, other_weights, after)


def share_out(k, part):
    pairs = []
    for ctx in range(lax.axis_size("ctx")):
        z, line = divmod(ctx, 16)
        for a in range(2):
            for b in range(2):
                to = ((a ^ k // 2) * 16 + line) * 4 + 2 * z + (b ^ k % 2)
                pairs.append((ctx * 4 + 2 * a + b, to))
    return lax.ppermute(part, ("ctx", "grp"), pairs)


def body(
    prefill_queries,
    latents,
    rope_keys,
    span_slots,
    decode_queries,
    new_latents,
    new_rope,
    context_lengths,
    page_table,
    value_up,
    out_proj,
):
    ctx = lax.axis_index("ctx").astype(jnp.int32).reshape(1)
    grp = lax.axis_index("grp").astype(jnp.int32).reshape(1)
    rows_local = page_table.shape[0]

    pieces = gather_caches(pack(latents, rope_keys))
    queries, row_queries, fresh = arrange(prefill_queries, decode_queries, new_latents, new_rope)
    keys, decode_values = decode(
        ctx, span_slots, page_table, context_lengths, row_queries, fresh, pieces, value_up
    )
    weights = out_proj.T
    other_weights = shift(weights, 1, 0, 0)
    all_values = exchange(decode_values).reshape(-1, decode_values.shape[2])
    prefill_values, prefill_done = prefill(ctx, span_slots, queries, keys, value_up)
    parts = project(ctx, grp, all_values, weights, other_weights, prefill_done)
    summed = sum(share_out(k, part).astype(jnp.float32) for k, part in enumerate(parts))
    decoded = summed.astype(jnp.bfloat16).reshape(-1, 2, rows_local, summed.shape[1])
    decoded = decoded.transpose(1, 0, 2, 3).reshape(2, -1, summed.shape[1])
    return (prefill_values, decoded)


def solution(mesh):
    placed = (
        P("ctx", "grp"),
        P("ctx", "grp"),
        P("ctx", None),
        P(),
        P(None, "ctx", "grp"),
        P(None, "ctx", "grp"),
        P(None, "ctx", None),
        P("ctx"),
        P("ctx", None),
        P("grp", None, None),
        P("grp", "ctx"),
    )
    return jax.shard_map(
        body,
        mesh=mesh,
        in_specs=placed,
        out_specs=(P("ctx", "grp"), P(None, "grp", "ctx")),
        check_vma=False,
    )
```

```python
import functools
import math

import jax
import jax.numpy as jnp
from jax import lax
from jax.experimental import pallas as pl
from jax.experimental.pallas import tpu as pltpu
from jax.sharding import PartitionSpec as P

SPAN = 64
LATENT = 256
ROPE = 64
KEYW = LATENT + ROPE
KPAD = 384
VDIM = 128

HEADS_TILE = 8
ROWS = HEADS_TILE * SPAN
KEYS = 512

EXP2_SCALE = 192.0 ** -0.5 * math.log2(math.e)
FAR_BELOW = -1e30
NT = (((1,), (1,)), ((), ()))
RING = (0, -1, 1, 2)


def exchange(copies):
    size = lax.axis_size("ctx")
    groups = [list(range(z * size // 2, (z + 1) * size // 2)) for z in range(2)]
    return lax.all_to_all(
        copies, "ctx", split_axis=0, concat_axis=0, axis_index_groups=groups, tiled=True
    )


def shift(value, dz, dx, dy):
    pairs = []
    for ctx in range(lax.axis_size("ctx")):
        z, x, y = ctx // 16, ctx // 4 % 4, ctx % 4
        pairs.append((ctx, (z + dz) % 2 * 16 + (x + dx) % 4 * 4 + (y + dy) % 4))
    return lax.ppermute(value, "ctx", pairs)


def along(axis, steps):
    return (0, steps, 0) if axis == "x" else (0, 0, steps)


def gather_caches(own):
    other = shift(own, 1, 0, 0)
    axes = ("yx", "xy")
    held = [jnp.stack([own[half], other[half]]) for half in range(2)]
    for half in range(2):
        ring = [shift(held[half], *along(axes[half][0], -off)) for off in RING[1:]]
        held[half] = jnp.concatenate([held[half]] + ring)
    near = [
        [shift(held[half], *along(axes[half][1], -off)) for off in RING[1:3]] for half in range(2)
    ]
    cut = held[0].shape[0] // 2
    pieces = []
    for half in range(2):
        after, before = near[half]
        far_first = shift(after[:cut], *along(axes[half][1], 1))
        far_second = shift(before[cut:], *along(axes[half][1], -1))
        pieces += [held[half], after, before, far_first, far_second]
    return pieces


def block_offsets(half):
    places = []
    for last in RING:
        for first in RING:
            for dz in range(2):
                places.append((dz, last, first) if half == 0 else (dz, first, last))
    return places


def pack_kernel(latents_ref, rope_ref, out_ref):
    rope = rope_ref[...].astype(jnp.float32).T
    for span in range(2):
        rows = slice(span * SPAN, (span + 1) * SPAN)
        out_ref[span, :SPAN, :] = latents_ref[rows, :]
        parts = [rope[span * SPAN + c * 16 : span * SPAN + (c + 1) * 16] for c in range(4)]
        out_ref[span, SPAN:, :] = jnp.concatenate(parts, axis=1).astype(jnp.bfloat16)


def pack(latents, rope_keys):
    return pl.pallas_call(
        pack_kernel,
        out_shape=jax.ShapeDtypeStruct((2, SPAN + SPAN // 4, LATENT), jnp.bfloat16),
    )(latents, rope_keys.T)


def copies_in_parts(source, target, sems, axis=0):
    parts = sems.shape[0]
    size = source.shape[axis] // parts
    where = [(slice(None),) * axis + (slice(i * size, (i + 1) * size),) for i in range(parts)]
    return [
        pltpu.make_async_copy(source.at[at], target.at[at], sems.at[i])
        for i, at in enumerate(where)
    ]


def start(copies):
    for copy in copies:
        copy.start()


def wait(copies):
    for copy in copies:
        copy.wait()


def repeat_to(source, target, sems):
    size = source.shape[0]
    return [
        pltpu.make_async_copy(source, target.at[i * size : (i + 1) * size], sems.at[i])
        for i in range(target.shape[0] // size)
    ]


def unpack(block, keys_ref, place):
    rows = pl.ds(pl.multiple_of(place * SPAN, SPAN), SPAN)
    keys_ref[rows, :LATENT] = block[:SPAN, :]
    packed = block[SPAN:, :].astype(jnp.float32)
    low_lanes = lax.broadcasted_iota(jnp.int32, (16, 128), 1) < ROPE
    parts = []
    for c in range(2):
        two = packed[:, c * 128 : (c + 1) * 128]
        parts.append(jnp.where(low_lanes, two, 0.0))
        parts.append(jnp.where(low_lanes, pltpu.roll(two, 64, 1), 0.0))
    keys_ref[rows, LATENT:] = jnp.concatenate(parts, axis=0).astype(jnp.bfloat16)


def decode_kernel(ctx_ref, spans_ref, pages_ref, lengths_ref, *refs):
    q_ref, fresh_ref, *piece_refs, up_hbm, keys_hbm, values_hbm = refs[:15]
    up_ref, keys_ref, cache, att, values, sems = refs[15:]
    up_copies = copies_in_parts(up_hbm, up_ref, sems.at[0])
    start(up_copies)
    rows_local, pages = pages_ref.shape
    slots = pages * SPAN
    width = cache.shape[1]
    z, x, y = ctx_ref[0] // 16, ctx_ref[0] // 4 % 4, ctx_ref[0] % 4
    for half in range(2):
        blocks = [ref.at[i] for ref in piece_refs[5 * half : 5 * half + 5] for i in range(ref.shape[0])]
        for block, (dz, dx, dy) in zip(blocks, block_offsets(half)):
            source = (z + dz) % 2 * 16 + (x + dx + 4) % 4 * 4 + (y + dy + 4) % 4
            unpack(block, keys_ref, spans_ref[2 * source + half])
    keys_copies = copies_in_parts(keys_ref, keys_hbm, sems.at[1])
    start(keys_copies)
    for b in range(rows_local):
        cache[b, slots : slots + 16, :] = fresh_ref[b]
        cache[b, slots + 16 :, :] = jnp.zeros((width - slots - 16, KPAD), jnp.bfloat16)

    cols = lax.broadcasted_iota(jnp.int32, (64, width), 1)
    step = lax.broadcasted_iota(jnp.int32, (64, width), 0) // 32
    fresh_seen = (cols >= slots) & (cols - slots <= step)
    for b in range(rows_local):
        for j in range(pages):
            page = pages_ref[b, j]
            cache[b, j * SPAN : (j + 1) * SPAN, :] = keys_ref[
                pl.ds(pl.multiple_of(page * SPAN, SPAN), SPAN), :
            ]
        scores = lax.dot_general(q_ref[b], cache[b], NT, preferred_element_type=jnp.float32)
        seen = (cols < lengths_ref[b]) | fresh_seen
        scores = jnp.where(seen, scores, FAR_BELOW)
        top = jnp.max(scores, axis=1, keepdims=True)
        weights = jnp.exp2(scores * EXP2_SCALE - top * EXP2_SCALE)
        total = jnp.sum(weights, axis=1, keepdims=True)
        attended = jnp.dot(
            weights.astype(jnp.bfloat16), cache[b, :, :LATENT], preferred_element_type=jnp.float32
        )
        attended = attended / total
        for s in range(2):
            for c in range(2):
                att[c, pl.ds(s * rows_local + b, 32, stride=16), :] = attended[
                    s * 32 : (s + 1) * 32, c * 128 : (c + 1) * 128
                ]
    wait(up_copies)
    for h in range(32):
        mine = slice(h * 16, (h + 1) * 16)
        attended = jnp.concatenate([att[0, mine, :], att[1, mine, :]], axis=1)
        head_values = jnp.dot(
            attended.astype(jnp.bfloat16), up_ref[h], preferred_element_type=jnp.float32
        ).astype(jnp.bfloat16)
        for i in range(values.shape[0]):
            values[i, :, h * VDIM : (h + 1) * VDIM] = head_values
    values_copies = repeat_to(values, values_hbm, sems.at[2])
    start(values_copies)
    wait(values_copies)
    wait(keys_copies)


def decode(ctx, spans, pages, lengths, queries, fresh, pieces, value_up):
    smem = pl.BlockSpec(memory_space=pltpu.SMEM)
    vmem = pl.BlockSpec(memory_space=pltpu.VMEM)
    hbm = pl.BlockSpec(memory_space=pltpu.HBM)
    rows_local = pages.shape[0]
    heads = value_up.shape[0]
    key_rows = spans.shape[0] * SPAN
    return pl.pallas_call(
        decode_kernel,
        out_shape=(
            jax.ShapeDtypeStruct((key_rows, KPAD), jnp.bfloat16),
            jax.ShapeDtypeStruct((16, 2 * rows_local, heads * VDIM), jnp.bfloat16),
        ),
        in_specs=[smem] * 4 + [vmem] * 12 + [hbm],
        out_specs=(hbm, hbm),
        scratch_shapes=[
            pltpu.VMEM(value_up.shape, jnp.bfloat16),
            pltpu.VMEM((key_rows, KPAD), jnp.bfloat16),
            pltpu.VMEM((rows_local, pages.shape[1] * SPAN + 128, KPAD), jnp.bfloat16),
            pltpu.VMEM((2, 16 * heads, 128), jnp.float32),
            pltpu.VMEM((4, 2 * rows_local, heads * VDIM), jnp.bfloat16),
            pltpu.SemaphoreType.DMA((3, 4)),
        ],
        compiler_params=pltpu.CompilerParams(vmem_limit_bytes=57 << 20),
        cost_estimate=pl.CostEstimate(
            flops=2 * 8 * 64 * 1152 * 640, bytes_accessed=12 << 20, transcendentals=8 * 64 * 1152
        ),
    )(ctx, spans, pages, lengths, queries, fresh, *pieces, value_up)


def arrange_kernel(q_ref, dq_ref, new_latents_ref, new_rope_ref, *refs):
    out_ref, decode_out_ref, fresh_out_ref, decode_rows, fresh = refs
    for pair in range(HEADS_TILE // 2):
        at = pair * 2 * KEYW
        for s in range(2):
            tokens = slice(s * SPAN, (s + 1) * SPAN)
            out_ref[s, 2 * pair * SPAN : (2 * pair + 1) * SPAN, :] = q_ref[tokens, at : at + KPAD]
            odd = q_ref[tokens, at + 256 : at + 640].astype(jnp.float32)
            out_ref[s, (2 * pair + 1) * SPAN : (2 * pair + 2) * SPAN, :] = pltpu.roll(
                odd, KPAD - 64, 1
            ).astype(jnp.bfloat16)

    @pl.when(pl.program_id(0) == 0)
    def _():
        rows_local = dq_ref.shape[1]
        fresh[...] = jnp.zeros_like(fresh)
        for s in range(2):
            for h in range(32):
                at = h // 2 * 2 * KEYW + h % 2 * 256
                rows = dq_ref[s, :, at : at + KPAD].astype(jnp.float32)
                if h % 2:
                    rows = pltpu.roll(rows, KPAD - 64, 1)
                for c in range(3):
                    decode_rows[c, pl.ds(s * 32 + h, rows_local, stride=64), :] = rows[
                        :, c * 128 : (c + 1) * 128
                    ]
            mine = pl.ds(s, rows_local, stride=16)
            latent_rows = new_latents_ref[s].astype(jnp.float32)
            fresh[0, mine, :] = latent_rows[:, :128]
            fresh[1, mine, :] = latent_rows[:, 128:]
            rope_rows = new_rope_ref[s].astype(jnp.float32)
            fresh[2, mine, :] = jnp.concatenate([rope_rows, jnp.zeros_like(rope_rows)], axis=1)
        for b in range(rows_local):
            for rows_ref, out, size in ((decode_rows, decode_out_ref, 64), (fresh, fresh_out_ref, 16)):
                rows = slice(b * size, (b + 1) * size)
                parts = [rows_ref[c, rows, :] for c in range(3)]
                out[b] = jnp.concatenate(parts, axis=1).astype(jnp.bfloat16)


def arrange(queries, decode_queries, latents, rope):
    vmem = pl.BlockSpec(memory_space=pltpu.VMEM)
    rows_local = decode_queries.shape[1]
    tiles = queries.shape[1] // (HEADS_TILE * KEYW)
    bf16 = jnp.bfloat16
    whole = [(rows_local, 64, KPAD), (rows_local, 16, KPAD)]
    return pl.pallas_call(
        arrange_kernel,
        grid=(tiles,),
        out_shape=[jax.ShapeDtypeStruct((2 * tiles, ROWS, KPAD), bf16)]
        + [jax.ShapeDtypeStruct(shape, bf16) for shape in whole],
        in_specs=[pl.BlockSpec((2 * SPAN, HEADS_TILE * KEYW), lambda i: (0, i))] + [vmem] * 3,
        out_specs=[pl.BlockSpec((2, ROWS, KPAD), lambda i: (i, 0, 0))]
        + [pl.BlockSpec(shape, lambda i: (0, 0, 0)) for shape in whole],
        scratch_shapes=[
            pltpu.VMEM((3, 64 * rows_local, 128), jnp.float32),
            pltpu.VMEM((3, 16 * rows_local, 128), jnp.float32),
        ],
        compiler_params=pltpu.CompilerParams(vmem_limit_bytes=16 << 20),
        cost_estimate=pl.CostEstimate(flops=0, bytes_accessed=12 << 20, transcendentals=0),
    )(queries, decode_queries, latents, rope)


def clear(top, total, acc, p_b, r_b):
    top[...] = jnp.full(top.shape, FAR_BELOW, jnp.float32)
    total[...] = jnp.zeros_like(total)
    acc[...] = jnp.zeros_like(acc)
    p_b[...] = jnp.zeros_like(p_b)
    r_b[...] = jnp.ones_like(r_b)


def prefill_kernel(ctx_ref, spans_ref, qs_hbm, k_hbm, up_hbm, out_hbm, done_ref, *scratch):
    out_ref, qs, k_ref, kt_ref, up_ref, s_a, s_b, p_a, p_b, top, total, r_a, r_b, acc, sems = scratch
    tiles = acc.shape[0] // 2
    k_copies = copies_in_parts(k_hbm, k_ref, sems.at[0])
    q_copies = copies_in_parts(qs_hbm, qs, sems.at[1])
    up_copies = copies_in_parts(up_hbm, up_ref, sems.at[2])
    start(k_copies + q_copies)
    clear(top, total, acc, p_b, r_b)
    pieces = kt_ref.shape[0]
    for n in range(pieces):
        if n % (pieces // len(k_copies)) == 0:
            k_copies[n // (pieces // len(k_copies))].wait()
        kt_ref[n] = k_ref[n * KEYS // 2 : (n + 1) * KEYS // 2, :].T
    span_of = [spans_ref[2 * ctx_ref[0] + s] for s in range(2)]
    blocks_of = [span // (KEYS // SPAN) for span in span_of]
    offset_of = [(span_of[s] - blocks_of[s] * (KEYS // SPAN)) * SPAN for s in range(2)]
    wait(q_copies)
    start(up_copies)

    def key_rows(block):
        return pl.ds(pl.multiple_of(block * KEYS, KEYS), KEYS)

    def score_part(unit, block, s_ref, part):
        cols = slice(part * KEYS // 2, (part + 1) * KEYS // 2)
        s_ref[:, cols] = jnp.dot(
            qs[unit], kt_ref[2 * block + part], preferred_element_type=jnp.float32
        )

    lead = lax.broadcasted_iota(jnp.int32, (SPAN, 128), 1)
    lead = lead - lax.broadcasted_iota(jnp.int32, (SPAN, 128), 0)

    def weigh_part(unit, s_ref, p_ref, r_ref, offset, part):
        for h in range(part * HEADS_TILE // 4, (part + 1) * HEADS_TILE // 4):
            rows = slice(h * SPAN, (h + 1) * SPAN)
            parts = [s_ref[rows, c * 128 : (c + 1) * 128] for c in range(KEYS // 128)]
            parts = [
                jnp.where(lead <= offset - c * 128, part, FAR_BELOW)
                for c, part in enumerate(parts)
            ]
            highest = functools.reduce(jnp.maximum, parts)
            old = top[unit, rows]
            new = jnp.maximum(old, jnp.max(highest, axis=1, keepdims=True))
            top[unit, rows] = new
            scaled = new * EXP2_SCALE
            rescale = jnp.exp2(old * EXP2_SCALE - scaled)
            r_ref[rows] = rescale
            weights = [jnp.exp2(part * EXP2_SCALE - scaled) for part in parts]
            total[unit, rows] = total[unit, rows] * rescale + sum(weights)
            for c, weight in enumerate(weights):
                p_ref[rows, c * 128 : (c + 1) * 128] = weight.astype(jnp.bfloat16)

    def add_part(unit, block, p_ref, r_ref, part):
        rows = slice(part * ROWS // 2, (part + 1) * ROWS // 2)
        product = jnp.dot(
            p_ref[rows, :], k_ref[key_rows(block), :LATENT], preferred_element_type=jnp.float32
        )
        r = r_ref[rows]
        acc[unit, rows, :128] = acc[unit, rows, :128] * r + product[:, :128]
        acc[unit, rows, 128:] = acc[unit, rows, 128:] * r + product[:, 128:]

    def step(later, here, before, s_later, s_here, p_here, r_here, p_before, r_before, offset):
        score_part(*later, s_later, 0)
        weigh_part(here[0], s_here, p_here, r_here, offset, 0)
        score_part(*later, s_later, 1)
        weigh_part(here[0], s_here, p_here, r_here, offset, 1)
        add_part(*before, p_before, r_before, 0)
        weigh_part(here[0], s_here, p_here, r_here, offset, 2)
        add_part(*before, p_before, r_before, 1)
        weigh_part(here[0], s_here, p_here, r_here, offset, 3)

    def last_block(unit):
        return jnp.where(unit % 2 == 0, blocks_of[0], blocks_of[1])

    def following(item):
        unit, block = item
        ends = block == last_block(unit)
        unit = jnp.minimum(jnp.where(ends, unit + 1, unit), 2 * tiles - 1)
        return unit, jnp.where(ends, 0, block + 1)

    def offset(item):
        unit, block = item
        own = jnp.where(unit % 2 == 0, offset_of[0], offset_of[1])
        return jnp.where(block == last_block(unit), own, KEYS)

    def two_items(i, carry):
        before, here = carry[:2], carry[2:]
        after = following(here)
        step(after, here, before, s_b, s_a, p_a, r_a, p_b, r_b, offset(here))
        later = following(after)
        step(later, after, here, s_a, s_b, p_b, r_b, p_a, r_a, offset(after))
        return after + later

    for part in range(2):
        score_part(0, 0, s_a, part)
    rounds = (blocks_of[0] + blocks_of[1] + 2) * (tiles // 2)
    before = lax.fori_loop(0, rounds, two_items, (jnp.int32(0),) * 4)[:2]
    for part in range(2):
        add_part(*before, p_b, r_b, part)
    wait(up_copies)

    def out_copy(tile):
        width = HEADS_TILE * VDIM
        columns = pl.ds(pl.multiple_of(tile * width, width), width)
        return pltpu.make_async_copy(
            out_ref.at[:, columns], out_hbm.at[:, columns], sems.at[3, tile]
        )

    def finish(tile, carry):
        attended = []
        for s in range(2):
            unit = 2 * tile + s
            share = 1.0 / jnp.sum(total[unit], axis=1, keepdims=True)
            attended.append((acc[unit] * share).astype(jnp.bfloat16))
        values = []
        for h in range(HEADS_TILE):
            rows = slice(h * SPAN, (h + 1) * SPAN)
            both = jnp.concatenate([attended[0][rows], attended[1][rows]], axis=0)
            values.append(
                jnp.dot(
                    both, up_ref[tile * HEADS_TILE + h], preferred_element_type=jnp.float32
                ).astype(jnp.bfloat16)
            )
        columns = HEADS_TILE * VDIM
        out_ref[:, pl.ds(pl.multiple_of(tile * columns, columns), columns)] = jnp.concatenate(
            values, axis=1
        )
        out_copy(tile).start()
        return carry

    lax.fori_loop(0, tiles, finish, 0)
    for tile in range(tiles):
        out_copy(tile).wait()
    done_ref[0] = 0


def prefill(ctx, spans, queries, keys, value_up):
    units = queries.shape[0]
    heads = value_up.shape[0]
    f32 = jnp.float32
    smem = pl.BlockSpec(memory_space=pltpu.SMEM)
    hbm = pl.BlockSpec(memory_space=pltpu.HBM)
    return pl.pallas_call(
        prefill_kernel,
        out_shape=(
            jax.ShapeDtypeStruct((2 * SPAN, heads * VDIM), jnp.bfloat16),
            jax.ShapeDtypeStruct((1,), jnp.int32),
        ),
        in_specs=[smem] * 2 + [hbm] * 3,
        out_specs=(hbm, smem),
        scratch_shapes=[
            pltpu.VMEM((2 * SPAN, heads * VDIM), jnp.bfloat16),
            pltpu.VMEM(queries.shape, jnp.bfloat16),
            pltpu.VMEM(keys.shape, jnp.bfloat16),
            pltpu.VMEM((2 * keys.shape[0] // KEYS, KPAD, KEYS // 2), jnp.bfloat16),
            pltpu.VMEM(value_up.shape, jnp.bfloat16),
            pltpu.VMEM((ROWS, KEYS), f32),
            pltpu.VMEM((ROWS, KEYS), f32),
            pltpu.VMEM((ROWS, KEYS), jnp.bfloat16),
            pltpu.VMEM((ROWS, KEYS), jnp.bfloat16),
            pltpu.VMEM((units, ROWS, 128), f32),
            pltpu.VMEM((units, ROWS, 128), f32),
            pltpu.VMEM((ROWS, 128), f32),
            pltpu.VMEM((ROWS, 128), f32),
            pltpu.VMEM((units, ROWS, LATENT), f32),
            pltpu.SemaphoreType.DMA((4, 4)),
        ],
        compiler_params=pltpu.CompilerParams(vmem_limit_bytes=59 << 20),
        cost_estimate=pl.CostEstimate(
            flops=units * ROWS * keys.shape[0] * 640,
            bytes_accessed=8 << 20,
            transcendentals=units * ROWS * keys.shape[0] // 2,
        ),
    )(ctx, spans, queries, keys, value_up)


def project_kernel(ctx_ref, grp_ref, rows_hbm, w_hbm, other_w_hbm, after_ref, *refs):
    out_refs, (rows_ref, w_ref, sums, sems) = refs[:4], refs[4:]
    chunks = sems.shape[1]
    width = rows_ref.shape[1] // chunks
    parts = [(slice(None), slice(c * width, (c + 1) * width)) for c in range(chunks)]
    sides = ((rows_hbm, rows_ref), (w_hbm, w_ref.at[0]), (other_w_hbm, w_ref.at[1]))
    copies = [
        [
            pltpu.make_async_copy(source.at[part], target.at[part], sems.at[i, c])
            for i, (source, target) in enumerate(sides)
        ]
        for c, part in enumerate(parts)
    ]
    for three in copies:
        for copy in three:
            copy.start()
    z, head_z, head_core = ctx_ref[0] // 16, grp_ref[0] // 2, grp_ref[0] % 2
    for c, part in enumerate(parts):
        for copy in copies[c]:
            copy.wait()
        for side in range(2):
            product = lax.dot_general(
                rows_ref[part], w_ref[side, :, part[1]], NT, preferred_element_type=jnp.float32
            )
            sums[side] = product if c == 0 else sums[side] + product
    share = sums.shape[1] // 2
    for k, out_ref in enumerate(out_refs):
        to_z, to_core = (head_z + k // 2) % 2, (head_core + k) % 2
        side = jnp.where(to_z == z, 0, 1)
        rows = pl.ds(pl.multiple_of(to_core * share, share), share)
        out_ref[...] = sums[side, rows, :].astype(jnp.bfloat16)


def project(ctx, grp, rows, weights, other_weights, after):
    smem = pl.BlockSpec(memory_space=pltpu.SMEM)
    vmem = pl.BlockSpec(memory_space=pltpu.VMEM)
    hbm = pl.BlockSpec(memory_space=pltpu.HBM)
    width, depth = weights.shape
    row_count = rows.shape[0]
    return pl.pallas_call(
        project_kernel,
        out_shape=(jax.ShapeDtypeStruct((row_count // 2, width), jnp.bfloat16),) * 4,
        in_specs=[smem, smem, hbm, hbm, hbm, smem],
        out_specs=(vmem,) * 4,
        scratch_shapes=[
            pltpu.VMEM(rows.shape, jnp.bfloat16),
            pltpu.VMEM((2, width, depth), jnp.bfloat16),
            pltpu.VMEM((2, row_count, width), jnp.float32),
            pltpu.SemaphoreType.DMA((3, 4)),
        ],
        compiler_params=pltpu.CompilerParams(vmem_limit_bytes=32 << 20),
        cost_estimate=pl.CostEstimate(
            flops=4 * row_count * depth * 256, bytes_accessed=8 << 20, transcendentals=0
        ),
    )(ctx, grp, rows, weights, other_weights, after)


def share_out(k, part):
    pairs = []
    for ctx in range(lax.axis_size("ctx")):
        z, line = divmod(ctx, 16)
        for a in range(2):
            for b in range(2):
                to = ((a ^ k // 2) * 16 + line) * 4 + 2 * z + (b ^ k % 2)
                pairs.append((ctx * 4 + 2 * a + b, to))
    return lax.ppermute(part, ("ctx", "grp"), pairs)


def body(
    prefill_queries,
    latents,
    rope_keys,
    span_slots,
    decode_queries,
    new_latents,
    new_rope,
    context_lengths,
    page_table,
    value_up,
    out_proj,
):
    ctx = lax.axis_index("ctx").astype(jnp.int32).reshape(1)
    grp = lax.axis_index("grp").astype(jnp.int32).reshape(1)
    rows_local = page_table.shape[0]

    pieces = gather_caches(pack(latents, rope_keys))
    queries, row_queries, fresh = arrange(prefill_queries, decode_queries, new_latents, new_rope)
    keys, decode_values = decode(
        ctx, span_slots, page_table, context_lengths, row_queries, fresh, pieces, value_up
    )
    weights = out_proj.T
    other_weights = shift(weights, 1, 0, 0)
    all_values = exchange(decode_values).reshape(-1, decode_values.shape[2])
    prefill_values, prefill_done = prefill(ctx, span_slots, queries, keys, value_up)
    parts = project(ctx, grp, all_values, weights, other_weights, prefill_done)
    summed = sum(share_out(k, part).astype(jnp.float32) for k, part in enumerate(parts))
    decoded = summed.astype(jnp.bfloat16).reshape(-1, 2, rows_local, summed.shape[1])
    decoded = decoded.transpose(1, 0, 2, 3).reshape(2, -1, summed.shape[1])
    return (prefill_values, decoded)


def solution(mesh):
    placed = (
        P("ctx", "grp"),
        P("ctx", "grp"),
        P("ctx", None),
        P(),
        P(None, "ctx", "grp"),
        P(None, "ctx", "grp"),
        P(None, "ctx", None),
        P("ctx"),
        P("ctx", None),
        P("grp", None, None),
        P("grp", "ctx"),
    )
    return jax.shard_map(
        body,
        mesh=mesh,
        in_specs=placed,
        out_specs=(P("ctx", "grp"), P(None, "grp", "ctx")),
        check_vma=False,
    )
```

```python
import functools
import math

import jax
import jax.numpy as jnp
from jax import lax
from jax.experimental import pallas as pl
from jax.experimental.pallas import tpu as pltpu
from jax.sharding import PartitionSpec as P

SPAN = 64
LATENT = 256
ROPE = 64
KEYW = LATENT + ROPE
KPAD = 384
VDIM = 128

HEADS_TILE = 8
ROWS = HEADS_TILE * SPAN
KEYS = 512

EXP2_SCALE = 192.0 ** -0.5 * math.log2(math.e)
FAR_BELOW = -1e30
TOTAL_LIMIT = 2.0**100
NT = (((1,), (1,)), ((), ()))
RING = (0, -1, 1, 2)


def exchange(copies):
    size = lax.axis_size("ctx")
    groups = [list(range(z * size // 2, (z + 1) * size // 2)) for z in range(2)]
    return lax.all_to_all(
        copies, "ctx", split_axis=0, concat_axis=0, axis_index_groups=groups, tiled=True
    )


def shift(value, dz, dx, dy):
    pairs = []
    for ctx in range(lax.axis_size("ctx")):
        z, x, y = ctx // 16, ctx // 4 % 4, ctx % 4
        pairs.append((ctx, (z + dz) % 2 * 16 + (x + dx) % 4 * 4 + (y + dy) % 4))
    return lax.ppermute(value, "ctx", pairs)


def along(axis, steps):
    return (0, steps, 0) if axis == "x" else (0, 0, steps)


def gather_caches(own):
    other = shift(own, 1, 0, 0)
    axes = ("yx", "xy")
    held = [jnp.stack([own[half], other[half]]) for half in range(2)]
    for half in range(2):
        ring = [shift(held[half], *along(axes[half][0], -off)) for off in RING[1:]]
        held[half] = jnp.concatenate([held[half]] + ring)
    near = [
        [shift(held[half], *along(axes[half][1], -off)) for off in RING[1:3]] for half in range(2)
    ]
    cut = held[0].shape[0] // 2
    pieces = []
    for half in range(2):
        after, before = near[half]
        far_first = shift(after[:cut], *along(axes[half][1], 1))
        far_second = shift(before[cut:], *along(axes[half][1], -1))
        pieces += [held[half], after, before, far_first, far_second]
    return pieces


def block_offsets(half):
    places = []
    for last in RING:
        for first in RING:
            for dz in range(2):
                places.append((dz, last, first) if half == 0 else (dz, first, last))
    return places


def pack_kernel(latents_ref, rope_ref, out_ref):
    rope = rope_ref[...].astype(jnp.float32).T
    for span in range(2):
        rows = slice(span * SPAN, (span + 1) * SPAN)
        out_ref[span, :SPAN, :] = latents_ref[rows, :]
        parts = [rope[span * SPAN + c * 16 : span * SPAN + (c + 1) * 16] for c in range(4)]
        out_ref[span, SPAN:, :] = jnp.concatenate(parts, axis=1).astype(jnp.bfloat16)


def pack(latents, rope_keys):
    return pl.pallas_call(
        pack_kernel,
        out_shape=jax.ShapeDtypeStruct((2, SPAN + SPAN // 4, LATENT), jnp.bfloat16),
    )(latents, rope_keys.T)


def copies_in_parts(source, target, sems, axis=0):
    parts = sems.shape[0]
    size = source.shape[axis] // parts
    where = [(slice(None),) * axis + (slice(i * size, (i + 1) * size),) for i in range(parts)]
    return [
        pltpu.make_async_copy(source.at[at], target.at[at], sems.at[i])
        for i, at in enumerate(where)
    ]


def start(copies):
    for copy in copies:
        copy.start()


def wait(copies):
    for copy in copies:
        copy.wait()


def repeat_to(source, target, sems):
    size = source.shape[0]
    return [
        pltpu.make_async_copy(source, target.at[i * size : (i + 1) * size], sems.at[i])
        for i in range(target.shape[0] // size)
    ]


def unpack(block, keys_ref, place):
    rows = pl.ds(pl.multiple_of(place * SPAN, SPAN), SPAN)
    keys_ref[rows, :LATENT] = block[:SPAN, :]
    packed = block[SPAN:, :].astype(jnp.float32)
    low_lanes = lax.broadcasted_iota(jnp.int32, (16, 128), 1) < ROPE
    parts = []
    for c in range(2):
        two = packed[:, c * 128 : (c + 1) * 128]
        parts.append(jnp.where(low_lanes, two, 0.0))
        parts.append(jnp.where(low_lanes, pltpu.roll(two, 64, 1), 0.0))
    keys_ref[rows, LATENT:] = jnp.concatenate(parts, axis=0).astype(jnp.bfloat16)


def decode_kernel(ctx_ref, spans_ref, pages_ref, lengths_ref, *refs):
    q_ref, fresh_ref, *piece_refs, up_hbm, keys_hbm, values_hbm = refs[:15]
    up_ref, keys_ref, cache, att, values, sems = refs[15:]
    up_copies = copies_in_parts(up_hbm, up_ref, sems.at[0])
    start(up_copies)
    rows_local, pages = pages_ref.shape
    slots = pages * SPAN
    width = cache.shape[1]
    z, x, y = ctx_ref[0] // 16, ctx_ref[0] // 4 % 4, ctx_ref[0] % 4
    for half in range(2):
        blocks = [ref.at[i] for ref in piece_refs[5 * half : 5 * half + 5] for i in range(ref.shape[0])]
        for block, (dz, dx, dy) in zip(blocks, block_offsets(half)):
            source = (z + dz) % 2 * 16 + (x + dx + 4) % 4 * 4 + (y + dy + 4) % 4
            unpack(block, keys_ref, spans_ref[2 * source + half])
    keys_copies = copies_in_parts(keys_ref, keys_hbm, sems.at[1])
    start(keys_copies)
    for b in range(rows_local):
        cache[b, slots : slots + 16, :] = fresh_ref[b]
        cache[b, slots + 16 :, :] = jnp.zeros((width - slots - 16, KPAD), jnp.bfloat16)

    cols = lax.broadcasted_iota(jnp.int32, (64, width), 1)
    step = lax.broadcasted_iota(jnp.int32, (64, width), 0) // 32
    fresh_seen = (cols >= slots) & (cols - slots <= step)
    for b in range(rows_local):
        for j in range(pages):
            page = pages_ref[b, j]
            cache[b, j * SPAN : (j + 1) * SPAN, :] = keys_ref[
                pl.ds(pl.multiple_of(page * SPAN, SPAN), SPAN), :
            ]
        scores = lax.dot_general(q_ref[b], cache[b], NT, preferred_element_type=jnp.float32)
        seen = (cols < lengths_ref[b]) | fresh_seen
        scores = jnp.where(seen, scores, FAR_BELOW)
        top = jnp.max(scores, axis=1, keepdims=True)
        weights = jnp.exp2(scores * EXP2_SCALE - top * EXP2_SCALE)
        total = jnp.sum(weights, axis=1, keepdims=True)
        attended = jnp.dot(
            weights.astype(jnp.bfloat16), cache[b, :, :LATENT], preferred_element_type=jnp.float32
        )
        attended = attended / total
        for s in range(2):
            for c in range(2):
                att[c, pl.ds(s * rows_local + b, 32, stride=16), :] = attended[
                    s * 32 : (s + 1) * 32, c * 128 : (c + 1) * 128
                ]
    wait(up_copies)
    for h in range(32):
        mine = slice(h * 16, (h + 1) * 16)
        attended = jnp.concatenate([att[0, mine, :], att[1, mine, :]], axis=1)
        head_values = jnp.dot(
            attended.astype(jnp.bfloat16), up_ref[h], preferred_element_type=jnp.float32
        ).astype(jnp.bfloat16)
        for i in range(values.shape[0]):
            values[i, :, h * VDIM : (h + 1) * VDIM] = head_values
    values_copies = repeat_to(values, values_hbm, sems.at[2])
    start(values_copies)
    wait(values_copies)
    wait(keys_copies)


def decode(ctx, spans, pages, lengths, queries, fresh, pieces, value_up):
    smem = pl.BlockSpec(memory_space=pltpu.SMEM)
    vmem = pl.BlockSpec(memory_space=pltpu.VMEM)
    hbm = pl.BlockSpec(memory_space=pltpu.HBM)
    rows_local = pages.shape[0]
    heads = value_up.shape[0]
    key_rows = spans.shape[0] * SPAN
    return pl.pallas_call(
        decode_kernel,
        out_shape=(
            jax.ShapeDtypeStruct((key_rows, KPAD), jnp.bfloat16),
            jax.ShapeDtypeStruct((16, 2 * rows_local, heads * VDIM), jnp.bfloat16),
        ),
        in_specs=[smem] * 4 + [vmem] * 12 + [hbm],
        out_specs=(hbm, hbm),
        scratch_shapes=[
            pltpu.VMEM(value_up.shape, jnp.bfloat16),
            pltpu.VMEM((key_rows, KPAD), jnp.bfloat16),
            pltpu.VMEM((rows_local, pages.shape[1] * SPAN + 128, KPAD), jnp.bfloat16),
            pltpu.VMEM((2, 16 * heads, 128), jnp.float32),
            pltpu.VMEM((4, 2 * rows_local, heads * VDIM), jnp.bfloat16),
            pltpu.SemaphoreType.DMA((3, 4)),
        ],
        compiler_params=pltpu.CompilerParams(vmem_limit_bytes=57 << 20),
        cost_estimate=pl.CostEstimate(
            flops=2 * 8 * 64 * 1152 * 640, bytes_accessed=12 << 20, transcendentals=8 * 64 * 1152
        ),
    )(ctx, spans, pages, lengths, queries, fresh, *pieces, value_up)


def arrange_kernel(q_ref, dq_ref, new_latents_ref, new_rope_ref, *refs):
    out_ref, decode_out_ref, fresh_out_ref, decode_rows, fresh = refs
    for pair in range(HEADS_TILE // 2):
        at = pair * 2 * KEYW
        for s in range(2):
            tokens = slice(s * SPAN, (s + 1) * SPAN)
            out_ref[s, 2 * pair * SPAN : (2 * pair + 1) * SPAN, :] = q_ref[tokens, at : at + KPAD]
            odd = q_ref[tokens, at + 256 : at + 640].astype(jnp.float32)
            out_ref[s, (2 * pair + 1) * SPAN : (2 * pair + 2) * SPAN, :] = pltpu.roll(
                odd, KPAD - 64, 1
            ).astype(jnp.bfloat16)

    @pl.when(pl.program_id(0) == 0)
    def _():
        rows_local = dq_ref.shape[1]
        fresh[...] = jnp.zeros_like(fresh)
        for s in range(2):
            for h in range(32):
                at = h // 2 * 2 * KEYW + h % 2 * 256
                rows = dq_ref[s, :, at : at + KPAD].astype(jnp.float32)
                if h % 2:
                    rows = pltpu.roll(rows, KPAD - 64, 1)
                for c in range(3):
                    decode_rows[c, pl.ds(s * 32 + h, rows_local, stride=64), :] = rows[
                        :, c * 128 : (c + 1) * 128
                    ]
            mine = pl.ds(s, rows_local, stride=16)
            latent_rows = new_latents_ref[s].astype(jnp.float32)
            fresh[0, mine, :] = latent_rows[:, :128]
            fresh[1, mine, :] = latent_rows[:, 128:]
            rope_rows = new_rope_ref[s].astype(jnp.float32)
            fresh[2, mine, :] = jnp.concatenate([rope_rows, jnp.zeros_like(rope_rows)], axis=1)
        for b in range(rows_local):
            for rows_ref, out, size in ((decode_rows, decode_out_ref, 64), (fresh, fresh_out_ref, 16)):
                rows = slice(b * size, (b + 1) * size)
                parts = [rows_ref[c, rows, :] for c in range(3)]
                out[b] = jnp.concatenate(parts, axis=1).astype(jnp.bfloat16)


def arrange(queries, decode_queries, latents, rope):
    vmem = pl.BlockSpec(memory_space=pltpu.VMEM)
    rows_local = decode_queries.shape[1]
    tiles = queries.shape[1] // (HEADS_TILE * KEYW)
    bf16 = jnp.bfloat16
    whole = [(rows_local, 64, KPAD), (rows_local, 16, KPAD)]
    return pl.pallas_call(
        arrange_kernel,
        grid=(tiles,),
        out_shape=[jax.ShapeDtypeStruct((2 * tiles, ROWS, KPAD), bf16)]
        + [jax.ShapeDtypeStruct(shape, bf16) for shape in whole],
        in_specs=[pl.BlockSpec((2 * SPAN, HEADS_TILE * KEYW), lambda i: (0, i))] + [vmem] * 3,
        out_specs=[pl.BlockSpec((2, ROWS, KPAD), lambda i: (i, 0, 0))]
        + [pl.BlockSpec(shape, lambda i: (0, 0, 0)) for shape in whole],
        scratch_shapes=[
            pltpu.VMEM((3, 64 * rows_local, 128), jnp.float32),
            pltpu.VMEM((3, 16 * rows_local, 128), jnp.float32),
        ],
        compiler_params=pltpu.CompilerParams(vmem_limit_bytes=16 << 20),
        cost_estimate=pl.CostEstimate(flops=0, bytes_accessed=12 << 20, transcendentals=0),
    )(queries, decode_queries, latents, rope)


def clear(top, total, acc, p_b, r_b):
    top[...] = jnp.full(top.shape, FAR_BELOW, jnp.float32)
    total[...] = jnp.zeros_like(total)
    acc[...] = jnp.zeros_like(acc)
    p_b[...] = jnp.zeros_like(p_b)
    r_b[...] = jnp.ones_like(r_b)


def prefill_kernel(ctx_ref, spans_ref, qs_hbm, k_hbm, up_hbm, out_hbm, done_ref, *scratch):
    out_ref, qs, k_ref, kt_ref, up_ref, s_a, s_b, p_a, p_b, top, total, r_a, r_b, acc, sems = scratch
    tiles = acc.shape[0] // 2
    k_copies = copies_in_parts(k_hbm, k_ref, sems.at[0])
    q_copies = copies_in_parts(qs_hbm, qs, sems.at[1])
    up_copies = copies_in_parts(up_hbm, up_ref, sems.at[2])
    start(k_copies + q_copies)
    clear(top, total, acc, p_b, r_b)
    pieces = kt_ref.shape[0]
    for n in range(pieces):
        if n % (pieces // len(k_copies)) == 0:
            k_copies[n // (pieces // len(k_copies))].wait()
        kt_ref[n] = k_ref[n * KEYS // 2 : (n + 1) * KEYS // 2, :].T
    span_of = [spans_ref[2 * ctx_ref[0] + s] for s in range(2)]
    blocks_of = [span // (KEYS // SPAN) for span in span_of]
    offset_of = [(span_of[s] - blocks_of[s] * (KEYS // SPAN)) * SPAN for s in range(2)]
    wait(q_copies)
    start(up_copies)

    def key_rows(block):
        return pl.ds(pl.multiple_of(block * KEYS, KEYS), KEYS)

    def score_part(unit, block, s_ref, part):
        cols = slice(part * KEYS // 2, (part + 1) * KEYS // 2)
        s_ref[:, cols] = jnp.dot(
            qs[unit], kt_ref[2 * block + part], preferred_element_type=jnp.float32
        )

    lead = lax.broadcasted_iota(jnp.int32, (SPAN, 128), 1)
    lead = lead - lax.broadcasted_iota(jnp.int32, (SPAN, 128), 0)

    def weigh_part(unit, s_ref, p_ref, r_ref, offset, part):
        for h in range(part * HEADS_TILE // 4, (part + 1) * HEADS_TILE // 4):
            rows = slice(h * SPAN, (h + 1) * SPAN)
            parts = [s_ref[rows, c * 128 : (c + 1) * 128] for c in range(KEYS // 128)]
            parts = [
                jnp.where(lead <= offset - c * 128, part, FAR_BELOW)
                for c, part in enumerate(parts)
            ]
            highest = functools.reduce(jnp.maximum, parts)
            old = top[unit, rows]
            new = jnp.maximum(old, jnp.max(highest, axis=1, keepdims=True))
            top[unit, rows] = new
            scaled = new * EXP2_SCALE
            rescale = jnp.exp2(old * EXP2_SCALE - scaled)
            r_ref[rows] = rescale
            weights = [jnp.exp2(part * EXP2_SCALE - scaled) for part in parts]
            total[unit, rows] = total[unit, rows] * rescale + sum(weights)
            for c, weight in enumerate(weights):
                p_ref[rows, c * 128 : (c + 1) * 128] = weight.astype(jnp.bfloat16)

    def add_part(unit, block, p_ref, r_ref, part):
        rows = slice(part * ROWS // 2, (part + 1) * ROWS // 2)
        product = jnp.dot(
            p_ref[rows, :], k_ref[key_rows(block), :LATENT], preferred_element_type=jnp.float32
        )
        r = r_ref[rows]
        acc[unit, rows, :128] = acc[unit, rows, :128] * r + product[:, :128]
        acc[unit, rows, 128:] = acc[unit, rows, 128:] * r + product[:, 128:]

    def step(later, here, before, s_later, s_here, p_here, r_here, p_before, r_before, offset):
        score_part(*later, s_later, 0)
        weigh_part(here[0], s_here, p_here, r_here, offset, 0)
        score_part(*later, s_later, 1)
        weigh_part(here[0], s_here, p_here, r_here, offset, 1)
        add_part(*before, p_before, r_before, 0)
        weigh_part(here[0], s_here, p_here, r_here, offset, 2)
        add_part(*before, p_before, r_before, 1)
        weigh_part(here[0], s_here, p_here, r_here, offset, 3)

    def last_block(unit):
        return jnp.where(unit % 2 == 0, blocks_of[0], blocks_of[1])

    def following(item):
        unit, block = item
        ends = block == last_block(unit)
        unit = jnp.minimum(jnp.where(ends, unit + 1, unit), 2 * tiles - 1)
        return unit, jnp.where(ends, 0, block + 1)

    def offset(item):
        unit, block = item
        own = jnp.where(unit % 2 == 0, offset_of[0], offset_of[1])
        return jnp.where(block == last_block(unit), own, KEYS)

    def two_items(i, carry):
        before, here = carry[:2], carry[2:]
        after = following(here)
        step(after, here, before, s_b, s_a, p_a, r_a, p_b, r_b, offset(here))
        later = following(after)
        step(later, after, here, s_a, s_b, p_b, r_b, p_a, r_a, offset(after))
        return after + later

    def first_weigh_part(item, s_ref, p_ref, part):
        unit, limit = item[0], offset(item)
        for h in range(part * HEADS_TILE // 4, (part + 1) * HEADS_TILE // 4):
            rows = slice(h * SPAN, (h + 1) * SPAN)
            parts = [
                jnp.where(
                    lead <= limit - c * 128, s_ref[rows, c * 128 : (c + 1) * 128], FAR_BELOW
                )
                for c in range(KEYS // 128)
            ]
            highest = jnp.max(functools.reduce(jnp.maximum, parts), axis=1, keepdims=True)
            top[unit, rows] = jnp.broadcast_to(highest * EXP2_SCALE, (SPAN, 128))
            keep_weights(unit, rows, parts, p_ref)

    def next_weigh_part(item, s_ref, p_ref, part):
        for h in range(part * HEADS_TILE // 4, (part + 1) * HEADS_TILE // 4):
            rows = slice(h * SPAN, (h + 1) * SPAN)
            parts = [s_ref[rows, c * 128 : (c + 1) * 128] for c in range(KEYS // 128)]
            keep_weights(item[0], rows, parts, p_ref)

    def keep_weights(unit, rows, parts, p_ref):
        shift = top[unit, rows]
        weights = [jnp.exp2(part * EXP2_SCALE - shift) for part in parts]
        total[unit, rows] = total[unit, rows] + sum(weights)
        for c, weight in enumerate(weights):
            p_ref[rows, c * 128 : (c + 1) * 128] = weight.astype(jnp.bfloat16)

    def plain_add_part(unit, block, p_ref, part):
        rows = slice(part * ROWS // 2, (part + 1) * ROWS // 2)
        acc[unit, rows, :] = acc[unit, rows, :] + jnp.dot(
            p_ref[rows, :], k_ref[key_rows(block), :LATENT], preferred_element_type=jnp.float32
        )

    def plain_step(weigh, later, here, before, s_later, s_here, p_here, p_before):
        score_part(*later, s_later, 0)
        weigh(here, s_here, p_here, 0)
        score_part(*later, s_later, 1)
        weigh(here, s_here, p_here, 1)
        plain_add_part(*before, p_before, 0)
        weigh(here, s_here, p_here, 2)
        plain_add_part(*before, p_before, 1)
        weigh(here, s_here, p_here, 3)

    def own_item(unit):
        return unit, last_block(unit)

    def following_whole(item):
        unit, block = item
        ends = block + 1 >= last_block(unit)
        skips = jnp.where(last_block(1 - unit % 2) == 0, 2, 1)
        unit = jnp.where(ends, unit + skips, unit)
        block = jnp.where(ends, 0, block + 1)
        over = unit >= 2 * tiles
        unit = jnp.where(over, 2 * tiles - 1, unit)
        return unit, jnp.where(over, last_block(unit), block)

    whole_blocks = blocks_of[0] + blocks_of[1]
    first_whole = jnp.where(blocks_of[0] == 0, 1, 0), jnp.int32(0)

    def two_own(i, before):
        even, odd = own_item(2 * i), own_item(2 * i + 1)
        plain_step(first_weigh_part, odd, even, before, s_b, s_a, p_a, p_b)
        later = own_item(jnp.minimum(2 * i + 2, 2 * tiles - 1))
        ends = (i == tiles - 1) & (whole_blocks > 0)
        later = tuple(jnp.where(ends, w, o) for w, o in zip(first_whole, later))
        plain_step(first_weigh_part, later, odd, even, s_a, s_b, p_b, p_a)
        return odd

    def two_whole(i, carry):
        before, here = carry[:2], carry[2:]
        after = following_whole(here)
        plain_step(next_weigh_part, after, here, before, s_b, s_a, p_a, p_b)
        later = following_whole(after)
        plain_step(next_weigh_part, later, after, here, s_a, s_b, p_b, p_a)
        return after + later

    for part in range(2):
        score_part(*own_item(0), s_a, part)
    before = lax.fori_loop(0, tiles, two_own, (jnp.int32(0), jnp.int32(0)))
    before = lax.fori_loop(0, whole_blocks * (tiles // 2), two_whole, before + first_whole)[:2]
    for part in range(2):
        plain_add_part(*before, p_b, part)

    @pl.when(jnp.logical_not(jnp.max(total[...]) < TOTAL_LIMIT))
    def _():
        clear(top, total, acc, p_b, r_b)
        for part in range(2):
            score_part(0, 0, s_a, part)
        rounds = (whole_blocks + 2) * (tiles // 2)
        before = lax.fori_loop(0, rounds, two_items, (jnp.int32(0),) * 4)[:2]
        for part in range(2):
            add_part(*before, p_b, r_b, part)

    wait(up_copies)

    def out_copy(tile):
        width = HEADS_TILE * VDIM
        columns = pl.ds(pl.multiple_of(tile * width, width), width)
        return pltpu.make_async_copy(
            out_ref.at[:, columns], out_hbm.at[:, columns], sems.at[3, tile]
        )

    def finish(tile, carry):
        attended = []
        for s in range(2):
            unit = 2 * tile + s
            share = 1.0 / jnp.sum(total[unit], axis=1, keepdims=True)
            attended.append((acc[unit] * share).astype(jnp.bfloat16))
        values = []
        for h in range(HEADS_TILE):
            rows = slice(h * SPAN, (h + 1) * SPAN)
            both = jnp.concatenate([attended[0][rows], attended[1][rows]], axis=0)
            values.append(
                jnp.dot(
                    both, up_ref[tile * HEADS_TILE + h], preferred_element_type=jnp.float32
                ).astype(jnp.bfloat16)
            )
        columns = HEADS_TILE * VDIM
        out_ref[:, pl.ds(pl.multiple_of(tile * columns, columns), columns)] = jnp.concatenate(
            values, axis=1
        )
        out_copy(tile).start()
        return carry

    lax.fori_loop(0, tiles, finish, 0)
    for tile in range(tiles):
        out_copy(tile).wait()
    done_ref[0] = 0


def prefill(ctx, spans, queries, keys, value_up):
    units = queries.shape[0]
    heads = value_up.shape[0]
    f32 = jnp.float32
    smem = pl.BlockSpec(memory_space=pltpu.SMEM)
    hbm = pl.BlockSpec(memory_space=pltpu.HBM)
    return pl.pallas_call(
        prefill_kernel,
        out_shape=(
            jax.ShapeDtypeStruct((2 * SPAN, heads * VDIM), jnp.bfloat16),
            jax.ShapeDtypeStruct((1,), jnp.int32),
        ),
        in_specs=[smem] * 2 + [hbm] * 3,
        out_specs=(hbm, smem),
        scratch_shapes=[
            pltpu.VMEM((2 * SPAN, heads * VDIM), jnp.bfloat16),
            pltpu.VMEM(queries.shape, jnp.bfloat16),
            pltpu.VMEM(keys.shape, jnp.bfloat16),
            pltpu.VMEM((2 * keys.shape[0] // KEYS, KPAD, KEYS // 2), jnp.bfloat16),
            pltpu.VMEM(value_up.shape, jnp.bfloat16),
            pltpu.VMEM((ROWS, KEYS), f32),
            pltpu.VMEM((ROWS, KEYS), f32),
            pltpu.VMEM((ROWS, KEYS), jnp.bfloat16),
            pltpu.VMEM((ROWS, KEYS), jnp.bfloat16),
            pltpu.VMEM((units, ROWS, 128), f32),
            pltpu.VMEM((units, ROWS, 128), f32),
            pltpu.VMEM((ROWS, 128), f32),
            pltpu.VMEM((ROWS, 128), f32),
            pltpu.VMEM((units, ROWS, LATENT), f32),
            pltpu.SemaphoreType.DMA((4, 4)),
        ],
        compiler_params=pltpu.CompilerParams(vmem_limit_bytes=59 << 20),
        cost_estimate=pl.CostEstimate(
            flops=units * ROWS * keys.shape[0] * 640,
            bytes_accessed=8 << 20,
            transcendentals=units * ROWS * keys.shape[0] // 2,
        ),
    )(ctx, spans, queries, keys, value_up)


def project_kernel(ctx_ref, grp_ref, rows_hbm, w_hbm, other_w_hbm, after_ref, *refs):
    out_refs, (rows_ref, w_ref, sums, sems) = refs[:4], refs[4:]
    chunks = sems.shape[1]
    width = rows_ref.shape[1] // chunks
    parts = [(slice(None), slice(c * width, (c + 1) * width)) for c in range(chunks)]
    sides = ((rows_hbm, rows_ref), (w_hbm, w_ref.at[0]), (other_w_hbm, w_ref.at[1]))
    copies = [
        [
            pltpu.make_async_copy(source.at[part], target.at[part], sems.at[i, c])
            for i, (source, target) in enumerate(sides)
        ]
        for c, part in enumerate(parts)
    ]
    for three in copies:
        for copy in three:
            copy.start()
    z, head_z, head_core = ctx_ref[0] // 16, grp_ref[0] // 2, grp_ref[0] % 2
    for c, part in enumerate(parts):
        for copy in copies[c]:
            copy.wait()
        for side in range(2):
            product = lax.dot_general(
                rows_ref[part], w_ref[side, :, part[1]], NT, preferred_element_type=jnp.float32
            )
            sums[side] = product if c == 0 else sums[side] + product
    share = sums.shape[1] // 2
    for k, out_ref in enumerate(out_refs):
        to_z, to_core = (head_z + k // 2) % 2, (head_core + k) % 2
        side = jnp.where(to_z == z, 0, 1)
        rows = pl.ds(pl.multiple_of(to_core * share, share), share)
        out_ref[...] = sums[side, rows, :].astype(jnp.bfloat16)


def project(ctx, grp, rows, weights, other_weights, after):
    smem = pl.BlockSpec(memory_space=pltpu.SMEM)
    vmem = pl.BlockSpec(memory_space=pltpu.VMEM)
    hbm = pl.BlockSpec(memory_space=pltpu.HBM)
    width, depth = weights.shape
    row_count = rows.shape[0]
    return pl.pallas_call(
        project_kernel,
        out_shape=(jax.ShapeDtypeStruct((row_count // 2, width), jnp.bfloat16),) * 4,
        in_specs=[smem, smem, hbm, hbm, hbm, smem],
        out_specs=(vmem,) * 4,
        scratch_shapes=[
            pltpu.VMEM(rows.shape, jnp.bfloat16),
            pltpu.VMEM((2, width, depth), jnp.bfloat16),
            pltpu.VMEM((2, row_count, width), jnp.float32),
            pltpu.SemaphoreType.DMA((3, 4)),
        ],
        compiler_params=pltpu.CompilerParams(vmem_limit_bytes=32 << 20),
        cost_estimate=pl.CostEstimate(
            flops=4 * row_count * depth * 256, bytes_accessed=8 << 20, transcendentals=0
        ),
    )(ctx, grp, rows, weights, other_weights, after)


def share_out(k, part):
    pairs = []
    for ctx in range(lax.axis_size("ctx")):
        z, line = divmod(ctx, 16)
        for a in range(2):
            for b in range(2):
                to = ((a ^ k // 2) * 16 + line) * 4 + 2 * z + (b ^ k % 2)
                pairs.append((ctx * 4 + 2 * a + b, to))
    return lax.ppermute(part, ("ctx", "grp"), pairs)


def body(
    prefill_queries,
    latents,
    rope_keys,
    span_slots,
    decode_queries,
    new_latents,
    new_rope,
    context_lengths,
    page_table,
    value_up,
    out_proj,
):
    ctx = lax.axis_index("ctx").astype(jnp.int32).reshape(1)
    grp = lax.axis_index("grp").astype(jnp.int32).reshape(1)
    rows_local = page_table.shape[0]

    pieces = gather_caches(pack(latents, rope_keys))
    queries, row_queries, fresh = arrange(prefill_queries, decode_queries, new_latents, new_rope)
    keys, decode_values = decode(
        ctx, span_slots, page_table, context_lengths, row_queries, fresh, pieces, value_up
    )
    weights = out_proj.T
    other_weights = shift(weights, 1, 0, 0)
    all_values = exchange(decode_values).reshape(-1, decode_values.shape[2])
    prefill_values, prefill_done = prefill(ctx, span_slots, queries, keys, value_up)
    parts = project(ctx, grp, all_values, weights, other_weights, prefill_done)
    summed = sum(share_out(k, part).astype(jnp.float32) for k, part in enumerate(parts))
    decoded = summed.astype(jnp.bfloat16).reshape(-1, 2, rows_local, summed.shape[1])
    decoded = decoded.transpose(1, 0, 2, 3).reshape(2, -1, summed.shape[1])
    return (prefill_values, decoded)


def solution(mesh):
    placed = (
        P("ctx", "grp"),
        P("ctx", "grp"),
        P("ctx", None),
        P(),
        P(None, "ctx", "grp"),
        P(None, "ctx", "grp"),
        P(None, "ctx", None),
        P("ctx"),
        P("ctx", None),
        P("grp", None, None),
        P("grp", "ctx"),
    )
    return jax.shard_map(
        body,
        mesh=mesh,
        in_specs=placed,
        out_specs=(P("ctx", "grp"), P(None, "grp", "ctx")),
        check_vma=False,
    )
```

```python
import functools
import math

import jax
import jax.numpy as jnp
from jax import lax
from jax.experimental import pallas as pl
from jax.experimental.pallas import tpu as pltpu
from jax.sharding import PartitionSpec as P

SPAN = 64
LATENT = 256
ROPE = 64
KEYW = LATENT + ROPE
KPAD = 384
VDIM = 128

HEADS_TILE = 8
ROWS = HEADS_TILE * SPAN
KEYS = 512

EXP2_SCALE = 192.0 ** -0.5 * math.log2(math.e)
FAR_BELOW = -1e30
TOTAL_LIMIT = 2.0**100
NT = (((1,), (1,)), ((), ()))
RING = (0, -1, 1, 2)


def exchange(copies):
    size = lax.axis_size("ctx")
    groups = [list(range(z * size // 2, (z + 1) * size // 2)) for z in range(2)]
    return lax.all_to_all(
        copies, "ctx", split_axis=0, concat_axis=0, axis_index_groups=groups, tiled=True
    )


def shift(value, dz, dx, dy):
    pairs = []
    for ctx in range(lax.axis_size("ctx")):
        z, x, y = ctx // 16, ctx // 4 % 4, ctx % 4
        pairs.append((ctx, (z + dz) % 2 * 16 + (x + dx) % 4 * 4 + (y + dy) % 4))
    return lax.ppermute(value, "ctx", pairs)


def along(axis, steps):
    return (0, steps, 0) if axis == "x" else (0, 0, steps)


def gather_caches(own):
    other = shift(own, 1, 0, 0)
    axes = ("yx", "xy")
    held = [jnp.stack([own[half], other[half]]) for half in range(2)]
    for half in range(2):
        ring = [shift(held[half], *along(axes[half][0], -off)) for off in RING[1:]]
        held[half] = jnp.concatenate([held[half]] + ring)
    near = [
        [shift(held[half], *along(axes[half][1], -off)) for off in RING[1:3]] for half in range(2)
    ]
    cut = held[0].shape[0] // 2
    pieces = []
    for half in range(2):
        after, before = near[half]
        far_first = shift(after[:cut], *along(axes[half][1], 1))
        far_second = shift(before[cut:], *along(axes[half][1], -1))
        pieces += [held[half], after, before, far_first, far_second]
    return pieces


def block_offsets(half):
    places = []
    for last in RING:
        for first in RING:
            for dz in range(2):
                places.append((dz, last, first) if half == 0 else (dz, first, last))
    return places


def pack_kernel(latents_ref, rope_ref, out_ref):
    rope = rope_ref[...].astype(jnp.float32).T
    for span in range(2):
        rows = slice(span * SPAN, (span + 1) * SPAN)
        out_ref[span, :SPAN, :] = latents_ref[rows, :]
        parts = [rope[span * SPAN + c * 16 : span * SPAN + (c + 1) * 16] for c in range(4)]
        out_ref[span, SPAN:, :] = jnp.concatenate(parts, axis=1).astype(jnp.bfloat16)


def pack(latents, rope_keys):
    return pl.pallas_call(
        pack_kernel,
        out_shape=jax.ShapeDtypeStruct((2, SPAN + SPAN // 4, LATENT), jnp.bfloat16),
    )(latents, rope_keys.T)


def copies_in_parts(source, target, sems, axis=0):
    parts = sems.shape[0]
    size = source.shape[axis] // parts
    where = [(slice(None),) * axis + (slice(i * size, (i + 1) * size),) for i in range(parts)]
    return [
        pltpu.make_async_copy(source.at[at], target.at[at], sems.at[i])
        for i, at in enumerate(where)
    ]


def start(copies):
    for copy in copies:
        copy.start()


def wait(copies):
    for copy in copies:
        copy.wait()


def repeat_to(source, target, sems):
    size = source.shape[0]
    return [
        pltpu.make_async_copy(source, target.at[i * size : (i + 1) * size], sems.at[i])
        for i in range(target.shape[0] // size)
    ]


def unpack(block, keys_ref, place):
    rows = pl.ds(pl.multiple_of(place * SPAN, SPAN), SPAN)
    keys_ref[rows, :LATENT] = block[:SPAN, :]
    packed = block[SPAN:, :].astype(jnp.float32)
    low_lanes = lax.broadcasted_iota(jnp.int32, (16, 128), 1) < ROPE
    parts = []
    for c in range(2):
        two = packed[:, c * 128 : (c + 1) * 128]
        parts.append(jnp.where(low_lanes, two, 0.0))
        parts.append(jnp.where(low_lanes, pltpu.roll(two, 64, 1), 0.0))
    keys_ref[rows, LATENT:] = jnp.concatenate(parts, axis=0).astype(jnp.bfloat16)


def decode_kernel(ctx_ref, spans_ref, pages_ref, lengths_ref, *refs):
    q_ref, fresh_ref, *piece_refs, up_hbm, keys_hbm, values_hbm = refs[:15]
    up_ref, keys_ref, cache, att, values, sems = refs[15:]
    up_copies = copies_in_parts(up_hbm, up_ref, sems.at[0])
    start(up_copies)
    rows_local, pages = pages_ref.shape
    slots = pages * SPAN
    width = cache.shape[1]
    z, x, y = ctx_ref[0] // 16, ctx_ref[0] // 4 % 4, ctx_ref[0] % 4
    for half in range(2):
        blocks = [ref.at[i] for ref in piece_refs[5 * half : 5 * half + 5] for i in range(ref.shape[0])]
        for block, (dz, dx, dy) in zip(blocks, block_offsets(half)):
            source = (z + dz) % 2 * 16 + (x + dx + 4) % 4 * 4 + (y + dy + 4) % 4
            unpack(block, keys_ref, spans_ref[2 * source + half])
    keys_copies = copies_in_parts(keys_ref, keys_hbm, sems.at[1])
    start(keys_copies)
    for b in range(rows_local):
        cache[b, slots : slots + 16, :] = fresh_ref[b]
        cache[b, slots + 16 :, :] = jnp.zeros((width - slots - 16, KPAD), jnp.bfloat16)

    cols = lax.broadcasted_iota(jnp.int32, (64, width), 1)
    step = lax.broadcasted_iota(jnp.int32, (64, width), 0) // 32
    fresh_seen = (cols >= slots) & (cols - slots <= step)
    for b in range(rows_local):
        for j in range(pages):
            page = pages_ref[b, j]
            cache[b, j * SPAN : (j + 1) * SPAN, :] = keys_ref[
                pl.ds(pl.multiple_of(page * SPAN, SPAN), SPAN), :
            ]
        scores = lax.dot_general(q_ref[b], cache[b], NT, preferred_element_type=jnp.float32)
        seen = (cols < lengths_ref[b]) | fresh_seen
        scores = jnp.where(seen, scores, FAR_BELOW)
        top = jnp.max(scores, axis=1, keepdims=True)
        weights = jnp.exp2(scores * EXP2_SCALE - top * EXP2_SCALE)
        total = jnp.sum(weights, axis=1, keepdims=True)
        attended = jnp.dot(
            weights.astype(jnp.bfloat16), cache[b, :, :LATENT], preferred_element_type=jnp.float32
        )
        attended = attended / total
        for s in range(2):
            for c in range(2):
                att[c, pl.ds(s * rows_local + b, 32, stride=16), :] = attended[
                    s * 32 : (s + 1) * 32, c * 128 : (c + 1) * 128
                ]
    wait(up_copies)
    for h in range(32):
        mine = slice(h * 16, (h + 1) * 16)
        attended = jnp.concatenate([att[0, mine, :], att[1, mine, :]], axis=1)
        head_values = jnp.dot(
            attended.astype(jnp.bfloat16), up_ref[h], preferred_element_type=jnp.float32
        ).astype(jnp.bfloat16)
        for i in range(values.shape[0]):
            values[i, :, h * VDIM : (h + 1) * VDIM] = head_values
    values_copies = repeat_to(values, values_hbm, sems.at[2])
    start(values_copies)
    wait(values_copies)
    wait(keys_copies)


def decode(ctx, spans, pages, lengths, queries, fresh, pieces, value_up):
    smem = pl.BlockSpec(memory_space=pltpu.SMEM)
    vmem = pl.BlockSpec(memory_space=pltpu.VMEM)
    hbm = pl.BlockSpec(memory_space=pltpu.HBM)
    rows_local = pages.shape[0]
    heads = value_up.shape[0]
    key_rows = spans.shape[0] * SPAN
    return pl.pallas_call(
        decode_kernel,
        out_shape=(
            jax.ShapeDtypeStruct((key_rows, KPAD), jnp.bfloat16),
            jax.ShapeDtypeStruct((16, 2 * rows_local, heads * VDIM), jnp.bfloat16),
        ),
        in_specs=[smem] * 4 + [vmem] * 12 + [hbm],
        out_specs=(hbm, hbm),
        scratch_shapes=[
            pltpu.VMEM(value_up.shape, jnp.bfloat16),
            pltpu.VMEM((key_rows, KPAD), jnp.bfloat16),
            pltpu.VMEM((rows_local, pages.shape[1] * SPAN + 128, KPAD), jnp.bfloat16),
            pltpu.VMEM((2, 16 * heads, 128), jnp.float32),
            pltpu.VMEM((4, 2 * rows_local, heads * VDIM), jnp.bfloat16),
            pltpu.SemaphoreType.DMA((3, 4)),
        ],
        compiler_params=pltpu.CompilerParams(vmem_limit_bytes=56 << 20),
        cost_estimate=pl.CostEstimate(
            flops=2 * 8 * 64 * 1152 * 640, bytes_accessed=12 << 20, transcendentals=8 * 64 * 1152
        ),
    )(ctx, spans, pages, lengths, queries, fresh, *pieces, value_up)


def arrange_kernel(q_ref, dq_ref, new_latents_ref, new_rope_ref, *refs):
    out_ref, decode_out_ref, fresh_out_ref, decode_rows, fresh = refs
    for pair in range(HEADS_TILE // 2):
        at = pair * 2 * KEYW
        for s in range(2):
            tokens = slice(s * SPAN, (s + 1) * SPAN)
            out_ref[s, 2 * pair * SPAN : (2 * pair + 1) * SPAN, :] = q_ref[tokens, at : at + KPAD]
            odd = q_ref[tokens, at + 256 : at + 640].astype(jnp.float32)
            out_ref[s, (2 * pair + 1) * SPAN : (2 * pair + 2) * SPAN, :] = pltpu.roll(
                odd, KPAD - 64, 1
            ).astype(jnp.bfloat16)

    @pl.when(pl.program_id(0) == 0)
    def _():
        rows_local = dq_ref.shape[1]
        fresh[...] = jnp.zeros_like(fresh)
        for s in range(2):
            for h in range(32):
                at = h // 2 * 2 * KEYW + h % 2 * 256
                rows = dq_ref[s, :, at : at + KPAD].astype(jnp.float32)
                if h % 2:
                    rows = pltpu.roll(rows, KPAD - 64, 1)
                for c in range(3):
                    decode_rows[c, pl.ds(s * 32 + h, rows_local, stride=64), :] = rows[
                        :, c * 128 : (c + 1) * 128
                    ]
            mine = pl.ds(s, rows_local, stride=16)
            latent_rows = new_latents_ref[s].astype(jnp.float32)
            fresh[0, mine, :] = latent_rows[:, :128]
            fresh[1, mine, :] = latent_rows[:, 128:]
            rope_rows = new_rope_ref[s].astype(jnp.float32)
            fresh[2, mine, :] = jnp.concatenate([rope_rows, jnp.zeros_like(rope_rows)], axis=1)
        for b in range(rows_local):
            for rows_ref, out, size in ((decode_rows, decode_out_ref, 64), (fresh, fresh_out_ref, 16)):
                rows = slice(b * size, (b + 1) * size)
                parts = [rows_ref[c, rows, :] for c in range(3)]
                out[b] = jnp.concatenate(parts, axis=1).astype(jnp.bfloat16)


def arrange(queries, decode_queries, latents, rope):
    vmem = pl.BlockSpec(memory_space=pltpu.VMEM)
    rows_local = decode_queries.shape[1]
    tiles = queries.shape[1] // (HEADS_TILE * KEYW)
    bf16 = jnp.bfloat16
    whole = [(rows_local, 64, KPAD), (rows_local, 16, KPAD)]
    return pl.pallas_call(
        arrange_kernel,
        grid=(tiles,),
        out_shape=[jax.ShapeDtypeStruct((2 * tiles, ROWS, KPAD), bf16)]
        + [jax.ShapeDtypeStruct(shape, bf16) for shape in whole],
        in_specs=[pl.BlockSpec((2 * SPAN, HEADS_TILE * KEYW), lambda i: (0, i))] + [vmem] * 3,
        out_specs=[pl.BlockSpec((2, ROWS, KPAD), lambda i: (i, 0, 0))]
        + [pl.BlockSpec(shape, lambda i: (0, 0, 0)) for shape in whole],
        scratch_shapes=[
            pltpu.VMEM((3, 64 * rows_local, 128), jnp.float32),
            pltpu.VMEM((3, 16 * rows_local, 128), jnp.float32),
        ],
        compiler_params=pltpu.CompilerParams(vmem_limit_bytes=16 << 20),
        cost_estimate=pl.CostEstimate(flops=0, bytes_accessed=12 << 20, transcendentals=0),
    )(queries, decode_queries, latents, rope)


def clear(top, total, acc, p_b, r_b):
    top[...] = jnp.full(top.shape, FAR_BELOW, jnp.float32)
    total[...] = jnp.zeros_like(total)
    acc[...] = jnp.zeros_like(acc)
    p_b[...] = jnp.zeros_like(p_b)
    r_b[...] = jnp.ones_like(r_b)


def prefill_kernel(ctx_ref, spans_ref, qs_hbm, k_hbm, up_hbm, out_hbm, done_ref, *scratch):
    out_ref, qs, k_ref, kt_ref, up_ref, s_a, s_b, p_a, p_b, top, total, r_a, r_b, acc, sems = scratch
    tiles = acc.shape[0] // 2
    k_copies = copies_in_parts(k_hbm, k_ref, sems.at[0])
    q_copies = copies_in_parts(qs_hbm, qs, sems.at[1])
    up_copies = copies_in_parts(up_hbm, up_ref, sems.at[2])
    start(k_copies + q_copies)
    clear(top, total, acc, p_b, r_b)
    pieces = kt_ref.shape[0]
    for n in range(pieces):
        if n % (pieces // len(k_copies)) == 0:
            k_copies[n // (pieces // len(k_copies))].wait()
        kt_ref[n] = k_ref[n * KEYS // 2 : (n + 1) * KEYS // 2, :].T
    span_of = [spans_ref[2 * ctx_ref[0] + s] for s in range(2)]
    blocks_of = [span // (KEYS // SPAN) for span in span_of]
    offset_of = [(span_of[s] - blocks_of[s] * (KEYS // SPAN)) * SPAN for s in range(2)]
    wait(q_copies)
    start(up_copies)

    def key_rows(block):
        return pl.ds(pl.multiple_of(block * KEYS, KEYS), KEYS)

    def score_part(unit, block, s_ref, part):
        cols = slice(part * KEYS // 2, (part + 1) * KEYS // 2)
        s_ref[:, cols] = jnp.dot(
            qs[unit], kt_ref[2 * block + part], preferred_element_type=jnp.float32
        )

    lead = lax.broadcasted_iota(jnp.int32, (SPAN, 128), 1)
    lead = lead - lax.broadcasted_iota(jnp.int32, (SPAN, 128), 0)

    def weigh_part(unit, s_ref, p_ref, r_ref, offset, part):
        for h in range(part * HEADS_TILE // 4, (part + 1) * HEADS_TILE // 4):
            rows = slice(h * SPAN, (h + 1) * SPAN)
            parts = [s_ref[rows, c * 128 : (c + 1) * 128] for c in range(KEYS // 128)]
            parts = [
                jnp.where(lead <= offset - c * 128, part, FAR_BELOW)
                for c, part in enumerate(parts)
            ]
            highest = functools.reduce(jnp.maximum, parts)
            old = top[unit, rows]
            new = jnp.maximum(old, jnp.max(highest, axis=1, keepdims=True))
            top[unit, rows] = new
            scaled = new * EXP2_SCALE
            rescale = jnp.exp2(old * EXP2_SCALE - scaled)
            r_ref[rows] = rescale
            weights = [jnp.exp2(part * EXP2_SCALE - scaled) for part in parts]
            total[unit, rows] = total[unit, rows] * rescale + sum(weights)
            for c, weight in enumerate(weights):
                p_ref[rows, c * 128 : (c + 1) * 128] = weight.astype(jnp.bfloat16)

    def add_part(unit, block, p_ref, r_ref, part):
        rows = slice(part * ROWS // 2, (part + 1) * ROWS // 2)
        product = jnp.dot(
            p_ref[rows, :], k_ref[key_rows(block), :LATENT], preferred_element_type=jnp.float32
        )
        r = r_ref[rows]
        acc[unit, rows, :128] = acc[unit, rows, :128] * r + product[:, :128]
        acc[unit, rows, 128:] = acc[unit, rows, 128:] * r + product[:, 128:]

    def step(later, here, before, s_later, s_here, p_here, r_here, p_before, r_before, offset):
        score_part(*later, s_later, 0)
        weigh_part(here[0], s_here, p_here, r_here, offset, 0)
        score_part(*later, s_later, 1)
        weigh_part(here[0], s_here, p_here, r_here, offset, 1)
        add_part(*before, p_before, r_before, 0)
        weigh_part(here[0], s_here, p_here, r_here, offset, 2)
        add_part(*before, p_before, r_before, 1)
        weigh_part(here[0], s_here, p_here, r_here, offset, 3)

    def last_block(unit):
        return jnp.where(unit % 2 == 0, blocks_of[0], blocks_of[1])

    def following(item):
        unit, block = item
        ends = block == last_block(unit)
        unit = jnp.minimum(jnp.where(ends, unit + 1, unit), 2 * tiles - 1)
        return unit, jnp.where(ends, 0, block + 1)

    def offset(item):
        unit, block = item
        own = jnp.where(unit % 2 == 0, offset_of[0], offset_of[1])
        return jnp.where(block == last_block(unit), own, KEYS)

    def two_items(i, carry):
        before, here = carry[:2], carry[2:]
        after = following(here)
        step(after, here, before, s_b, s_a, p_a, r_a, p_b, r_b, offset(here))
        later = following(after)
        step(later, after, here, s_a, s_b, p_b, r_b, p_a, r_a, offset(after))
        return after + later

    def first_weigh_part(item, s_ref, p_ref, part):
        unit, limit = item[0], offset(item)
        for h in range(part * HEADS_TILE // 4, (part + 1) * HEADS_TILE // 4):
            rows = slice(h * SPAN, (h + 1) * SPAN)
            parts = [
                jnp.where(
                    lead <= limit - c * 128, s_ref[rows, c * 128 : (c + 1) * 128], FAR_BELOW
                )
                for c in range(KEYS // 128)
            ]
            highest = jnp.max(functools.reduce(jnp.maximum, parts), axis=1, keepdims=True)
            top[unit, rows] = jnp.broadcast_to(highest * EXP2_SCALE, (SPAN, 128))
            keep_weights(unit, rows, parts, p_ref)

    def next_weigh_part(item, s_ref, p_ref, part):
        for h in range(part * HEADS_TILE // 4, (part + 1) * HEADS_TILE // 4):
            rows = slice(h * SPAN, (h + 1) * SPAN)
            parts = [s_ref[rows, c * 128 : (c + 1) * 128] for c in range(KEYS // 128)]
            keep_weights(item[0], rows, parts, p_ref)

    def keep_weights(unit, rows, parts, p_ref):
        shift = top[unit, rows]
        weights = [jnp.exp2(part * EXP2_SCALE - shift) for part in parts]
        total[unit, rows] = total[unit, rows] + sum(weights)
        for c, weight in enumerate(weights):
            p_ref[rows, c * 128 : (c + 1) * 128] = weight.astype(jnp.bfloat16)

    def plain_add_part(unit, block, p_ref, part):
        rows = slice(part * ROWS // 2, (part + 1) * ROWS // 2)
        acc[unit, rows, :] = acc[unit, rows, :] + jnp.dot(
            p_ref[rows, :], k_ref[key_rows(block), :LATENT], preferred_element_type=jnp.float32
        )

    def plain_step(weigh, later, here, before, s_later, s_here, p_here, p_before):
        score_part(*later, s_later, 0)
        weigh(here, s_here, p_here, 0)
        score_part(*later, s_later, 1)
        weigh(here, s_here, p_here, 1)
        plain_add_part(*before, p_before, 0)
        weigh(here, s_here, p_here, 2)
        plain_add_part(*before, p_before, 1)
        weigh(here, s_here, p_here, 3)

    def own_item(unit):
        return unit, last_block(unit)

    def following_whole(item):
        unit, block = item
        ends = block + 1 >= last_block(unit)
        skips = jnp.where(last_block(1 - unit % 2) == 0, 2, 1)
        unit = jnp.where(ends, unit + skips, unit)
        block = jnp.where(ends, 0, block + 1)
        over = unit >= 2 * tiles
        unit = jnp.where(over, 2 * tiles - 1, unit)
        return unit, jnp.where(over, last_block(unit), block)

    whole_blocks = blocks_of[0] + blocks_of[1]
    first_whole = jnp.where(blocks_of[0] == 0, 1, 0), jnp.int32(0)

    def two_own(i, before):
        even, odd = own_item(2 * i), own_item(2 * i + 1)
        plain_step(first_weigh_part, odd, even, before, s_b, s_a, p_a, p_b)
        later = own_item(jnp.minimum(2 * i + 2, 2 * tiles - 1))
        ends = (i == tiles - 1) & (whole_blocks > 0)
        later = tuple(jnp.where(ends, w, o) for w, o in zip(first_whole, later))
        plain_step(first_weigh_part, later, odd, even, s_a, s_b, p_b, p_a)
        return odd

    def two_whole(i, carry):
        before, here = carry[:2], carry[2:]
        after = following_whole(here)
        plain_step(next_weigh_part, after, here, before, s_b, s_a, p_a, p_b)
        later = following_whole(after)
        plain_step(next_weigh_part, later, after, here, s_a, s_b, p_b, p_a)
        return after + later

    for part in range(2):
        score_part(*own_item(0), s_a, part)
    before = lax.fori_loop(0, tiles, two_own, (jnp.int32(0), jnp.int32(0)))
    before = lax.fori_loop(0, whole_blocks * (tiles // 2), two_whole, before + first_whole)[:2]
    for part in range(2):
        plain_add_part(*before, p_b, part)

    @pl.when(jnp.logical_not(jnp.max(total[...]) < TOTAL_LIMIT))
    def _():
        clear(top, total, acc, p_b, r_b)
        for part in range(2):
            score_part(0, 0, s_a, part)
        rounds = (whole_blocks + 2) * (tiles // 2)
        before = lax.fori_loop(0, rounds, two_items, (jnp.int32(0),) * 4)[:2]
        for part in range(2):
            add_part(*before, p_b, r_b, part)

    wait(up_copies)

    def out_copy(tile):
        width = HEADS_TILE * VDIM
        columns = pl.ds(pl.multiple_of(tile * width, width), width)
        return pltpu.make_async_copy(
            out_ref.at[:, columns], out_hbm.at[:, columns], sems.at[3, tile]
        )

    def finish(tile, carry):
        attended = []
        for s in range(2):
            unit = 2 * tile + s
            share = 1.0 / jnp.sum(total[unit], axis=1, keepdims=True)
            attended.append((acc[unit] * share).astype(jnp.bfloat16))
        values = []
        for h in range(HEADS_TILE):
            rows = slice(h * SPAN, (h + 1) * SPAN)
            both = jnp.concatenate([attended[0][rows], attended[1][rows]], axis=0)
            values.append(
                jnp.dot(
                    both, up_ref[tile * HEADS_TILE + h], preferred_element_type=jnp.float32
                ).astype(jnp.bfloat16)
            )
        columns = HEADS_TILE * VDIM
        out_ref[:, pl.ds(pl.multiple_of(tile * columns, columns), columns)] = jnp.concatenate(
            values, axis=1
        )
        out_copy(tile).start()
        return carry

    lax.fori_loop(0, tiles, finish, 0)
    for tile in range(tiles):
        out_copy(tile).wait()
    done_ref[0] = 0


def prefill(ctx, spans, queries, keys, value_up):
    units = queries.shape[0]
    heads = value_up.shape[0]
    f32 = jnp.float32
    smem = pl.BlockSpec(memory_space=pltpu.SMEM)
    hbm = pl.BlockSpec(memory_space=pltpu.HBM)
    return pl.pallas_call(
        prefill_kernel,
        out_shape=(
            jax.ShapeDtypeStruct((2 * SPAN, heads * VDIM), jnp.bfloat16),
            jax.ShapeDtypeStruct((1,), jnp.int32),
        ),
        in_specs=[smem] * 2 + [hbm] * 3,
        out_specs=(hbm, smem),
        scratch_shapes=[
            pltpu.VMEM((2 * SPAN, heads * VDIM), jnp.bfloat16),
            pltpu.VMEM(queries.shape, jnp.bfloat16),
            pltpu.VMEM(keys.shape, jnp.bfloat16),
            pltpu.VMEM((2 * keys.shape[0] // KEYS, KPAD, KEYS // 2), jnp.bfloat16),
            pltpu.VMEM(value_up.shape, jnp.bfloat16),
            pltpu.VMEM((ROWS, KEYS), f32),
            pltpu.VMEM((ROWS, KEYS), f32),
            pltpu.VMEM((ROWS, KEYS), jnp.bfloat16),
            pltpu.VMEM((ROWS, KEYS), jnp.bfloat16),
            pltpu.VMEM((units, ROWS, 128), f32),
            pltpu.VMEM((units, ROWS, 128), f32),
            pltpu.VMEM((ROWS, 128), f32),
            pltpu.VMEM((ROWS, 128), f32),
            pltpu.VMEM((units, ROWS, LATENT), f32),
            pltpu.SemaphoreType.DMA((4, 4)),
        ],
        compiler_params=pltpu.CompilerParams(vmem_limit_bytes=59 << 20),
        cost_estimate=pl.CostEstimate(
            flops=units * ROWS * keys.shape[0] * 640,
            bytes_accessed=8 << 20,
            transcendentals=units * ROWS * keys.shape[0] // 2,
        ),
    )(ctx, spans, queries, keys, value_up)


def project_kernel(ctx_ref, grp_ref, rows_hbm, w_hbm, other_w_hbm, after_ref, *refs):
    out_refs, (rows_ref, w_ref, sums, sems) = refs[:4], refs[4:]
    chunks = sems.shape[1]
    width = rows_ref.shape[1] // chunks
    parts = [(slice(None), slice(c * width, (c + 1) * width)) for c in range(chunks)]
    sides = ((rows_hbm, rows_ref), (w_hbm, w_ref.at[0]), (other_w_hbm, w_ref.at[1]))
    copies = [
        [
            pltpu.make_async_copy(source.at[part], target.at[part], sems.at[i, c])
            for i, (source, target) in enumerate(sides)
        ]
        for c, part in enumerate(parts)
    ]
    for three in copies:
        for copy in three:
            copy.start()
    z, head_z, head_core = ctx_ref[0] // 16, grp_ref[0] // 2, grp_ref[0] % 2
    for c, part in enumerate(parts):
        for copy in copies[c]:
            copy.wait()
        for side in range(2):
            product = lax.dot_general(
                rows_ref[part], w_ref[side, :, part[1]], NT, preferred_element_type=jnp.float32
            )
            sums[side] = product if c == 0 else sums[side] + product
    share = sums.shape[1] // 2
    for k, out_ref in enumerate(out_refs):
        to_z, to_core = (head_z + k // 2) % 2, (head_core + k) % 2
        side = jnp.where(to_z == z, 0, 1)
        rows = pl.ds(pl.multiple_of(to_core * share, share), share)
        out_ref[...] = sums[side, rows, :].astype(jnp.bfloat16)


def project(ctx, grp, rows, weights, other_weights, after):
    smem = pl.BlockSpec(memory_space=pltpu.SMEM)
    vmem = pl.BlockSpec(memory_space=pltpu.VMEM)
    hbm = pl.BlockSpec(memory_space=pltpu.HBM)
    width, depth = weights.shape
    row_count = rows.shape[0]
    return pl.pallas_call(
        project_kernel,
        out_shape=(jax.ShapeDtypeStruct((row_count // 2, width), jnp.bfloat16),) * 4,
        in_specs=[smem, smem, hbm, hbm, hbm, smem],
        out_specs=(vmem,) * 4,
        scratch_shapes=[
            pltpu.VMEM(rows.shape, jnp.bfloat16),
            pltpu.VMEM((2, width, depth), jnp.bfloat16),
            pltpu.VMEM((2, row_count, width), jnp.float32),
            pltpu.SemaphoreType.DMA((3, 4)),
        ],
        compiler_params=pltpu.CompilerParams(vmem_limit_bytes=57 << 20),
        cost_estimate=pl.CostEstimate(
            flops=4 * row_count * depth * 256, bytes_accessed=8 << 20, transcendentals=0
        ),
    )(ctx, grp, rows, weights, other_weights, after)


def share_out(k, part):
    pairs = []
    for ctx in range(lax.axis_size("ctx")):
        z, line = divmod(ctx, 16)
        for a in range(2):
            for b in range(2):
                to = ((a ^ k // 2) * 16 + line) * 4 + 2 * z + (b ^ k % 2)
                pairs.append((ctx * 4 + 2 * a + b, to))
    return lax.ppermute(part, ("ctx", "grp"), pairs)


def body(
    prefill_queries,
    latents,
    rope_keys,
    span_slots,
    decode_queries,
    new_latents,
    new_rope,
    context_lengths,
    page_table,
    value_up,
    out_proj,
):
    ctx = lax.axis_index("ctx").astype(jnp.int32).reshape(1)
    grp = lax.axis_index("grp").astype(jnp.int32).reshape(1)
    rows_local = page_table.shape[0]

    pieces = gather_caches(pack(latents, rope_keys))
    queries, row_queries, fresh = arrange(prefill_queries, decode_queries, new_latents, new_rope)
    keys, decode_values = decode(
        ctx, span_slots, page_table, context_lengths, row_queries, fresh, pieces, value_up
    )
    weights = out_proj.T
    other_weights = shift(weights, 1, 0, 0)
    all_values = exchange(decode_values).reshape(-1, decode_values.shape[2])
    prefill_values, prefill_done = prefill(ctx, span_slots, queries, keys, value_up)
    parts = project(ctx, grp, all_values, weights, other_weights, prefill_done)
    summed = sum(share_out(k, part).astype(jnp.float32) for k, part in enumerate(parts))
    decoded = summed.astype(jnp.bfloat16).reshape(-1, 2, rows_local, summed.shape[1])
    decoded = decoded.transpose(1, 0, 2, 3).reshape(2, -1, summed.shape[1])
    return (prefill_values, decoded)


def solution(mesh):
    placed = (
        P("ctx", "grp"),
        P("ctx", "grp"),
        P("ctx", None),
        P(),
        P(None, "ctx", "grp"),
        P(None, "ctx", "grp"),
        P(None, "ctx", None),
        P("ctx"),
        P("ctx", None),
        P("grp", None, None),
        P("grp", "ctx"),
    )
    return jax.shard_map(
        body,
        mesh=mesh,
        in_specs=placed,
        out_specs=(P("ctx", "grp"), P(None, "grp", "ctx")),
        check_vma=False,
    )
```

```python
import functools
import math

import jax
import jax.numpy as jnp
from jax import lax
from jax.experimental import pallas as pl
from jax.experimental.pallas import tpu as pltpu
from jax.sharding import PartitionSpec as P

SPAN = 64
LATENT = 256
ROPE = 64
KEYW = LATENT + ROPE
KPAD = 384
VDIM = 128

HEADS_TILE = 16
ROWS = HEADS_TILE * SPAN
KEYS = 512

EXP2_SCALE = 192.0 ** -0.5 * math.log2(math.e)
FAR_BELOW = -1e30
TOTAL_LIMIT = 2.0**100
NT = (((1,), (1,)), ((), ()))
RING = (0, -1, 1, 2)


def exchange(copies):
    size = lax.axis_size("ctx")
    groups = [list(range(z * size // 2, (z + 1) * size // 2)) for z in range(2)]
    return lax.all_to_all(
        copies, "ctx", split_axis=0, concat_axis=0, axis_index_groups=groups, tiled=True
    )


def shift(value, dz, dx, dy):
    pairs = []
    for ctx in range(lax.axis_size("ctx")):
        z, x, y = ctx // 16, ctx // 4 % 4, ctx % 4
        pairs.append((ctx, (z + dz) % 2 * 16 + (x + dx) % 4 * 4 + (y + dy) % 4))
    return lax.ppermute(value, "ctx", pairs)


def along(axis, steps):
    return (0, steps, 0) if axis == "x" else (0, 0, steps)


def gather_caches(own):
    other = shift(own, 1, 0, 0)
    axes = ("yx", "xy")
    held = [jnp.stack([own[half], other[half]]) for half in range(2)]
    for half in range(2):
        ring = [shift(held[half], *along(axes[half][0], -off)) for off in RING[1:]]
        held[half] = jnp.concatenate([held[half]] + ring)
    near = [
        [shift(held[half], *along(axes[half][1], -off)) for off in RING[1:3]] for half in range(2)
    ]
    cut = held[0].shape[0] // 2
    pieces = []
    for half in range(2):
        after, before = near[half]
        far_first = shift(after[:cut], *along(axes[half][1], 1))
        far_second = shift(before[cut:], *along(axes[half][1], -1))
        pieces += [held[half], after, before, far_first, far_second]
    return pieces


def block_offsets(half):
    places = []
    for last in RING:
        for first in RING:
            for dz in range(2):
                places.append((dz, last, first) if half == 0 else (dz, first, last))
    return places


def pack_kernel(latents_ref, rope_ref, out_ref):
    rope = rope_ref[...].astype(jnp.float32).T
    for span in range(2):
        rows = slice(span * SPAN, (span + 1) * SPAN)
        out_ref[span, :SPAN, :] = latents_ref[rows, :]
        parts = [rope[span * SPAN + c * 16 : span * SPAN + (c + 1) * 16] for c in range(4)]
        out_ref[span, SPAN:, :] = jnp.concatenate(parts, axis=1).astype(jnp.bfloat16)


def pack(latents, rope_keys):
    return pl.pallas_call(
        pack_kernel,
        out_shape=jax.ShapeDtypeStruct((2, SPAN + SPAN // 4, LATENT), jnp.bfloat16),
    )(latents, rope_keys.T)


def copies_in_parts(source, target, sems, axis=0):
    parts = sems.shape[0]
    size = source.shape[axis] // parts
    where = [(slice(None),) * axis + (slice(i * size, (i + 1) * size),) for i in range(parts)]
    return [
        pltpu.make_async_copy(source.at[at], target.at[at], sems.at[i])
        for i, at in enumerate(where)
    ]


def start(copies):
    for copy in copies:
        copy.start()


def wait(copies):
    for copy in copies:
        copy.wait()


def repeat_to(source, target, sems):
    size = source.shape[0]
    return [
        pltpu.make_async_copy(source, target.at[i * size : (i + 1) * size], sems.at[i])
        for i in range(target.shape[0] // size)
    ]


def unpack(block, keys_ref, place):
    rows = pl.ds(pl.multiple_of(place * SPAN, SPAN), SPAN)
    keys_ref[rows, :LATENT] = block[:SPAN, :]
    packed = block[SPAN:, :].astype(jnp.float32)
    low_lanes = lax.broadcasted_iota(jnp.int32, (16, 128), 1) < ROPE
    parts = []
    for c in range(2):
        two = packed[:, c * 128 : (c + 1) * 128]
        parts.append(jnp.where(low_lanes, two, 0.0))
        parts.append(jnp.where(low_lanes, pltpu.roll(two, 64, 1), 0.0))
    keys_ref[rows, LATENT:] = jnp.concatenate(parts, axis=0).astype(jnp.bfloat16)


def decode_kernel(ctx_ref, spans_ref, pages_ref, lengths_ref, *refs):
    q_ref, fresh_ref, *piece_refs, up_hbm, keys_hbm, values_hbm = refs[:15]
    up_ref, keys_ref, cache, att, values, sems = refs[15:]
    up_copies = copies_in_parts(up_hbm, up_ref, sems.at[0])
    start(up_copies)
    rows_local, pages = pages_ref.shape
    slots = pages * SPAN
    width = cache.shape[1]
    z, x, y = ctx_ref[0] // 16, ctx_ref[0] // 4 % 4, ctx_ref[0] % 4
    for half in range(2):
        blocks = [ref.at[i] for ref in piece_refs[5 * half : 5 * half + 5] for i in range(ref.shape[0])]
        for block, (dz, dx, dy) in zip(blocks, block_offsets(half)):
            source = (z + dz) % 2 * 16 + (x + dx + 4) % 4 * 4 + (y + dy + 4) % 4
            unpack(block, keys_ref, spans_ref[2 * source + half])
    keys_copies = copies_in_parts(keys_ref, keys_hbm, sems.at[1])
    start(keys_copies)
    for b in range(rows_local):
        cache[b, slots : slots + 16, :] = fresh_ref[b]
        cache[b, slots + 16 :, :] = jnp.zeros((width - slots - 16, KPAD), jnp.bfloat16)

    cols = lax.broadcasted_iota(jnp.int32, (64, width), 1)
    step = lax.broadcasted_iota(jnp.int32, (64, width), 0) // 32
    fresh_seen = (cols >= slots) & (cols - slots <= step)
    for b in range(rows_local):
        for j in range(pages):
            page = pages_ref[b, j]
            cache[b, j * SPAN : (j + 1) * SPAN, :] = keys_ref[
                pl.ds(pl.multiple_of(page * SPAN, SPAN), SPAN), :
            ]
        scores = lax.dot_general(q_ref[b], cache[b], NT, preferred_element_type=jnp.float32)
        seen = (cols < lengths_ref[b]) | fresh_seen
        scores = jnp.where(seen, scores, FAR_BELOW)
        top = jnp.max(scores, axis=1, keepdims=True)
        weights = jnp.exp2(scores * EXP2_SCALE - top * EXP2_SCALE)
        total = jnp.sum(weights, axis=1, keepdims=True)
        attended = jnp.dot(
            weights.astype(jnp.bfloat16), cache[b, :, :LATENT], preferred_element_type=jnp.float32
        )
        attended = attended / total
        for s in range(2):
            for c in range(2):
                att[c, pl.ds(s * rows_local + b, 32, stride=16), :] = attended[
                    s * 32 : (s + 1) * 32, c * 128 : (c + 1) * 128
                ]
    wait(up_copies)
    for h in range(32):
        mine = slice(h * 16, (h + 1) * 16)
        attended = jnp.concatenate([att[0, mine, :], att[1, mine, :]], axis=1)
        head_values = jnp.dot(
            attended.astype(jnp.bfloat16), up_ref[h], preferred_element_type=jnp.float32
        ).astype(jnp.bfloat16)
        for i in range(values.shape[0]):
            values[i, :, h * VDIM : (h + 1) * VDIM] = head_values
    values_copies = repeat_to(values, values_hbm, sems.at[2])
    start(values_copies)
    wait(values_copies)
    wait(keys_copies)


def decode(ctx, spans, pages, lengths, queries, fresh, pieces, value_up):
    smem = pl.BlockSpec(memory_space=pltpu.SMEM)
    vmem = pl.BlockSpec(memory_space=pltpu.VMEM)
    hbm = pl.BlockSpec(memory_space=pltpu.HBM)
    rows_local = pages.shape[0]
    heads = value_up.shape[0]
    key_rows = spans.shape[0] * SPAN
    return pl.pallas_call(
        decode_kernel,
        out_shape=(
            jax.ShapeDtypeStruct((key_rows, KPAD), jnp.bfloat16),
            jax.ShapeDtypeStruct((16, 2 * rows_local, heads * VDIM), jnp.bfloat16),
        ),
        in_specs=[smem] * 4 + [vmem] * 12 + [hbm],
        out_specs=(hbm, hbm),
        scratch_shapes=[
            pltpu.VMEM(value_up.shape, jnp.bfloat16),
            pltpu.VMEM((key_rows, KPAD), jnp.bfloat16),
            pltpu.VMEM((rows_local, pages.shape[1] * SPAN + 128, KPAD), jnp.bfloat16),
            pltpu.VMEM((2, 16 * heads, 128), jnp.float32),
            pltpu.VMEM((4, 2 * rows_local, heads * VDIM), jnp.bfloat16),
            pltpu.SemaphoreType.DMA((3, 4)),
        ],
        compiler_params=pltpu.CompilerParams(vmem_limit_bytes=57 << 20),
        cost_estimate=pl.CostEstimate(
            flops=2 * 8 * 64 * 1152 * 640, bytes_accessed=12 << 20, transcendentals=8 * 64 * 1152
        ),
    )(ctx, spans, pages, lengths, queries, fresh, *pieces, value_up)


def arrange_kernel(q_ref, dq_ref, new_latents_ref, new_rope_ref, *refs):
    out_ref, decode_out_ref, fresh_out_ref, decode_rows, fresh = refs
    for pair in range(HEADS_TILE // 2):
        at = pair * 2 * KEYW
        for s in range(2):
            tokens = slice(s * SPAN, (s + 1) * SPAN)
            out_ref[s, 2 * pair * SPAN : (2 * pair + 1) * SPAN, :] = q_ref[tokens, at : at + KPAD]
            odd = q_ref[tokens, at + 256 : at + 640].astype(jnp.float32)
            out_ref[s, (2 * pair + 1) * SPAN : (2 * pair + 2) * SPAN, :] = pltpu.roll(
                odd, KPAD - 64, 1
            ).astype(jnp.bfloat16)

    @pl.when(pl.program_id(0) == 0)
    def _():
        rows_local = dq_ref.shape[1]
        fresh[...] = jnp.zeros_like(fresh)
        for s in range(2):
            for h in range(32):
                at = h // 2 * 2 * KEYW + h % 2 * 256
                rows = dq_ref[s, :, at : at + KPAD].astype(jnp.float32)
                if h % 2:
                    rows = pltpu.roll(rows, KPAD - 64, 1)
                for c in range(3):
                    decode_rows[c, pl.ds(s * 32 + h, rows_local, stride=64), :] = rows[
                        :, c * 128 : (c + 1) * 128
                    ]
            mine = pl.ds(s, rows_local, stride=16)
            latent_rows = new_latents_ref[s].astype(jnp.float32)
            fresh[0, mine, :] = latent_rows[:, :128]
            fresh[1, mine, :] = latent_rows[:, 128:]
            rope_rows = new_rope_ref[s].astype(jnp.float32)
            fresh[2, mine, :] = jnp.concatenate([rope_rows, jnp.zeros_like(rope_rows)], axis=1)
        for b in range(rows_local):
            for rows_ref, out, size in ((decode_rows, decode_out_ref, 64), (fresh, fresh_out_ref, 16)):
                rows = slice(b * size, (b + 1) * size)
                parts = [rows_ref[c, rows, :] for c in range(3)]
                out[b] = jnp.concatenate(parts, axis=1).astype(jnp.bfloat16)


def arrange(queries, decode_queries, latents, rope):
    vmem = pl.BlockSpec(memory_space=pltpu.VMEM)
    rows_local = decode_queries.shape[1]
    tiles = queries.shape[1] // (HEADS_TILE * KEYW)
    bf16 = jnp.bfloat16
    whole = [(rows_local, 64, KPAD), (rows_local, 16, KPAD)]
    return pl.pallas_call(
        arrange_kernel,
        grid=(tiles,),
        out_shape=[jax.ShapeDtypeStruct((2 * tiles, ROWS, KPAD), bf16)]
        + [jax.ShapeDtypeStruct(shape, bf16) for shape in whole],
        in_specs=[pl.BlockSpec((2 * SPAN, HEADS_TILE * KEYW), lambda i: (0, i))] + [vmem] * 3,
        out_specs=[pl.BlockSpec((2, ROWS, KPAD), lambda i: (i, 0, 0))]
        + [pl.BlockSpec(shape, lambda i: (0, 0, 0)) for shape in whole],
        scratch_shapes=[
            pltpu.VMEM((3, 64 * rows_local, 128), jnp.float32),
            pltpu.VMEM((3, 16 * rows_local, 128), jnp.float32),
        ],
        compiler_params=pltpu.CompilerParams(vmem_limit_bytes=16 << 20),
        cost_estimate=pl.CostEstimate(flops=0, bytes_accessed=12 << 20, transcendentals=0),
    )(queries, decode_queries, latents, rope)


def clear(top, total, acc, p_b, r_b):
    top[...] = jnp.full(top.shape, FAR_BELOW, jnp.float32)
    total[...] = jnp.zeros_like(total)
    acc[...] = jnp.zeros_like(acc)
    p_b[...] = jnp.zeros_like(p_b)
    r_b[...] = jnp.ones_like(r_b)


def prefill_kernel(ctx_ref, spans_ref, qs_hbm, k_hbm, up_hbm, out_hbm, done_ref, *scratch):
    out_ref, qs, k_ref, kt_ref, up_ref, s_a, s_b, p_a, p_b, top, total, r_a, r_b, acc, sems = scratch
    tiles = acc.shape[0] // 2
    k_copies = copies_in_parts(k_hbm, k_ref, sems.at[0])
    q_copies = copies_in_parts(qs_hbm, qs, sems.at[1])
    up_copies = copies_in_parts(up_hbm, up_ref, sems.at[2])
    start(k_copies + q_copies)
    clear(top, total, acc, p_b, r_b)
    pieces = kt_ref.shape[0]
    for n in range(pieces):
        if n % (pieces // len(k_copies)) == 0:
            k_copies[n // (pieces // len(k_copies))].wait()
        kt_ref[n] = k_ref[n * KEYS // 2 : (n + 1) * KEYS // 2, :].T
    span_of = [spans_ref[2 * ctx_ref[0] + s] for s in range(2)]
    blocks_of = [span // (KEYS // SPAN) for span in span_of]
    offset_of = [(span_of[s] - blocks_of[s] * (KEYS // SPAN)) * SPAN for s in range(2)]
    wait(q_copies)
    start(up_copies)

    def key_rows(block):
        return pl.ds(pl.multiple_of(block * KEYS, KEYS), KEYS)

    def score_part(unit, block, s_ref, part):
        cols = slice(part * KEYS // 2, (part + 1) * KEYS // 2)
        s_ref[:, cols] = jnp.dot(
            qs[unit], kt_ref[2 * block + part], preferred_element_type=jnp.float32
        )

    lead = lax.broadcasted_iota(jnp.int32, (SPAN, 128), 1)
    lead = lead - lax.broadcasted_iota(jnp.int32, (SPAN, 128), 0)

    def weigh_part(unit, s_ref, p_ref, r_ref, offset, part):
        for h in range(part * HEADS_TILE // 4, (part + 1) * HEADS_TILE // 4):
            rows = slice(h * SPAN, (h + 1) * SPAN)
            parts = [s_ref[rows, c * 128 : (c + 1) * 128] for c in range(KEYS // 128)]
            parts = [
                jnp.where(lead <= offset - c * 128, part, FAR_BELOW)
                for c, part in enumerate(parts)
            ]
            highest = functools.reduce(jnp.maximum, parts)
            old = top[unit, rows]
            new = jnp.maximum(old, jnp.max(highest, axis=1, keepdims=True))
            top[unit, rows] = new
            scaled = new * EXP2_SCALE
            rescale = jnp.exp2(old * EXP2_SCALE - scaled)
            r_ref[rows] = rescale
            weights = [jnp.exp2(part * EXP2_SCALE - scaled) for part in parts]
            total[unit, rows] = total[unit, rows] * rescale + sum(weights)
            for c, weight in enumerate(weights):
                p_ref[rows, c * 128 : (c + 1) * 128] = weight.astype(jnp.bfloat16)

    def add_part(unit, block, p_ref, r_ref, part):
        rows = slice(part * ROWS // 2, (part + 1) * ROWS // 2)
        product = jnp.dot(
            p_ref[rows, :], k_ref[key_rows(block), :LATENT], preferred_element_type=jnp.float32
        )
        r = r_ref[rows]
        acc[unit, rows, :128] = acc[unit, rows, :128] * r + product[:, :128]
        acc[unit, rows, 128:] = acc[unit, rows, 128:] * r + product[:, 128:]

    def step(later, here, before, s_later, s_here, p_here, r_here, p_before, r_before, offset):
        score_part(*later, s_later, 0)
        weigh_part(here[0], s_here, p_here, r_here, offset, 0)
        score_part(*later, s_later, 1)
        weigh_part(here[0], s_here, p_here, r_here, offset, 1)
        add_part(*before, p_before, r_before, 0)
        weigh_part(here[0], s_here, p_here, r_here, offset, 2)
        add_part(*before, p_before, r_before, 1)
        weigh_part(here[0], s_here, p_here, r_here, offset, 3)

    def last_block(unit):
        return jnp.where(unit % 2 == 0, blocks_of[0], blocks_of[1])

    def following(item):
        unit, block = item
        ends = block == last_block(unit)
        unit = jnp.minimum(jnp.where(ends, unit + 1, unit), 2 * tiles - 1)
        return unit, jnp.where(ends, 0, block + 1)

    def offset(item):
        unit, block = item
        own = jnp.where(unit % 2 == 0, offset_of[0], offset_of[1])
        return jnp.where(block == last_block(unit), own, KEYS)

    def two_items(i, carry):
        before, here = carry[:2], carry[2:]
        after = following(here)
        step(after, here, before, s_b, s_a, p_a, r_a, p_b, r_b, offset(here))
        later = following(after)
        step(later, after, here, s_a, s_b, p_b, r_b, p_a, r_a, offset(after))
        return after + later

    def first_weigh_part(item, s_ref, p_ref, part):
        unit, limit = item[0], offset(item)
        for h in range(part * HEADS_TILE // 4, (part + 1) * HEADS_TILE // 4):
            rows = slice(h * SPAN, (h + 1) * SPAN)
            parts = [
                jnp.where(
                    lead <= limit - c * 128, s_ref[rows, c * 128 : (c + 1) * 128], FAR_BELOW
                )
                for c in range(KEYS // 128)
            ]
            highest = jnp.max(functools.reduce(jnp.maximum, parts), axis=1, keepdims=True)
            top[unit, rows] = jnp.broadcast_to(highest * EXP2_SCALE, (SPAN, 128))
            keep_weights(unit, rows, parts, p_ref)

    def next_weigh_part(item, s_ref, p_ref, part):
        for h in range(part * HEADS_TILE // 4, (part + 1) * HEADS_TILE // 4):
            rows = slice(h * SPAN, (h + 1) * SPAN)
            parts = [s_ref[rows, c * 128 : (c + 1) * 128] for c in range(KEYS // 128)]
            keep_weights(item[0], rows, parts, p_ref)

    def keep_weights(unit, rows, parts, p_ref):
        shift = top[unit, rows]
        weights = [jnp.exp2(part * EXP2_SCALE - shift) for part in parts]
        total[unit, rows] = total[unit, rows] + sum(weights)
        for c, weight in enumerate(weights):
            p_ref[rows, c * 128 : (c + 1) * 128] = weight.astype(jnp.bfloat16)

    def plain_add_part(unit, block, p_ref, part):
        rows = slice(part * ROWS // 2, (part + 1) * ROWS // 2)
        acc[unit, rows, :] = acc[unit, rows, :] + jnp.dot(
            p_ref[rows, :], k_ref[key_rows(block), :LATENT], preferred_element_type=jnp.float32
        )

    def plain_step(weigh, later, here, before, s_later, s_here, p_here, p_before):
        score_part(*later, s_later, 0)
        weigh(here, s_here, p_here, 0)
        score_part(*later, s_later, 1)
        weigh(here, s_here, p_here, 1)
        plain_add_part(*before, p_before, 0)
        weigh(here, s_here, p_here, 2)
        plain_add_part(*before, p_before, 1)
        weigh(here, s_here, p_here, 3)

    def own_item(unit):
        return unit, last_block(unit)

    def following_whole(item):
        unit, block = item
        ends = block + 1 >= last_block(unit)
        skips = jnp.where(last_block(1 - unit % 2) == 0, 2, 1)
        unit = jnp.where(ends, unit + skips, unit)
        block = jnp.where(ends, 0, block + 1)
        over = unit >= 2 * tiles
        unit = jnp.where(over, 2 * tiles - 1, unit)
        return unit, jnp.where(over, last_block(unit), block)

    whole_blocks = blocks_of[0] + blocks_of[1]
    first_whole = jnp.where(blocks_of[0] == 0, 1, 0), jnp.int32(0)

    def two_own(i, before):
        even, odd = own_item(2 * i), own_item(2 * i + 1)
        plain_step(first_weigh_part, odd, even, before, s_b, s_a, p_a, p_b)
        later = own_item(jnp.minimum(2 * i + 2, 2 * tiles - 1))
        ends = (i == tiles - 1) & (whole_blocks > 0)
        later = tuple(jnp.where(ends, w, o) for w, o in zip(first_whole, later))
        plain_step(first_weigh_part, later, odd, even, s_a, s_b, p_b, p_a)
        return odd

    def two_whole(i, carry):
        before, here = carry[:2], carry[2:]
        after = following_whole(here)
        plain_step(next_weigh_part, after, here, before, s_b, s_a, p_a, p_b)
        later = following_whole(after)
        plain_step(next_weigh_part, later, after, here, s_a, s_b, p_b, p_a)
        return after + later

    for part in range(2):
        score_part(*own_item(0), s_a, part)
    before = lax.fori_loop(0, tiles, two_own, (jnp.int32(0), jnp.int32(0)))
    before = lax.fori_loop(0, whole_blocks * (tiles // 2), two_whole, before + first_whole)[:2]
    for part in range(2):
        plain_add_part(*before, p_b, part)

    @pl.when(jnp.logical_not(jnp.max(total[...]) < TOTAL_LIMIT))
    def _():
        clear(top, total, acc, p_b, r_b)
        for part in range(2):
            score_part(0, 0, s_a, part)
        rounds = (whole_blocks + 2) * (tiles // 2)
        before = lax.fori_loop(0, rounds, two_items, (jnp.int32(0),) * 4)[:2]
        for part in range(2):
            add_part(*before, p_b, r_b, part)

    wait(up_copies)

    def out_copy(tile):
        width = HEADS_TILE * VDIM
        columns = pl.ds(pl.multiple_of(tile * width, width), width)
        return pltpu.make_async_copy(
            out_ref.at[:, columns], out_hbm.at[:, columns], sems.at[3, tile]
        )

    def finish(tile, carry):
        attended = []
        for s in range(2):
            unit = 2 * tile + s
            share = 1.0 / jnp.sum(total[unit], axis=1, keepdims=True)
            attended.append((acc[unit] * share).astype(jnp.bfloat16))
        values = []
        for h in range(HEADS_TILE):
            rows = slice(h * SPAN, (h + 1) * SPAN)
            both = jnp.concatenate([attended[0][rows], attended[1][rows]], axis=0)
            values.append(
                jnp.dot(
                    both, up_ref[tile * HEADS_TILE + h], preferred_element_type=jnp.float32
                ).astype(jnp.bfloat16)
            )
        columns = HEADS_TILE * VDIM
        out_ref[:, pl.ds(pl.multiple_of(tile * columns, columns), columns)] = jnp.concatenate(
            values, axis=1
        )
        out_copy(tile).start()
        return carry

    lax.fori_loop(0, tiles, finish, 0)
    for tile in range(tiles):
        out_copy(tile).wait()
    done_ref[0] = 0


def prefill(ctx, spans, queries, keys, value_up):
    units = queries.shape[0]
    heads = value_up.shape[0]
    f32 = jnp.float32
    smem = pl.BlockSpec(memory_space=pltpu.SMEM)
    hbm = pl.BlockSpec(memory_space=pltpu.HBM)
    return pl.pallas_call(
        prefill_kernel,
        out_shape=(
            jax.ShapeDtypeStruct((2 * SPAN, heads * VDIM), jnp.bfloat16),
            jax.ShapeDtypeStruct((1,), jnp.int32),
        ),
        in_specs=[smem] * 2 + [hbm] * 3,
        out_specs=(hbm, smem),
        scratch_shapes=[
            pltpu.VMEM((2 * SPAN, heads * VDIM), jnp.bfloat16),
            pltpu.VMEM(queries.shape, jnp.bfloat16),
            pltpu.VMEM(keys.shape, jnp.bfloat16),
            pltpu.VMEM((2 * keys.shape[0] // KEYS, KPAD, KEYS // 2), jnp.bfloat16),
            pltpu.VMEM(value_up.shape, jnp.bfloat16),
            pltpu.VMEM((ROWS, KEYS), f32),
            pltpu.VMEM((ROWS, KEYS), f32),
            pltpu.VMEM((ROWS, KEYS), jnp.bfloat16),
            pltpu.VMEM((ROWS, KEYS), jnp.bfloat16),
            pltpu.VMEM((units, ROWS, 128), f32),
            pltpu.VMEM((units, ROWS, 128), f32),
            pltpu.VMEM((ROWS, 128), f32),
            pltpu.VMEM((ROWS, 128), f32),
            pltpu.VMEM((units, ROWS, LATENT), f32),
            pltpu.SemaphoreType.DMA((4, 4)),
        ],
        compiler_params=pltpu.CompilerParams(vmem_limit_bytes=59 << 20),
        cost_estimate=pl.CostEstimate(
            flops=units * ROWS * keys.shape[0] * 640,
            bytes_accessed=8 << 20,
            transcendentals=units * ROWS * keys.shape[0] // 2,
        ),
    )(ctx, spans, queries, keys, value_up)


def project_kernel(ctx_ref, grp_ref, rows_hbm, w_hbm, other_w_hbm, after_ref, *refs):
    out_refs, (rows_ref, w_ref, sums, sems) = refs[:4], refs[4:]
    chunks = sems.shape[1]
    width = rows_ref.shape[1] // chunks
    parts = [(slice(None), slice(c * width, (c + 1) * width)) for c in range(chunks)]
    sides = ((rows_hbm, rows_ref), (w_hbm, w_ref.at[0]), (other_w_hbm, w_ref.at[1]))
    copies = [
        [
            pltpu.make_async_copy(source.at[part], target.at[part], sems.at[i, c])
            for i, (source, target) in enumerate(sides)
        ]
        for c, part in enumerate(parts)
    ]
    for three in copies:
        for copy in three:
            copy.start()
    z, head_z, head_core = ctx_ref[0] // 16, grp_ref[0] // 2, grp_ref[0] % 2
    for c, part in enumerate(parts):
        for copy in copies[c]:
            copy.wait()
        for side in range(2):
            product = lax.dot_general(
                rows_ref[part], w_ref[side, :, part[1]], NT, preferred_element_type=jnp.float32
            )
            sums[side] = product if c == 0 else sums[side] + product
    share = sums.shape[1] // 2
    for k, out_ref in enumerate(out_refs):
        to_z, to_core = (head_z + k // 2) % 2, (head_core + k) % 2
        side = jnp.where(to_z == z, 0, 1)
        rows = pl.ds(pl.multiple_of(to_core * share, share), share)
        out_ref[...] = sums[side, rows, :].astype(jnp.bfloat16)


def project(ctx, grp, rows, weights, other_weights, after):
    smem = pl.BlockSpec(memory_space=pltpu.SMEM)
    vmem = pl.BlockSpec(memory_space=pltpu.VMEM)
    hbm = pl.BlockSpec(memory_space=pltpu.HBM)
    width, depth = weights.shape
    row_count = rows.shape[0]
    return pl.pallas_call(
        project_kernel,
        out_shape=(jax.ShapeDtypeStruct((row_count // 2, width), jnp.bfloat16),) * 4,
        in_specs=[smem, smem, hbm, hbm, hbm, smem],
        out_specs=(vmem,) * 4,
        scratch_shapes=[
            pltpu.VMEM(rows.shape, jnp.bfloat16),
            pltpu.VMEM((2, width, depth), jnp.bfloat16),
            pltpu.VMEM((2, row_count, width), jnp.float32),
            pltpu.SemaphoreType.DMA((3, 4)),
        ],
        compiler_params=pltpu.CompilerParams(vmem_limit_bytes=32 << 20),
        cost_estimate=pl.CostEstimate(
            flops=4 * row_count * depth * 256, bytes_accessed=8 << 20, transcendentals=0
        ),
    )(ctx, grp, rows, weights, other_weights, after)


def share_out(k, part):
    pairs = []
    for ctx in range(lax.axis_size("ctx")):
        z, line = divmod(ctx, 16)
        for a in range(2):
            for b in range(2):
                to = ((a ^ k // 2) * 16 + line) * 4 + 2 * z + (b ^ k % 2)
                pairs.append((ctx * 4 + 2 * a + b, to))
    return lax.ppermute(part, ("ctx", "grp"), pairs)


def body(
    prefill_queries,
    latents,
    rope_keys,
    span_slots,
    decode_queries,
    new_latents,
    new_rope,
    context_lengths,
    page_table,
    value_up,
    out_proj,
):
    ctx = lax.axis_index("ctx").astype(jnp.int32).reshape(1)
    grp = lax.axis_index("grp").astype(jnp.int32).reshape(1)
    rows_local = page_table.shape[0]

    pieces = gather_caches(pack(latents, rope_keys))
    queries, row_queries, fresh = arrange(prefill_queries, decode_queries, new_latents, new_rope)
    keys, decode_values = decode(
        ctx, span_slots, page_table, context_lengths, row_queries, fresh, pieces, value_up
    )
    weights = out_proj.T
    other_weights = shift(weights, 1, 0, 0)
    all_values = exchange(decode_values).reshape(-1, decode_values.shape[2])
    prefill_values, prefill_done = prefill(ctx, span_slots, queries, keys, value_up)
    parts = project(ctx, grp, all_values, weights, other_weights, prefill_done)
    summed = sum(share_out(k, part).astype(jnp.float32) for k, part in enumerate(parts))
    decoded = summed.astype(jnp.bfloat16).reshape(-1, 2, rows_local, summed.shape[1])
    decoded = decoded.transpose(1, 0, 2, 3).reshape(2, -1, summed.shape[1])
    return (prefill_values, decoded)


def solution(mesh):
    placed = (
        P("ctx", "grp"),
        P("ctx", "grp"),
        P("ctx", None),
        P(),
        P(None, "ctx", "grp"),
        P(None, "ctx", "grp"),
        P(None, "ctx", None),
        P("ctx"),
        P("ctx", None),
        P("grp", None, None),
        P("grp", "ctx"),
    )
    return jax.shard_map(
        body,
        mesh=mesh,
        in_specs=placed,
        out_specs=(P("ctx", "grp"), P(None, "grp", "ctx")),
        check_vma=False,
    )
```
